128 devices in a mesh: ctx: 8 (over y_lo, x), shard: 16 (over z, y_hi, core).
Axes of the slice: x: 4, y: 4 (y_hi: 2, y_lo: 2; y = y_hi * 2 + y_lo), z: 4, core: 2. Of those that a mesh axis runs over, the one named last changes fastest.
Arguments:
- tokens: bfloat16 [16, 1152, 2048], P('shard', 'ctx'), may hold values from -6 to 6
- cotangent: bfloat16 [16, 1152, 2048], P('shard', 'ctx'), may hold values from -6 to 6
- query_matrix: bfloat16 [2048, 2048], P('shard'), may hold values from -0.125 to 0.125
- key_matrix: bfloat16 [2048, 2048], P('shard'), may hold values from -0.125 to 0.125
- value_matrix: bfloat16 [2048, 2048], P('shard'), may hold values from -0.125 to 0.125
- output_matrix: bfloat16 [2048, 2048], P('shard'), may hold values from -0.125 to 0.125
- gate_matrix: bfloat16 [2048, 8192], P('shard'), may hold values from -0.125 to 0.125
- upward_matrix: bfloat16 [2048, 8192], P('shard'), may hold values from -0.125 to 0.125
- down_matrix: bfloat16 [8192, 2048], P('shard'), may hold values from -0.0625 to 0.0625
- norm_gain_vectors: float32 [4, 2048], replicated, may hold values from 0.1 to 1.9
- adapter_down_inputs: bfloat16 [8, 6, 16, 2048], replicated, may hold values from -0.125 to 0.125
- adapter_down_feedforward: bfloat16 [8, 16, 8192], replicated, may hold values from -0.0625 to 0.0625
- adapter_up_model_maps: bfloat16 [8, 5, 16, 2048], replicated, may hold values from -0.375 to 0.375
- adapter_up_hidden_maps: bfloat16 [8, 2, 16, 8192], replicated, may hold values from -0.375 to 0.375
- group_adapter_index: int32 [16, 1], P('shard'), may hold values from 0 to 7
- continuation_lengths: int32 [16, 2], P('shard'), may hold values from 32 to 96, as said below
Outputs:
- output: bfloat16 [16, 1152, 2048], P('shard', 'ctx')
- grad_tokens: bfloat16 [16, 1152, 2048], P('shard', 'ctx')
- grad_down_in: float32 [8, 6, 16, 2048], replicated
- grad_down_ff: float32 [8, 16, 8192], replicated
- grad_up_model: float32 [8, 5, 16, 2048], replicated
- grad_up_hidden: float32 [8, 2, 16, 8192], replicated
The draws below stay inside these ranges and needn't reach their ends.
Inputs may be any that keep to these rules, and one draw needn't show every extreme that they name: `group_adapter_index`: every adapter is used by some group. `continuation_lengths`: each group's two lengths sum to 128; the longer one lies between 64 and 96, and in group 0 it is exactly 96.
All inputs are finite; a program needn't handle non-finite values.
Results may differ from the reference program's by a relative error of at most 0.035.
Values may be sent and summed in bfloat16 or wider, within the bound.
No kernel may reach another device: no remote copies, remote signals or barrier semaphores. Data moves between devices by JAX's collectives and lax.ppermute only.
A program may use at most 448 MiB of HBM per device.

```python
import jax
import jax.numpy as jnp
from jax import lax

MODEL_WIDTH = 2048
H = 16
HD = 128
HIDDEN_UNITS = 8192
ADAPTER_RANK = 16
ADAPTER_TOTAL = 8
PROMPT = 1024
CONT_LEN = 64
GROUP_TOK = 1152
GROUPS = 16


def draw_continuation_lengths(key, part):
    key = jax.random.fold_in(key, 11)
    most = CONT_LEN + CONT_LEN // 2
    key_long, key_side = jax.random.split(key)
    longer = jax.random.randint(key_long, (GROUPS,), CONT_LEN, most + 1, dtype=jnp.int32)
    rows = jnp.arange(GROUPS, dtype=jnp.int32)
    longer = jnp.where(rows == 0, most, longer)
    shorter = 2 * CONT_LEN - longer
    side = jax.random.randint(key_side, (GROUPS,), 0, 2, dtype=jnp.int32)
    first = jnp.where(side == 0, longer, shorter)
    second = jnp.where(side == 0, shorter, longer)
    return jnp.stack([first, second], axis=1).astype(jnp.int32)


def levels(rng, dims, cuts, smallest, high):
    def one(dim, parts):
        draws = jax.random.uniform(jax.random.fold_in(jax.random.fold_in(rng, 6), dim), (parts,), jnp.float32, smallest / len(cuts), high / len(cuts))
        return jnp.repeat(jnp.exp(draws), dims[dim] // parts).reshape((-1,) + (1,) * (len(dims) - dim - 1))

    loudness = one(*cuts[0])
    for cut in cuts[1:]:
        loudness = loudness * one(*cut)
    return loudness


def choose_distinct(key, rows, count, top, lift):
    ranking = jax.random.permutation(jax.random.fold_in(key, 1), count)
    boost = ranking
    for power in range(3):
        boost = boost * boost // count
    boost = boost * lift // count
    lots = jax.random.randint(jax.random.fold_in(key, 2), (rows, count), 0, 4096) + boost
    sure = jax.random.permutation(jax.random.fold_in(key, 3), rows)[jnp.arange(count) % rows]
    lots = jnp.where(jnp.arange(rows)[:, None] == sure[None, :], 1 << 14, lots)
    score = lots * count + jnp.arange(count)
    return lax.top_k(score.astype(jnp.int32), top)[1].astype(jnp.int32)


def gaussian(own_key, shape, scale, limit, pieces=(), kind=jnp.bfloat16):
    level = levels(own_key, shape, pieces, -0.22, 0.18) if pieces else 1.0
    array = jax.random.normal(own_key, shape, jnp.float32) * scale * level
    return jnp.minimum(jnp.maximum(array, -limit), limit).astype(kind)


def setup_inputs(seed: int = 0) -> dict:
    key_of = jax.random.split(jax.random.key(seed), 17)
    tokens = gaussian(key_of[0], (GROUPS, GROUP_TOK, MODEL_WIDTH), 1.0, 6.0, ((0, 16), (1, 8)))
    cotangent = gaussian(key_of[1], (GROUPS, GROUP_TOK, MODEL_WIDTH), 1.0, 6.0, ((0, 16), (1, 8)))
    query_matrix = gaussian(key_of[2], (MODEL_WIDTH, MODEL_WIDTH), MODEL_WIDTH ** -0.5, 0.125, ((0, 16),))
    key_matrix = gaussian(key_of[3], (MODEL_WIDTH, MODEL_WIDTH), MODEL_WIDTH ** -0.5, 0.125, ((0, 16),))
    value_matrix = gaussian(key_of[4], (MODEL_WIDTH, MODEL_WIDTH), MODEL_WIDTH ** -0.5, 0.125, ((0, 16),))
    output_matrix = gaussian(key_of[5], (MODEL_WIDTH, MODEL_WIDTH), MODEL_WIDTH ** -0.5, 0.125, ((0, 16),))
    gate_matrix = gaussian(key_of[6], (MODEL_WIDTH, HIDDEN_UNITS), MODEL_WIDTH ** -0.5, 0.125, ((0, 16),))
    upward_matrix = gaussian(key_of[7], (MODEL_WIDTH, HIDDEN_UNITS), MODEL_WIDTH ** -0.5, 0.125, ((0, 16),))
    down_matrix = gaussian(key_of[8], (HIDDEN_UNITS, MODEL_WIDTH), HIDDEN_UNITS ** -0.5, 0.0625, ((0, 16),))
    norm_gain_vectors = jnp.clip(1.0 + 0.18 * jax.random.normal(key_of[9], (4, MODEL_WIDTH), jnp.float32), 0.1, 1.9)
    adapter_down_inputs = gaussian(key_of[10], (ADAPTER_TOTAL, 6, ADAPTER_RANK, MODEL_WIDTH), MODEL_WIDTH ** -0.5, 0.125)
    adapter_down_feedforward = gaussian(key_of[11], (ADAPTER_TOTAL, ADAPTER_RANK, HIDDEN_UNITS), HIDDEN_UNITS ** -0.5, 0.0625)
    adapter_up_model_maps = gaussian(key_of[12], (ADAPTER_TOTAL, 5, ADAPTER_RANK, MODEL_WIDTH), (16 * ADAPTER_RANK) ** -0.5, 0.375)
    adapter_up_hidden_maps = gaussian(key_of[13], (ADAPTER_TOTAL, 2, ADAPTER_RANK, HIDDEN_UNITS), (16 * ADAPTER_RANK) ** -0.5, 0.375)
    group_adapter_index = choose_distinct(key_of[14], GROUPS, ADAPTER_TOTAL, 1, 0)
    continuation_lengths = draw_continuation_lengths(jax.random.fold_in(key_of[16], 71), 0)
    return dict(tokens=tokens, cotangent=cotangent, query_matrix=query_matrix, key_matrix=key_matrix, value_matrix=value_matrix, output_matrix=output_matrix, gate_matrix=gate_matrix, upward_matrix=upward_matrix, down_matrix=down_matrix, norm_gain_vectors=norm_gain_vectors, adapter_down_inputs=adapter_down_inputs, adapter_down_feedforward=adapter_down_feedforward, adapter_up_model_maps=adapter_up_model_maps, adapter_up_hidden_maps=adapter_up_hidden_maps, group_adapter_index=group_adapter_index, continuation_lengths=continuation_lengths)


@jax.custom_vjp
def low(v):
    return lax.optimization_barrier(v.astype(jnp.bfloat16)).astype(jnp.float32)

@jax.custom_vjp
def low_back(v):
    return v

def low_keep(v):
    return (low(v), None)

def low_pass(kept, grad):
    return (grad,)

def back_keep(v):
    return (v, None)

def back_low(kept, grad):
    return (low(grad),)
low.defvjp(low_keep, low_pass)
low_back.defvjp(back_keep, back_low)
adapter_scale = 2.0
norm_eps = 1e-06
rope_base = 500000.0
masked_score = -1e+30

def layout(lengths, prompt, total):
    csum = jnp.cumsum(lengths, axis=1, dtype=jnp.int32)
    bounds = prompt + csum - lengths
    places = jnp.arange(total, dtype=jnp.int32)
    after = places[None, :, None] >= bounds[:, None, :]
    segment = lax.optimization_barrier(jnp.sum(after.astype(jnp.int32), axis=2, dtype=jnp.int32))
    begin = lax.optimization_barrier(jnp.max(jnp.where(after, bounds[:, None, :], 0), axis=2))
    position = jnp.where(segment == 0, places[None, :], prompt + places[None, :] - begin)
    return (segment, position)

def rope_tables(position, head_dim):
    half = head_dim // 2
    freq = rope_base ** (-(jnp.arange(half, dtype=jnp.float32) * 2.0 / head_dim))
    angle = position.astype(jnp.float32)[..., None] * freq
    return (jnp.cos(angle), jnp.sin(angle))

def rotate(field, cosine, sine, heads):
    shape = field.shape
    split = field.reshape(shape[:-1] + (heads, 2, shape[-1] // heads // 2))
    first = split[..., 0, :]
    second = split[..., 1, :]
    cos_part = cosine[..., None, :]
    sin_part = sine[..., None, :]
    turned = jnp.stack([first * cos_part - second * sin_part, second * cos_part + first * sin_part], axis=-2)
    return turned.reshape(shape)

def normalize(field, gain):
    return field * lax.rsqrt(lax.optimization_barrier(jnp.mean(field * field, axis=-1, keepdims=True)) + norm_eps) * gain

def one_group(tokens, pick, segment, position, down_in, down_ff, up_model, up_hidden, weights, gains):
    highest_precision = lax.Precision.HIGHEST
    query_matrix, key_matrix, value_matrix, output_matrix, gate_matrix, upward_matrix, down_matrix = weights
    chosen_in = jnp.einsum('a,ajrd->jrd', pick, down_in, precision=highest_precision)
    chosen_ff = jnp.einsum('a,ard->rd', pick, down_ff, precision=highest_precision)
    chosen_model = jnp.einsum('a,ajrd->jrd', pick, up_model, precision=highest_precision)
    chosen_hidden = jnp.einsum('a,ajrd->jrd', pick, up_hidden, precision=highest_precision)

    def project(inputs, weight, adapter_down, adapter_lift_map):
        reduced_rank_output = low(low_back(jnp.dot(inputs, adapter_down.T, precision=highest_precision, preferred_element_type=jnp.float32)))
        frozen_output = jnp.dot(inputs, weight, precision=highest_precision, preferred_element_type=jnp.float32)
        return frozen_output + adapter_scale * jnp.dot(reduced_rank_output, adapter_lift_map, precision=highest_precision, preferred_element_type=jnp.float32)
    length = tokens.shape[0]
    score_scale = HD ** (-0.5)
    cosine, sine = rope_tables(position, HD)
    query_pre = low_back(project(tokens, query_matrix, chosen_in[0], chosen_model[0]))
    key_pre = low_back(project(tokens, key_matrix, chosen_in[1], chosen_model[1]))
    value_pre = low_back(project(tokens, value_matrix, chosen_in[2], chosen_model[2]))
    query = low(rotate(normalize(query_pre, gains[0]), cosine, sine, H))
    key = low(rotate(normalize(key_pre, gains[1]), cosine, sine, H))
    value = low(value_pre)
    places = jnp.arange(length, dtype=jnp.int32)
    allowed = (places[None, :] <= places[:, None]) & ((segment[None, :] == 0) | (segment[None, :] == segment[:, None]))
    scores = jnp.einsum('qhe,khe->hqk', query.reshape(length, H, HD), key.reshape(length, H, HD), precision=highest_precision)
    scores = low_back(scores * score_scale)
    probs = jax.nn.softmax(jnp.where(allowed[None], scores, masked_score), axis=-1)
    attended = jnp.einsum('hqk,khe->qhe', low(probs), value.reshape(length, H, HD), precision=highest_precision).reshape(length, MODEL_WIDTH)
    attended_low = low(low_back(attended))
    attn_pre = low_back(project(attended_low, output_matrix, chosen_in[3], chosen_model[3]))
    hidden = tokens + normalize(attn_pre, gains[2])
    hidden_low = low(hidden)
    gate = low_back(project(hidden_low, gate_matrix, chosen_in[4], chosen_hidden[0]))
    upward = low_back(project(hidden_low, upward_matrix, chosen_in[5], chosen_hidden[1]))
    mixed = low(jax.nn.silu(gate) * upward)
    mlp_pre = low_back(project(mixed, down_matrix, chosen_ff, chosen_model[4]))
    return hidden + normalize(mlp_pre, gains[3])

def reference(tokens, cotangent, query_matrix, key_matrix, value_matrix, output_matrix, gate_matrix, upward_matrix, down_matrix, norm_gain_vectors, adapter_down_inputs, adapter_down_feedforward, adapter_up_model_maps, adapter_up_hidden_maps, group_adapter_index, continuation_lengths):
    weights = tuple((item.astype(jnp.float32) for item in (query_matrix, key_matrix, value_matrix, output_matrix, gate_matrix, upward_matrix, down_matrix)))
    gains = norm_gain_vectors.astype(jnp.float32)
    segment, position = layout(continuation_lengths, PROMPT, GROUP_TOK)
    picks = (group_adapter_index == jnp.arange(ADAPTER_TOTAL, dtype=jnp.int32)[None, :]).astype(jnp.float32)
    grouped = jax.checkpoint(one_group)

    def forward_pass(inputs, down_in, down_ff, up_model, up_hidden):

        def step(carry, item):
            return (carry, grouped(item[0], item[1], item[2], item[3], down_in, down_ff, up_model, up_hidden, weights, gains))
        carry, result = lax.scan(step, jnp.zeros((), jnp.float32), (inputs, picks, segment, position))
        return result
    output, reverse_gradient = jax.vjp(forward_pass, tokens.astype(jnp.float32), adapter_down_inputs.astype(jnp.float32), adapter_down_feedforward.astype(jnp.float32), adapter_up_model_maps.astype(jnp.float32), adapter_up_hidden_maps.astype(jnp.float32))
    grads = reverse_gradient(cotangent.astype(jnp.float32))
    return (output.astype(jnp.bfloat16), grads[0].astype(jnp.bfloat16), grads[1], grads[2], grads[3], grads[4])
```

```python
import jax
import jax.numpy as jnp
from jax import lax
from jax.experimental import pallas as pl
from jax.experimental.pallas import tpu as pltpu
from jax.sharding import Mesh, PartitionSpec as P

HD = 128
PROMPT = 1024
ROWS = 144
TOTAL = 1152
D = 2048
HALF = 1024
FF = 4096
RANK = 16
SCALE = HD**-0.5
EPS = 1e-06
BASE = 500000.0
ALL = ("yl", "x", "z", "yh", "c")
CTX = ("yl", "x")
BF = jnp.bfloat16
F32 = jnp.float32
CUT_A = (1536, 512)
CUT_G = (3072, 2560)
CUT_D = (512, 512)
EARLY, LATE = 2176, 768


DEPTH = 4
ORDER = (
    "sA0", "czA", "sM0", "sA1", "czD", "sA2", "pzA", "sM1", "cxA", "y0A0",
    "pxA", "sM2", "czG", "y1A0", "z0A0", "z0G0", "pzG", "cxG", "z1A0", "y1A1",
    "z0A1", "pxG", "cxD", "z1A1", "y0A1", "pzD", "z0A2", "y0A2", "z1A2", "y1A2",
    "y1D0", "z1G0", "pxD", "y0G0", "z0G1", "y1G0", "z0D0", "y0G1", "z1G1", "y1G1",
    "z0G2", "z1G2", "y0G2", "z1D0", "y1G2", "y0D0", "z0D1", "z1D1", "y0D1", "y1D1",
    "z0D2", "z1D2", "y1D2", "y0D2",
)


def _place(yl, x, z, yh, c):
    return (((yl * 4 + x) * 4 + z) * 2 + yh) * 2 + c


def _permutation(move):
    pairs = []
    for yl in range(2):
        for x in range(4):
            for z in range(4):
                for yh in range(2):
                    for c in range(2):
                        nx, ny, nz, nc = move(x, 2 * yh + yl, z, c)
                        pairs.append(
                            (_place(yl, x, z, yh, c), _place(ny % 2, nx % 4, nz % 4, (ny % 4) // 2, nc))
                        )
    return pairs


STEPS = {
    "y": _permutation(lambda x, y, z, c: (x, (y + 1 - 2 * c) % 4, z, c)),
    "z": _permutation(lambda x, y, z, c: (x, y, z + 1 - 2 * c, c)),
    "cross": _permutation(lambda x, y, z, c: (x, 3 - y, z, c)),
    "pair": _permutation(lambda x, y, z, c: (x, y ^ 1, z, c)),
    "core": _permutation(lambda x, y, z, c: (x, y, z, 1 - c)),
}


def swap(value):
    return lax.ppermute(value, ALL, STEPS["core"])


class Queue:
    def __init__(self, depth):
        self.depth = depth
        self.sent = []

    def send(self, value, how):
        if len(self.sent) >= self.depth:
            value, _ = lax.optimization_barrier((value, self.sent[-self.depth]))
        got = lax.ppermute(value, ALL, STEPS[how])
        self.sent.append(got)
        return got


def _smem():
    return pl.BlockSpec(memory_space=pltpu.SMEM)


def _vmem():
    return pl.BlockSpec(memory_space=pltpu.VMEM)


def _plain(body, name, outs, ins, scalars, scratch=(), limit=48):
    size = sum(v.size * v.dtype.itemsize for v in list(ins) + list(outs))
    return pl.pallas_call(
        body,
        out_shape=outs,
        in_specs=[_smem()] * len(scalars) + [_vmem()] * len(ins),
        out_specs=[_vmem()] * len(outs),
        scratch_shapes=list(scratch),
        compiler_params=pltpu.CompilerParams(vmem_limit_bytes=limit * 2**20),
        cost_estimate=pl.CostEstimate(flops=0, bytes_accessed=size, transcendentals=0),
        name=name,
    )(*scalars, *ins)


def bf(*shape):
    return jax.ShapeDtypeStruct(shape, BF)


def split_a(core, q, k, v):
    def body(core, q, k, v, keep, give):
        for n, w in enumerate((q, k, v)):
            for h in range(8):
                here = slice(n * HALF + HD * h, n * HALF + HD * (h + 1))
                keep[:, here] = w[:, pl.ds(pl.multiple_of((2 * h + core[0]) * HD, HD), HD)]
                give[:, here] = w[:, pl.ds(pl.multiple_of((2 * h + 1 - core[0]) * HD, HD), HD)]

    return _plain(body, "split_a", [bf(HD, 3 * HALF)] * 2, [q, k, v], [core])


def split_g(core, gate, upward):
    def body(core, gate, upward, keep, give):
        for m in range(FF // 128):
            for n, w in enumerate((gate, upward)):
                here = slice(256 * m + 128 * n, 256 * m + 128 * (n + 1))
                for side, out in ((core[0], keep), (1 - core[0], give)):
                    start = (2 * (m // 4) + side) * 512 + (m % 4) * 128
                    out[:, here] = w[:, pl.ds(pl.multiple_of(start, 128), 128)]

    return _plain(body, "split_g", [bf(HD, 2 * FF)] * 2, [gate, upward], [core])


def parts_a(me, keep, got, out):
    cx, cy = CUT_A
    cz = 4 * HALF - cx - cy
    first = 3 * HALF - cx - cy

    def body(me, keep, got, out, zpart, small):
        for side, w in ((me[CORE], keep), (1 - me[CORE], got)):
            rows = pl.ds(pl.multiple_of(side * HD, HD), HD)
            zpart[rows, :first] = w[:, cx + cy :]
            small[rows, : cx // 4] = w[:, pl.ds(pl.multiple_of(me[X] * (cx // 4), 128), cx // 4)]
            small[rows, cx // 4 :] = w[:, pl.ds(pl.multiple_of(cx + me[YL] * (cy // 2), 128), cy // 2)]
        zpart[:HD, first:] = out[:, :HALF]
        zpart[HD:, first:] = out[:, HALF:]

    return _plain(body, "parts_a", [bf(256, cz), bf(256, cx // 4 + cy // 2)], [keep, got, out], [me])


def parts_m(me, keep, got, down):
    gx, gy = CUT_G
    dx, dy = CUT_D
    gz, dz = 2 * FF - gx - gy, D - dx - dy
    widths = [gx // 4, gy // 2, dx // 4, dx // 4, dy // 2, dy // 2]
    starts = [sum(widths[:n]) for n in range(7)]

    def body(me, keep, got, down, zg, zd, small):
        for side, w in ((me[CORE], keep), (1 - me[CORE], got)):
            rows = pl.ds(pl.multiple_of(side * HD, HD), HD)
            zg[rows, :] = w[:, gx + gy :]
            small[rows, : starts[1]] = w[:, pl.ds(pl.multiple_of(me[X] * (gx // 4), 128), gx // 4)]
            small[rows, starts[1] : starts[2]] = w[:, pl.ds(pl.multiple_of(gx + me[YL] * (gy // 2), 128), gy // 2)]
        zd[...] = down[:, dx + dy :]
        for n in range(2):
            rows = slice(256 * n, 256 * (n + 1))
            small[:, starts[2 + n] : starts[3 + n]] = down[rows, pl.ds(pl.multiple_of(me[X] * (dx // 4), 128), dx // 4)]
            small[:, starts[4 + n] : starts[5 + n]] = down[
                rows, pl.ds(pl.multiple_of(dx + me[YL] * (dy // 2), 128), dy // 2)
            ]

    return _plain(body, "parts_m", [bf(256, gz), bf(512, dz), bf(256, starts[6])], [keep, got, down], [me])


def spread(me, got, column, rows, cut):
    wx, wy, fold = cut[0] // 4, cut[1] // 2, rows // 256

    def body(me, *refs):
        chunks, (xs, y0, y1) = refs[:4], refs[4:]
        for k in range(4):
            z = me[Z0 + k]
            for n in range(fold):
                start = column + n * wx
                at = pl.multiple_of(z * rows + 256 * n, 256)
                xs[pl.ds(at, 256), :] = chunks[k][:, start : start + wx]
                start = column + fold * wx + n * wy
                for half, out in ((0, y0), (1, y1)):

                    @pl.when(z // 2 == half)
                    def _():
                        here = pl.ds(pl.multiple_of((z - 2 * half) * rows + 256 * n, 256), 256)
                        out[here, :] = chunks[k][:, start : start + wy]

    outs = [bf(4 * rows, wx), bf(2 * rows, wy), bf(2 * rows, wy)]
    return _plain(body, "spread", outs, list(got), [me]), column + fold * (wx + wy)


def join_x(me, own, near, far):
    rows = own.shape[0] // 4

    def body(me, own, near, far, out):
        for z in range(4):
            out[pl.ds(pl.multiple_of((2 * z + me[YH]) * rows, rows), rows), :] = own[z * rows : (z + 1) * rows]
        for z in range(2):
            for half, piece in ((me[YL], near), (1 - me[YL], far)):
                at = pl.multiple_of((2 * (2 * half + z) + 1 - me[YH]) * rows, rows)
                out[pl.ds(at, rows), :] = piece[z * rows : (z + 1) * rows]

    return _plain(body, "join_x", [bf(8 * rows, own.shape[1])], [own, near, far], [me])[0]


class Chunks:
    def __init__(self, rows, cut, width, places, xg, y, z):
        self.rows, self.cx, self.cy = rows, cut[0], cut[1]
        self.cz = width - sum(cut)
        self.depth = 8 * rows
        self.places = places
        self.arrays = [xg] + y[0] + y[1] + z[0] + z[1]


def _y_rows(places, rows, half, j, k):
    return pl.multiple_of((2 * half + j) * 2 * rows + places[0, k] * rows, rows)


def _z_rows(places, rows, half, k):
    return pl.multiple_of(places[2, k] * 2 * rows + places[3, half] * rows, rows)


def _assemble_body(w, places, *refs):
    rows, cx, cy, cz = w.rows, w.cx, w.cy, w.cz
    xg, y, z, out, sems = refs[0], refs[1:9], refs[9:17], refs[17], refs[18]
    copies = []
    for k in range(4):
        copies.append((xg.at[k], out.at[:, pl.ds(k * (cx // 4), cx // 4)]))
        column = pl.multiple_of(cx + places[1, k] * (cy // 2), 128)
        for half in range(2):
            for j in range(2):
                row = _y_rows(places, rows, half, j, k)
                copies.append(
                    (
                        y[4 * half + k].at[pl.ds(j * rows, rows)],
                        out.at[pl.ds(row, rows), pl.ds(column, cy // 2)],
                    )
                )
            row = _z_rows(places, rows, half, k)
            copies.append((z[4 * half + k], out.at[pl.ds(row, rows), pl.ds(cx + cy, cz)]))
    started = [pltpu.make_async_copy(s, d, sems.at[n]) for n, (s, d) in enumerate(copies)]
    for copy in started:
        copy.start()
    for copy in started:
        copy.wait()


def assemble(w):
    anywhere = pl.BlockSpec(memory_space=pl.ANY)
    width = w.cx + w.cy + w.cz

    def body(*refs):
        _assemble_body(w, *refs)

    return pl.pallas_call(
        body,
        out_shape=jax.ShapeDtypeStruct((w.depth, width), BF),
        in_specs=[pl.BlockSpec(memory_space=pltpu.SMEM)] + [anywhere] * 17,
        out_specs=pl.BlockSpec(memory_space=pltpu.VMEM),
        scratch_shapes=[pltpu.SemaphoreType.DMA((28,))],
        compiler_params=pltpu.CompilerParams(vmem_limit_bytes=48 * 2**20),
        cost_estimate=pl.CostEstimate(flops=0, bytes_accessed=4 * w.depth * width, transcendentals=0),
        name="assemble",
    )(w.places, *w.arrays)


class Resident:
    def __init__(self, w, panels, zcuts):
        self.w = w
        cx, cy, cz = w.cx, w.cy, w.cz
        self.panels, self.zcuts = panels, zcuts
        step = cx // 4 * panels
        self.pieces = [(n * step, step) for n in range(4 // panels)] + [(cx, cy)]
        self.pieces += [(cx + cy + n * (cz // zcuts), cz // zcuts) for n in range(zcuts)]

    def scratch(self):
        w = self.w
        return [pltpu.VMEM((w.depth, w.cx + w.cy + w.cz), BF), pltpu.SemaphoreType.DMA((20 + 8 * self.zcuts,))]

    def start(self, places, refs, whole, sems):
        w = self.w
        rows, cx, cy, cz = w.rows, w.cx, w.cy, w.cz
        xg, y, z = refs[0], refs[1:9], refs[9:17]
        pieces = [[] for _ in self.pieces]
        for k in range(4):
            pieces[k // self.panels].append((xg.at[k], whole.at[:, pl.ds(k * (cx // 4), cx // 4)]))
        first = 4 // self.panels
        part = cz // self.zcuts
        for k in range(4):
            column = pl.multiple_of(cx + places[1, k] * (cy // 2), 128)
            for half in range(2):
                for j in range(2):
                    row = _y_rows(places, rows, half, j, k)
                    pieces[first].append(
                        (
                            y[4 * half + k].at[pl.ds(j * rows, rows)],
                            whole.at[pl.ds(row, rows), pl.ds(column, cy // 2)],
                        )
                    )
                row = _z_rows(places, rows, half, k)
                for n in range(self.zcuts):
                    pieces[first + 1 + n].append(
                        (
                            z[4 * half + k].at[:, pl.ds(n * part, part)],
                            whole.at[pl.ds(row, rows), pl.ds(cx + cy + n * part, part)],
                        )
                    )
        numbers = [sum(len(p) for p in pieces[:n]) for n in range(len(pieces))]
        copies = [
            [pltpu.make_async_copy(a, b, sems.at[first + m]) for m, (a, b) in enumerate(piece)]
            for first, piece in zip(numbers, pieces)
        ]

        def begin(n):
            if n < len(copies):
                for copy in copies[n]:
                    copy.start()

        def arrive(n):
            for copy in copies[n]:
                copy.wait()

        begin(0)
        begin(1)
        return begin, arrive

    def forward(self, places, refs, whole, sems, x, tile, finish):
        begin, arrive = self.start(places, refs, whole, sems)
        for n, (start, width) in enumerate(self.pieces):
            arrive(n)
            begin(n + 2)
            for column in range(start, start + width, tile):
                size = min(tile, start + width - column)
                finish(jnp.dot(x[...], whole[:, column : column + size], preferred_element_type=F32), column)

    def backward(self, places, refs, whole, sems, dy, tile, finish):
        begin, arrive = self.start(places, refs, whole, sems)
        for n, (start, width) in enumerate(self.pieces):
            arrive(n)
            begin(n + 2)
            left = dy[:, start : start + width]
            for row in range(0, self.w.depth, tile):
                finish(lax.dot_general(left, whole[row : row + tile, start : start + width], **NT), row, n)

    def call(self, body, name, ins, outs, flops):
        w = self.w
        anywhere = pl.BlockSpec(memory_space=pl.ANY)
        size = 2 * w.depth * (w.cx + w.cy + w.cz) + sum(v.size * v.dtype.itemsize for v in ins)
        return pl.pallas_call(
            body,
            out_shape=outs,
            in_specs=[_smem()] + [anywhere] * 17 + [_vmem()] * len(ins),
            out_specs=[_vmem()] * len(outs),
            scratch_shapes=self.scratch(),
            compiler_params=pltpu.CompilerParams(vmem_limit_bytes=60 * 2**20),
            cost_estimate=pl.CostEstimate(flops=flops, bytes_accessed=size, transcendentals=0),
            name=name,
        )(w.places, *w.arrays, *ins)


def gate_and_up(w, x, low, up):
    rows = x.shape[0]
    plan = Resident(w, 1, 2)

    def body(places, *refs):
        weights, (x_ref, low_ref, up_ref, gu, mixed, whole, sems) = refs[:17], refs[17:]

        def finish(total, column):
            width = total.shape[1]
            total = total + jnp.dot(low_ref[...], up_ref[:, column : column + width], preferred_element_type=F32)
            gu[:, column : column + width] = total.astype(BF)
            unit = column // 2
            for m in range(width // 256):
                g, u = total[:, 256 * m : 256 * m + 128], total[:, 256 * m + 128 : 256 * m + 256]
                mixed[:, unit + 128 * m : unit + 128 * (m + 1)] = (g * jax.nn.sigmoid(g) * u).astype(BF)

        plan.forward(places, weights, whole, sems, x_ref, 768, finish)

    outs = [jax.ShapeDtypeStruct((rows, 2 * FF), BF), jax.ShapeDtypeStruct((rows, FF), BF)]
    return plan.call(body, "gate_and_up", [x, low, up], outs, 2 * rows * D * 2 * FF)


def down(w, x):
    rows = x.shape[0]
    plan = Resident(w, 2, 2)

    def body(places, *refs):
        weights, (x_ref, out, whole, sems) = refs[:17], refs[17:]

        def finish(total, column):
            out[:, column : column + total.shape[1]] = total

        plan.forward(places, weights, whole, sems, x_ref, 512, finish)

    return plan.call(body, "down", [x], [jax.ShapeDtypeStruct((rows, D), F32)], 2 * rows * D * FF)[0]


def down_back(w, dy, low, ff_down, gu):
    rows = dy.shape[0]
    plan = Resident(w, 4, 1)

    def body(places, *refs):
        weights, (dy_ref, low_ref, ff_ref, gu_ref, out, whole, sems, sums) = refs[:17], refs[17:]

        def finish(part_sum, row, part):
            units = slice(row, row + part_sum.shape[1])
            if part == 0:
                sums[:, units] = part_sum + jnp.dot(low_ref[...], ff_ref[:, units], preferred_element_type=F32)
            elif part == 1:
                sums[:, units] += part_sum
            else:
                d_mixed = sums[:, units] + part_sum
                column = 2 * row
                for m in range(part_sum.shape[1] // 128):
                    g = gu_ref[:, column + 256 * m : column + 256 * m + 128].astype(F32)
                    u = gu_ref[:, column + 256 * m + 128 : column + 256 * (m + 1)].astype(F32)
                    d = d_mixed[:, 128 * m : 128 * (m + 1)]
                    s = jax.nn.sigmoid(g)
                    out[:, column + 256 * m : column + 256 * m + 128] = (d * u * s * (1.0 + g * (1.0 - s))).astype(BF)
                    out[:, column + 256 * m + 128 : column + 256 * (m + 1)] = (d * g * s).astype(BF)

        plan.backward(places, weights, whole, sems, dy_ref, 1024, finish)

    outs = [jax.ShapeDtypeStruct((rows, 2 * FF), BF)]
    plan_scratch = plan.scratch
    plan.scratch = lambda: plan_scratch() + [pltpu.VMEM((rows, FF), F32)]
    return plan.call(body, "down_back", [dy, low, ff_down, gu], outs, 2 * rows * D * FF)[0]


def gate_and_up_back(w, dy):
    rows = dy.shape[0]
    plan = Resident(w, 2, 1)

    def body(places, *refs):
        weights, (dy_ref, out, whole, sems) = refs[:17], refs[17:]

        def finish(part_sum, row, part):
            units = slice(row, row + part_sum.shape[1])
            if part == 0:
                out[:, units] = part_sum
            else:
                out[:, units] += part_sum

        plan.backward(places, weights, whole, sems, dy_ref, 1024, finish)

    outs = [jax.ShapeDtypeStruct((rows, D), F32)]
    return plan.call(body, "gate_and_up_back", [dy], outs, 2 * rows * D * 2 * FF)[0]


CORE, X, YL, YH, Z0 = 0, 1, 2, 3, 4


class Gather:
    def __init__(self):
        core = lax.axis_index("c")
        x, z = lax.axis_index("x"), lax.axis_index("z")
        yl, yh = lax.axis_index("yl"), lax.axis_index("yh")
        y = 2 * yh + yl
        sign = 1 - 2 * core
        ys = [lax.rem(y - sign * k + 8, 4) for k in range(4)]
        zs = [lax.rem(z - sign * k + 8, 4) for k in range(4)]
        self.yl = yl
        self.me = jnp.stack([core, x, yl, yh] + zs).astype(jnp.int32)
        self.places = jnp.stack(
            [
                jnp.stack([v // 2 for v in ys]),
                jnp.stack([v % 2 for v in ys]),
                jnp.stack(zs),
                jnp.stack([yh, 1 - yh, yh, yh]),
            ]
        ).astype(jnp.int32)

    def halves(self, value):
        n = value.shape[0] // 2
        upper, lower = value[:n], value[n:]
        return jnp.where(self.yl == 0, upper, lower), jnp.where(self.yl == 0, lower, upper)


def gather_weights(plan, split, out_shard, split_m, down_shard):
    me = plan.me
    queue = Queue(DEPTH)
    state = {}
    shapes = {"A": (256, CUT_A, 4 * HALF), "G": (256, CUT_G, 2 * FF), "D": (512, CUT_D, D)}
    zpart = {}
    zpart["A"], small_a = parts_a(me, *split, out_shard)
    zpart["G"], zpart["D"], small_m = parts_m(me, *split_m, down_shard)
    ring = {"sA": [small_a], "sM": [small_m]}
    for g in "AGD":
        ring["z0" + g] = [zpart[g]]
    cross = {}

    def need(key):
        if key in ring or key in cross:
            return
        kind, g = key[:-1], key[-1]
        rows, cut, _ = shapes[g]
        if kind in ("y0", "y1", "x"):
            if g == "A":
                (xs, y0, y1), _ = spread(me, ring["sA"], 0, rows, cut)
                values = {"A": (xs, y0, y1)}
            else:
                values = {}
                values["G"], column = spread(me, ring["sM"], 0, *shapes["G"][:2])
                values["D"], _ = spread(me, ring["sM"], column, *shapes["D"][:2])
            for n, (xs, y0, y1) in values.items():
                cross["x" + n], ring["y0" + n], ring["y1" + n] = xs, [y0], [y1]
        elif kind == "z1":
            near, far = cross["near_z" + g], cross["far_z" + g]
            ring[key] = [
                jnp.where(plan.yl == 0, jnp.concatenate([near, far]), jnp.concatenate([far, near]))
            ]

    panels = {}
    for entry in ORDER:
        if entry[0] == "c":
            kind, g = entry[1], entry[2]
            if kind == "x":
                need("x" + g)
            source = cross["x" + g] if kind == "x" else zpart[g]
            cross["near_" + kind + g] = queue.send(plan.halves(source)[1], "cross")
        elif entry[0] == "p":
            kind, g = entry[1], entry[2]
            cross["far_" + kind + g] = queue.send(cross["near_" + kind + g], "pair")
            if kind == "x":
                full = join_x(me, cross["x" + g], cross["near_x" + g], cross["far_x" + g])
                panels[g] = lax.all_gather(full, "x")
        else:
            key = entry[:-1]
            need(key)
            ring[key].append(queue.send(ring[key][-1], "y" if key[0] == "y" else "z"))
    chunks = []
    for g in "AGD":
        rows, cut, width = shapes[g]
        y, z = (ring["y0" + g], ring["y1" + g]), (ring["z0" + g], ring["z1" + g])
        chunks.append(Chunks(rows, cut, width, plan.places, panels[g], y, z))
    return chunks


def turn(value, cosine, sine):
    return value * cosine + pltpu.roll(value, 64, 1) * sine


def _pack_body(me, q, k, v, scales, gains, cosine, sine, out):
    c, s = cosine[...], sine[...]
    out[0, :, 0:HD] = turn(q[...] * scales[:, 0:1] * gains[0:1], c, s).astype(BF)
    out[0, :, HD : 2 * HD] = turn(k[...] * scales[:, 1:2] * gains[1:2], c, s).astype(BF)
    out[0, :, 2 * HD :] = v[...].astype(BF)


def pack_heads(me, qkv, scales, gains, cosine, sine):
    rows = qkv.shape[0]
    whole = lambda shape: pl.BlockSpec(shape, lambda i, me: (0, 0))
    return pl.pallas_call(
        _pack_body,
        out_shape=jax.ShapeDtypeStruct((8, rows, 3 * HD), BF),
        grid_spec=pltpu.PrefetchScalarGridSpec(
            num_scalar_prefetch=1,
            grid=(8,),
            in_specs=[
            pl.BlockSpec((rows, HD), lambda i, me: (0, i)),
            pl.BlockSpec((rows, HD), lambda i, me: (0, 8 + i)),
            pl.BlockSpec((rows, HD), lambda i, me: (0, 16 + i)),
            whole((rows, 2)),
            pl.BlockSpec((4, HD), lambda i, me: (0, 2 * i + me[CORE])),
            whole((rows, HD)),
            whole((rows, HD)),
        ],
            out_specs=pl.BlockSpec((1, rows, 3 * HD), lambda i, me: (i, 0, 0)),
        ),
        name="pack_heads",
    )(me, qkv, qkv, qkv, scales, gains, cosine, sine)


def _unpack_body(me, d, q, k, gains, cosine, sine, wq, wk, dv, sums):
    c, s = cosine[...], -sine[...]
    i = pl.program_id(0)
    gq = turn(d[0, :, 0:HD].astype(F32), c, s) * gains[0:1]
    gk = turn(d[0, :, HD : 2 * HD].astype(F32), c, s) * gains[1:2]
    wq[...] = gq
    wk[...] = gk
    dv[...] = d[0, :, 2 * HD :]

    @pl.when(i == 0)
    def _():
        sums[...] = jnp.zeros_like(sums)

    sums[:, 0:HD] += gq * q[...]
    sums[:, HD:] += gk * k[...]


def unpack_heads(me, d, qkv, gains, cosine, sine):
    rows = qkv.shape[0]
    whole = lambda shape: pl.BlockSpec(shape, lambda i, me: (0, 0))
    column = pl.BlockSpec((rows, HD), lambda i, me: (0, i))
    return pl.pallas_call(
        _unpack_body,
        out_shape=[
            jax.ShapeDtypeStruct((rows, HALF), F32),
            jax.ShapeDtypeStruct((rows, HALF), F32),
            jax.ShapeDtypeStruct((rows, HALF), BF),
            jax.ShapeDtypeStruct((rows, 2 * HD), F32),
        ],
        grid_spec=pltpu.PrefetchScalarGridSpec(
            num_scalar_prefetch=1,
            grid=(8,),
            in_specs=[
            pl.BlockSpec((1, rows, 3 * HD), lambda i, me: (i, 0, 0)),
            pl.BlockSpec((rows, HD), lambda i, me: (0, i)),
            pl.BlockSpec((rows, HD), lambda i, me: (0, 8 + i)),
            pl.BlockSpec((4, HD), lambda i, me: (0, 2 * i + me[CORE])),
            whole((rows, HD)),
            whole((rows, HD)),
        ],
            out_specs=[column, column, column, whole((rows, 2 * HD))],
        ),
        name="unpack_heads",
    )(me, d, qkv, qkv, gains, cosine, sine)


TILE = 128
NT = dict(dimension_numbers=(((1,), (1,)), ((), ())), preferred_element_type=F32)
TN = dict(dimension_numbers=(((0,), (0,)), ((), ())), preferred_element_type=F32)


def hidden_pairs(t, bound):
    query = t * TILE + lax.broadcasted_iota(jnp.int32, (TILE, TILE), 0)
    key = t * TILE + lax.broadcasted_iota(jnp.int32, (TILE, TILE), 1)
    hidden = key > query
    if t * TILE >= PROMPT:
        hidden = hidden | ((query >= bound) & (key < bound))
    return hidden


def tile_scores(q, k, t, bound):
    n = (t + 1) * TILE
    s = lax.dot_general(q[t * TILE : n], k[:n], **NT) * SCALE
    last = jnp.where(hidden_pairs(t, bound), -1e30, s[:, n - TILE :])
    return last if t == 0 else jnp.concatenate([s[:, : n - TILE], last], axis=1)


def _attend_body(bounds, qkv, out, exact, total):
    bound = bounds[pl.program_id(0)]
    q = qkv[:, 0, :, 0:HD].reshape(TOTAL, HD)
    k = qkv[:, 0, :, HD : 2 * HD].reshape(TOTAL, HD)
    v = qkv[:, 0, :, 2 * HD :].reshape(TOTAL, HD)
    for t in range(TOTAL // TILE):
        n = (t + 1) * TILE
        s = tile_scores(q, k, t, bound)
        top = jnp.max(s, axis=1, keepdims=True)
        p = jnp.exp(s - top)
        denom = jnp.sum(p, axis=1, keepdims=True)
        o = jnp.dot(p.astype(BF), v[:n], preferred_element_type=F32) / denom
        exact[0, t * TILE : n] = o
        total[0, t * TILE : n] = top + jnp.log(denom)
    out[:, 0] = exact[0].reshape(8, ROWS, HD).astype(BF)


def attend(bounds, qkv):
    return pl.pallas_call(
        _attend_body,
        grid=(2,),
        out_shape=[
            jax.ShapeDtypeStruct((8, 2, ROWS, HD), BF),
            jax.ShapeDtypeStruct((2, TOTAL, HD), F32),
            jax.ShapeDtypeStruct((2, TOTAL, 1), F32),
        ],
        in_specs=[
            pl.BlockSpec(memory_space=pltpu.SMEM),
            pl.BlockSpec((8, 1, ROWS, 3 * HD), lambda g: (0, g, 0, 0)),
        ],
        out_specs=[
            pl.BlockSpec((8, 1, ROWS, HD), lambda g: (0, g, 0, 0)),
            pl.BlockSpec((1, TOTAL, HD), lambda g: (g, 0, 0)),
            pl.BlockSpec((1, TOTAL, 1), lambda g: (g, 0, 0)),
        ],
        compiler_params=pltpu.CompilerParams(vmem_limit_bytes=40 * 2**20),
        cost_estimate=pl.CostEstimate(flops=900_000_000, bytes_accessed=5_000_000, transcendentals=1_500_000),
        name="attend",
    )(bounds, qkv)


def _attend_back_body(bounds, qkv, grad, exact, total, out, dk, dv, dq):
    bound = bounds[pl.program_id(0)]
    q = qkv[:, 0, :, 0:HD].reshape(TOTAL, HD)
    k = qkv[:, 0, :, HD : 2 * HD].reshape(TOTAL, HD)
    v = qkv[:, 0, :, 2 * HD :].reshape(TOTAL, HD)
    g = grad[:, 0].reshape(TOTAL, HD)
    dk[...] = jnp.zeros_like(dk)
    dv[...] = jnp.zeros_like(dv)
    for t in range(TOTAL // TILE):
        n = (t + 1) * TILE
        here = slice(t * TILE, n)
        s = tile_scores(q, k, t, bound)
        p = jnp.exp(s - total[0, here])
        delta = jnp.sum(g[here].astype(F32) * exact[0, here], axis=1, keepdims=True)
        dp = lax.dot_general(g[here], v[:n], **NT)
        ds = (p * (dp - delta)).astype(BF)
        dq[here] = jnp.dot(ds, k[:n], preferred_element_type=F32) * SCALE
        dk[:n] += lax.dot_general(ds, q[here], **TN) * SCALE
        dv[:n] += lax.dot_general(p.astype(BF), g[here], **TN)
    out[:, 0, :, 0:HD] = dq[...].reshape(8, ROWS, HD).astype(BF)
    out[:, 0, :, HD : 2 * HD] = dk[...].reshape(8, ROWS, HD).astype(BF)
    out[:, 0, :, 2 * HD :] = dv[...].reshape(8, ROWS, HD).astype(BF)


def attend_back(bounds, qkv, grad, exact, total):
    return pl.pallas_call(
        _attend_back_body,
        grid=(2,),
        out_shape=jax.ShapeDtypeStruct((8, 2, ROWS, 3 * HD), BF),
        in_specs=[
            pl.BlockSpec(memory_space=pltpu.SMEM),
            pl.BlockSpec((8, 1, ROWS, 3 * HD), lambda g: (0, g, 0, 0)),
            pl.BlockSpec((8, 1, ROWS, HD), lambda g: (0, g, 0, 0)),
            pl.BlockSpec((1, TOTAL, HD), lambda g: (g, 0, 0)),
            pl.BlockSpec((1, TOTAL, 1), lambda g: (g, 0, 0)),
        ],
        out_specs=pl.BlockSpec((8, 1, ROWS, 3 * HD), lambda g: (0, g, 0, 0)),
        scratch_shapes=[pltpu.VMEM((TOTAL, HD), F32)] * 3,
        compiler_params=pltpu.CompilerParams(vmem_limit_bytes=40 * 2**20),
        cost_estimate=pl.CostEstimate(flops=2_300_000_000, bytes_accessed=8_000_000, transcendentals=1_500_000),
        name="attend_back",
    )(bounds, qkv, grad, exact, total)


def dot(a, b):
    return jnp.dot(a, b, preferred_element_type=F32)


def dot_nt(a, b):
    return lax.dot_general(a, b, **NT)


def dot_tn(a, b):
    return lax.dot_general(a, b, **TN)


def normalize_back(field, inverse, gain, grad):
    weighted = grad * gain
    return inverse * weighted - field * inverse**3 * jnp.mean(weighted * field, axis=-1, keepdims=True)


def choose_adapters(slots, down_in, down_ff, up_model, up_hidden):
    def body(slots, down_in, down_ff, up_model, up_hidden, qkv_down, gu_down, out_down, ff_down, qkv_up, out_up, ff_up, gu_up):
        core = slots[2]
        qkv_down[...] = down_in[0, :3].reshape(3 * RANK, D)
        gu_down[...] = down_in[0, 4:].reshape(2 * RANK, D)
        out_up[...] = up_model[0, 3]
        ff_up[...] = up_model[0, 4]
        qkv_up[...] = jnp.zeros_like(qkv_up)
        gu_up[...] = jnp.zeros_like(gu_up)
        for h in range(8):
            head = pl.ds(pl.multiple_of((2 * h + core) * HD, HD), HD)
            out_down[:, HD * h : HD * (h + 1)] = down_in[0, 3, :, head]
            for n in range(3):
                here = slice(n * HALF + HD * h, n * HALF + HD * (h + 1))
                qkv_up[n * RANK : (n + 1) * RANK, here] = up_model[0, n, :, head]
        for m in range(FF // 128):
            start = (2 * (m // 4) + core) * 512 + (m % 4) * 128
            units = pl.ds(pl.multiple_of(start, 128), 128)
            ff_down[:, 128 * m : 128 * (m + 1)] = down_ff[0, :, units]
            for n in range(2):
                here = slice(256 * m + 128 * n, 256 * m + 128 * (n + 1))
                gu_up[n * RANK : (n + 1) * RANK, here] = up_hidden[0, n, :, units]

    def chosen(shape):
        return pl.BlockSpec((1,) + shape[1:], lambda g, slots: (slots[g],) + (0,) * (len(shape) - 1))

    shapes = [(48, D), (32, D), (16, HALF), (16, FF), (48, 3 * HALF), (16, D), (16, D), (32, 2 * FF)]
    maps = [down_in, down_ff, up_model, up_hidden]
    return pl.pallas_call(
        body,
        out_shape=[bf(2 * r, c) for r, c in shapes],
        grid_spec=pltpu.PrefetchScalarGridSpec(
            num_scalar_prefetch=1,
            grid=(2,),
            in_specs=[chosen(m.shape) for m in maps],
            out_specs=[pl.BlockSpec(shape, lambda g, slots: (g, 0)) for shape in shapes],
        ),
        cost_estimate=pl.CostEstimate(flops=0, bytes_accessed=7_000_000, transcendentals=0),
        name="choose_adapters",
    )(slots, *maps)


def rank_gradients(lows, acts, core, name, plan, width):
    def body(core, *refs):
        lows, acts, out = refs[: len(lows_)], refs[len(lows_) : -1], refs[-1]
        at = 0
        for low, act, column, stride, starts in plan:
            picked = jnp.concatenate(
                [lows[low][:, g * stride + column : g * stride + column + RANK] for g in range(2)], axis=1
            )
            for start in starts(core[0]):
                right = acts[act][:, start if isinstance(start, slice) else pl.ds(pl.multiple_of(start, 128), 128)]
                n = right.shape[1]
                grad = lax.dot_general(picked, right, **TN).astype(BF)
                for b in range(n // 128):
                    block, slot = divmod(at, width // 128)
                    out[block, :, 128 * slot : 128 * (slot + 1)] = grad[:, 128 * b : 128 * (b + 1)]
                    at += 1

    lows_ = lows
    return _plain(body, name, [bf(8, 2 * RANK, width)], list(lows) + list(acts), [core])[0]


def adapter_outputs(core, early, early_other, late, late_other):
    shapes = [(8, 6, RANK, D), (8, RANK, 2 * FF), (8, 5, RANK, D), (8, 2, RANK, 2 * FF)]

    def body(core, early, early_other, late, late_other, down_in, down_ff, up_model, up_hidden):
        for side, e, l in ((core[0], early, late), (1 - core[0], early_other, late_other)):

            def piece(half, at):
                block, slot = divmod(at, half.shape[3] // 128)
                return half[block, 0, :, 128 * slot : 128 * (slot + 1)].astype(F32)

            def place(start):
                return pl.ds(pl.multiple_of(start, 128), 128)

            for m in range(FF // 128):
                units = place((2 * (m // 4) + side) * 512 + (m % 4) * 128)
                up_hidden[0, 0, :, units] = piece(e, m)
                up_hidden[0, 1, :, units] = piece(e, 32 + m)
                down_ff[0, :, units] = piece(e, 64 + m)
            for m in range(8):
                whole, head = place(side * HALF + 128 * m), place((2 * m + side) * HD)
                down_in[0, 4, :, whole] = piece(e, 96 + m)
                down_in[0, 5, :, whole] = piece(e, 104 + m)
                down_in[0, 3, :, head] = piece(e, 112 + m)
                up_model[0, 3, :, whole] = piece(e, 120 + m)
                up_model[0, 4, :, whole] = piece(e, 128 + m)
                for n in range(3):
                    down_in[0, n, :, whole] = piece(l, 8 * n + m)
                    up_model[0, n, :, head] = piece(l, 24 + 8 * n + m)

    halves = [early, early_other, late, late_other]
    return pl.pallas_call(
        body,
        grid=(8,),
        out_shape=[jax.ShapeDtypeStruct(s, F32) for s in shapes],
        in_specs=[_smem()] + [pl.BlockSpec((8, 1) + v.shape[2:], lambda i: (0, i, 0, 0)) for v in halves],
        out_specs=[pl.BlockSpec((1,) + s[1:], lambda i, n=len(s): (i,) + (0,) * (n - 1)) for s in shapes],
        compiler_params=pltpu.CompilerParams(vmem_limit_bytes=40 * 2**20),
        cost_estimate=pl.CostEstimate(flops=0, bytes_accessed=37_000_000, transcendentals=0),
        name="adapter_outputs",
    )(core, *halves)


def on_device(
    tokens,
    cotangent,
    query_matrix,
    key_matrix,
    value_matrix,
    output_matrix,
    gate_matrix,
    upward_matrix,
    down_matrix,
    gains,
    adapter_down_inputs,
    adapter_down_feedforward,
    adapter_up_model_maps,
    adapter_up_hidden_maps,
    group_adapter_index,
    continuation_lengths,
):
    core = lax.axis_index("c")
    first = core == 0
    ctx = lax.axis_index("yl") * 4 + lax.axis_index("x")
    tokens, cotangent = tokens[0], cotangent[0]

    def both(own, other):
        return jnp.where(first, jnp.stack([own, other]), jnp.stack([other, own]))

    def rows_of_both(own):
        return both(own, swap(own)).reshape(2 * own.shape[0], own.shape[1])

    def mine(pair):
        return jnp.where(first, pair[0], pair[1])

    def exchange_sum(part):
        upper, lower = part[:ROWS], part[ROWS:]
        sent = jnp.where(first, lower, upper)
        kept = jnp.where(first, upper, lower)
        return kept.astype(F32) + swap(sent.astype(BF)).astype(F32)

    plan = Gather()
    keep_a, give_a = split_a(plan.me, query_matrix, key_matrix, value_matrix)
    keep_g, give_g = split_g(plan.me, gate_matrix, upward_matrix)
    got_a, got_g = swap(give_a), swap(give_g)
    wa, wg, wd = gather_weights(plan, (keep_a, got_a), output_matrix, (keep_g, got_g), down_matrix)
    wa = assemble(wa)
    w_qkv = wa[:, : 3 * HALF]
    w_out = wa[:, 3 * HALF :].reshape(8, 2, HD, HALF).transpose(0, 2, 1, 3).reshape(HALF, D)

    facts = jnp.concatenate([group_adapter_index[0], continuation_lengths[0]]).astype(F32)
    facts = jnp.broadcast_to(jnp.pad(facts, (0, 125))[None], (8, 128))
    pair_facts = both(facts, swap(facts))[:, 0, :2].astype(jnp.int32)
    slots = pair_facts[:, 0]
    bounds = PROMPT + pair_facts[:, 1]
    (qkv_down, gu_down, out_down, ff_down, qkv_up, out_up2, ff_up2, gu_up) = choose_adapters(
        jnp.concatenate([slots, plan.me[:1]]),
        adapter_down_inputs,
        adapter_down_feedforward,
        adapter_up_model_maps,
        adapter_up_hidden_maps,
    )

    def of_own(maps):
        n = maps.shape[0] // 2
        return lax.dynamic_slice_in_dim(maps, core * n, n, 0)

    group_row = lax.broadcasted_iota(jnp.int32, (2 * ROWS, 1), 0) // ROWS

    def own_columns(low, count):
        group_column = lax.broadcasted_iota(jnp.int32, (1, 2 * count), 1) // count
        return jnp.where(group_row == group_column, low, jnp.zeros_like(low))

    place = ctx * ROWS + lax.broadcasted_iota(jnp.int32, (2, ROWS), 1)
    position = jnp.where(place >= bounds[:, None], PROMPT + place - bounds[:, None], place)
    freq = BASE ** (-(jnp.arange(HD // 2, dtype=F32) * 2.0 / HD))
    angle = position.reshape(2 * ROWS, 1).astype(F32) * freq[None]
    cosine = jnp.concatenate([jnp.cos(angle)] * 2, axis=1)
    sine = jnp.concatenate([-jnp.sin(angle), jnp.sin(angle)], axis=1)

    x2 = rows_of_both(tokens)
    qkv_low = own_columns((2.0 * dot_nt(x2, qkv_down).astype(BF)).astype(BF), 3 * RANK)
    qkv = dot(x2, w_qkv) + dot(qkv_low, qkv_up)
    q_pre, k_pre = qkv[:, :HALF], qkv[:, HALF : 2 * HALF]
    squares = jnp.stack([jnp.sum(q_pre * q_pre, axis=1), jnp.sum(k_pre * k_pre, axis=1)])
    squares = squares + swap(squares)
    inverse = lax.rsqrt(squares.T / D + EPS)
    packed = pack_heads(plan.me, qkv, inverse, gains, cosine, sine)
    heads = lax.all_to_all(packed, CTX, 0, 0, tiled=True).reshape(8, 2, ROWS, 3 * HD)
    out_heads, exact, log_total = attend(bounds, heads)
    attended = lax.all_to_all(out_heads, CTX, 0, 0, tiled=True).reshape(8, 2 * ROWS, HD)
    attended = jnp.swapaxes(attended, 0, 1).reshape(2 * ROWS, HALF)

    def fold_groups(low, count):
        return low[:, :count] + low[:, count:]

    part = dot(attended, w_out)
    part_low = fold_groups(own_columns(dot_nt(attended, out_down), RANK), RANK)
    summed = exchange_sum(jnp.concatenate([part, jnp.pad(part_low, ((0, 0), (0, 112)))], axis=1))
    out_low = summed[:, D : D + RANK].astype(BF)
    out_up = of_own(out_up2)
    attn_pre = summed[:, :D] + 2.0 * dot(out_low, out_up)
    attn_inverse = lax.rsqrt(jnp.mean(attn_pre * attn_pre, axis=1, keepdims=True) + EPS)
    hidden = tokens.astype(F32) + attn_pre * attn_inverse * gains[2]

    h2 = rows_of_both(hidden.astype(BF))
    gu_low = own_columns((2.0 * dot_nt(h2, gu_down).astype(BF)).astype(BF), 2 * RANK)
    gu, mixed = gate_and_up(wg, h2, gu_low, gu_up)
    part = down(wd, mixed)
    part_low = fold_groups(own_columns(dot_nt(mixed, ff_down), RANK), RANK)
    summed = exchange_sum(jnp.concatenate([part, jnp.pad(part_low, ((0, 0), (0, 112)))], axis=1))
    ff_low = summed[:, D : D + RANK].astype(BF)
    ff_up = of_own(ff_up2)
    mlp_pre = summed[:, :D] + 2.0 * dot(ff_low, ff_up)
    mlp_inverse = lax.rsqrt(jnp.mean(mlp_pre * mlp_pre, axis=1, keepdims=True) + EPS)
    output = (hidden + mlp_pre * mlp_inverse * gains[3]).astype(BF)

    cot = cotangent.astype(F32)
    d_mlp = rows_of_both(normalize_back(mlp_pre, mlp_inverse, gains[3], cot).astype(BF))
    ff_grad_low = own_columns((2.0 * dot_nt(d_mlp, ff_up2)).astype(BF), RANK)
    d_gu = down_back(wd, d_mlp, ff_grad_low, ff_down, gu)
    part = gate_and_up_back(wg, d_gu)
    part_low = own_columns(dot_nt(d_gu, gu_up), 2 * RANK)
    part_low = fold_groups(part_low, 2 * RANK)
    summed = exchange_sum(jnp.concatenate([part, jnp.pad(part_low, ((0, 0), (0, 96)))], axis=1))
    gu_grad_low = (2.0 * summed[:, D : D + 2 * RANK]).astype(BF)
    gu_down_own = of_own(gu_down)
    d_hidden = cot + summed[:, :D] + dot(gu_grad_low, gu_down_own)

    d_attn = rows_of_both(normalize_back(attn_pre, attn_inverse, gains[2], d_hidden).astype(BF))
    out_grad_low = own_columns((2.0 * dot_nt(d_attn, out_up2)).astype(BF), RANK)
    d_attended = (dot_nt(d_attn, w_out) + dot(out_grad_low, out_down)).astype(BF)
    d_out_heads = jnp.swapaxes(d_attended.reshape(2 * ROWS, 8, HD), 0, 1)
    d_out_heads = lax.all_to_all(d_out_heads, CTX, 0, 0, tiled=True).reshape(8, 2, ROWS, HD)
    d_heads = attend_back(bounds, heads, d_out_heads, exact, log_total)
    d_heads = lax.all_to_all(d_heads, CTX, 0, 0, tiled=True).reshape(8, 2 * ROWS, 3 * HD)
    w_q, w_k, d_v, sums = unpack_heads(plan.me, d_heads, qkv, gains, cosine, sine)
    sums = jnp.stack([jnp.sum(sums[:, :HD], axis=1), jnp.sum(sums[:, HD:], axis=1)])
    sums = ((sums + swap(sums)) / D).T
    d_q = inverse[:, :1] * w_q - q_pre * (inverse[:, :1] ** 3 * sums[:, :1])
    d_k = inverse[:, 1:] * w_k - k_pre * (inverse[:, 1:] ** 3 * sums[:, 1:])
    d_qkv = jnp.concatenate([d_q.astype(BF), d_k.astype(BF), d_v], axis=1)
    part = dot_nt(d_qkv, w_qkv)
    part_low = fold_groups(own_columns(dot_nt(d_qkv, qkv_up), 3 * RANK), 3 * RANK)
    summed = exchange_sum(jnp.concatenate([part, jnp.pad(part_low, ((0, 0), (0, 80)))], axis=1))
    qkv_grad_low = (2.0 * summed[:, D : D + 3 * RANK]).astype(BF)
    qkv_down_own = of_own(qkv_down)
    grad_tokens = (d_hidden + summed[:, :D] + dot(qkv_grad_low, qkv_down_own)).astype(BF)

    def low_of_both(own, count):
        pair = rows_of_both(jnp.pad(own, ((0, 0), (0, 128 - count))))[:, :count]
        return own_columns(jnp.concatenate([pair, pair], axis=1), count)

    def whole(n):
        return lambda core: [slice(0, n)]

    def half(core):
        return [core * HALF + 128 * m for m in range(8)]

    def turns(n):
        return lambda core: [slice(256 * m + 128 * n, 256 * m + 128 * (n + 1)) for m in range(FF // 128)]

    def third(n):
        return lambda core: [slice(n * HALF, (n + 1) * HALF)]

    shard = ("z", "yh")
    early = rank_gradients(
        [gu_low, ff_grad_low, low_of_both(gu_grad_low, 2 * RANK), out_grad_low]
        + [2 * low_of_both(out_low, RANK), 2 * low_of_both(ff_low, RANK)],
        [d_gu, mixed, h2, attended, d_attn, d_mlp],
        plan.me,
        "early_gradients",
        [
            (0, 0, 0, 2 * RANK, turns(0)),
            (0, 0, RANK, 2 * RANK, turns(1)),
            (1, 1, 0, RANK, whole(FF)),
            (2, 2, 0, 2 * RANK, half),
            (2, 2, RANK, 2 * RANK, half),
            (3, 3, 0, RANK, whole(HALF)),
            (4, 4, 0, RANK, half),
            (5, 5, 0, RANK, half),
        ],
        EARLY,
    )
    own = lax.psum_scatter(early.reshape(8 * 2 * RANK, EARLY), CTX, scatter_dimension=0, tiled=True)
    own_slot = jnp.repeat(slots, RANK)[:, None] == lax.broadcasted_iota(jnp.int32, (1, 128), 1)
    own = jnp.concatenate([own, own_slot.astype(BF)], axis=1)
    groups = lax.all_gather(own, shard).reshape(16, RANK, EARLY + 128)
    picker = groups[:, 0, EARLY : EARLY + 8]

    def by_slot(groups):
        flat = groups.reshape(16, -1)
        return lax.dot_general(picker, flat, **TN).astype(BF).reshape(8 * RANK, -1)

    early = lax.all_gather(by_slot(groups[:, :, :EARLY]), CTX)
    early_other = swap(early)
    qkv_grad_low2 = low_of_both(qkv_grad_low, 3 * RANK)
    late = rank_gradients(
        [qkv_grad_low2, qkv_low],
        [x2, d_qkv],
        plan.me,
        "late_gradients",
        [(0, 0, n * RANK, 3 * RANK, half) for n in range(3)] + [(1, 1, n * RANK, 3 * RANK, third(n)) for n in range(3)],
        LATE,
    )

    def spread_over(value, axes):
        return lax.all_to_all(jnp.broadcast_to(value[None], (8,) + value.shape), axes, 0, 0, tiled=True)

    late = lax.all_to_all(late, CTX, 0, 0, tiled=True)
    late = jnp.sum(late.astype(F32), axis=0).astype(BF)
    late = by_slot(spread_over(late, shard).reshape(16, RANK, LATE))
    late = spread_over(late, CTX)
    late_other = swap(late)
    grads = adapter_outputs(
        plan.me,
        early.reshape(8, 8, RANK, EARLY),
        early_other.reshape(8, 8, RANK, EARLY),
        late.reshape(8, 8, RANK, LATE),
        late_other.reshape(8, 8, RANK, LATE),
    )
    return (output[None], grad_tokens[None], *grads)


def solution(mesh):
    fine = Mesh(mesh.devices.reshape(2, 4, 4, 2, 2), ALL)
    shard = ("z", "yh", "c")
    rows = P(shard, None)
    per_token = P(shard, CTX, None)
    return jax.shard_map(
        on_device,
        mesh=fine,
        in_specs=(per_token, per_token) + (rows,) * 7 + (P(),) * 5 + (rows, rows),
        out_specs=(per_token, per_token, P(), P(), P(), P()),
        check_vma=False,
    )
```

```python
import jax
import jax.numpy as jnp
from jax import lax
from jax.experimental import pallas as pl
from jax.experimental.pallas import tpu as pltpu
from jax.sharding import Mesh, PartitionSpec as P

HD = 128
PROMPT = 1024
ROWS = 144
TOTAL = 1152
D = 2048
HALF = 1024
FF = 4096
RANK = 16
SCALE = HD**-0.5
EPS = 1e-06
BASE = 500000.0
ALL = ("yl", "x", "z", "yh", "c")
CTX = ("yl", "x")
BF = jnp.bfloat16
F32 = jnp.float32
CUT_A, CUT_G, CUT_D = 2048, 5120, 1536
EARLY, LATE = 1664, 1280


NT = dict(dimension_numbers=(((1,), (1,)), ((), ())), preferred_element_type=F32)
TN = dict(dimension_numbers=(((0,), (0,)), ((), ())), preferred_element_type=F32)


CORE, X, YL, YH, Z0 = 0, 1, 2, 3, 4


def _place(yl, x, z, yh, c):
    return (((yl * 4 + x) * 4 + z) * 2 + yh) * 2 + c


def _permutation(move):
    pairs = []
    for yl in range(2):
        for x in range(4):
            for z in range(4):
                for yh in range(2):
                    for c in range(2):
                        nx, ny, nz, nc = move(x, 2 * yh + yl, z, c)
                        pairs.append(
                            (_place(yl, x, z, yh, c), _place(ny % 2, nx % 4, nz % 4, (ny % 4) // 2, nc))
                        )
    return pairs


STEPS = {
    "y": _permutation(lambda x, y, z, c: (x, (y + 1 - 2 * c) % 4, z, c)),
    "z": _permutation(lambda x, y, z, c: (x, y, z + 1 - 2 * c, c)),
    "cross": _permutation(lambda x, y, z, c: (x, 3 - y, z, c)),
    "core": _permutation(lambda x, y, z, c: (x, y, z, 1 - c)),
}


def swap(value):
    return lax.ppermute(value, ALL, STEPS["core"])


class Lane:
    def __init__(self):
        self.last = None

    def send(self, value, how):
        if self.last is not None:
            value, _ = lax.optimization_barrier((value, self.last))
        self.last = lax.ppermute(value, ALL, STEPS[how])
        return self.last


def after(value, *others):
    return lax.optimization_barrier((value, *others))[0]


def _smem():
    return pl.BlockSpec(memory_space=pltpu.SMEM)


def _vmem():
    return pl.BlockSpec(memory_space=pltpu.VMEM)


def _plain(body, name, outs, ins, scalars, scratch=(), limit=48):
    size = sum(v.size * v.dtype.itemsize for v in list(ins) + list(outs))
    return pl.pallas_call(
        body,
        out_shape=outs,
        in_specs=[_smem()] * len(scalars) + [_vmem()] * len(ins),
        out_specs=[_vmem()] * len(outs),
        scratch_shapes=list(scratch),
        compiler_params=pltpu.CompilerParams(vmem_limit_bytes=limit * 2**20),
        cost_estimate=pl.CostEstimate(flops=0, bytes_accessed=size, transcendentals=0),
        name=name,
    )(*scalars, *ins)


def bf(*shape):
    return jax.ShapeDtypeStruct(shape, BF)


def split_a(core, q, k, v):
    def body(core, q, k, v, keep, give):
        for n, w in enumerate((q, k, v)):
            for h in range(8):
                here = slice(n * HALF + HD * h, n * HALF + HD * (h + 1))
                keep[:, here] = w[:, pl.ds(pl.multiple_of((2 * h + core[0]) * HD, HD), HD)]
                give[:, here] = w[:, pl.ds(pl.multiple_of((2 * h + 1 - core[0]) * HD, HD), HD)]

    return _plain(body, "split_a", [bf(HD, 3 * HALF)] * 2, [q, k, v], [core])


def split_g(core, gate, upward):
    def body(core, gate, upward, keep, give):
        for m in range(FF // 128):
            for n, w in enumerate((gate, upward)):
                here = slice(256 * m + 128 * n, 256 * m + 128 * (n + 1))
                for side, out in ((core[0], keep), (1 - core[0], give)):
                    start = (2 * (m // 4) + side) * 512 + (m % 4) * 128
                    out[:, here] = w[:, pl.ds(pl.multiple_of(start, 128), 128)]

    return _plain(body, "split_g", [bf(HD, 2 * FF)] * 2, [gate, upward], [core])


def parts_a(me, keep, got, out):
    quarter = CUT_A // 4

    def body(me, keep, got, out, xs, ys):
        for side, w in ((me[CORE], keep), (1 - me[CORE], got)):
            rows = pl.ds(pl.multiple_of(side * HD, HD), HD)
            xs[rows, :] = w[:, pl.ds(pl.multiple_of(me[X] * quarter, 128), quarter)]

            @pl.when(me[YL] == 0)
            def _():
                ys[rows, :] = w[:, 2 * HALF :]

        @pl.when(me[YL] == 1)
        def _():
            ys[:HD, :] = out[:, :HALF]
            ys[HD:, :] = out[:, HALF:]

    return _plain(body, "parts_a", [bf(256, quarter), bf(256, HALF)], [keep, got, out], [me])


def parts_m(me, keep, got, down):
    gx, dx = CUT_G // 4, CUT_D // 4
    gy, dy = FF - CUT_G // 2, HALF - CUT_D // 2

    def body(me, keep, got, down, xs, yg, yd):
        for side, w in ((me[CORE], keep), (1 - me[CORE], got)):
            rows = pl.ds(pl.multiple_of(side * HD, HD), HD)
            xs[rows, :gx] = w[:, pl.ds(pl.multiple_of(me[X] * gx, 128), gx)]
            yg[rows, :] = w[:, pl.ds(pl.multiple_of(CUT_G + me[YL] * gy, 128), gy)]
        for n in range(2):
            rows = slice(256 * n, 256 * (n + 1))
            xs[:, gx + n * dx : gx + (n + 1) * dx] = down[rows, pl.ds(pl.multiple_of(me[X] * dx, 128), dx)]
            yd[:, n * dy : (n + 1) * dy] = down[rows, pl.ds(pl.multiple_of(CUT_D + me[YL] * dy, 128), dy)]

    outs = [bf(256, gx + 2 * dx), bf(256, gy), bf(256, 2 * dy)]
    return _plain(body, "parts_m", outs, [keep, got, down], [me])


def spread(me, got, pieces, name):
    def body(me, *refs):
        chunks, outs = refs[:4], refs[4:]
        for k in range(4):
            z = me[Z0 + k]
            for p, (column, width, folds) in enumerate(pieces):
                for half in range(2):

                    @pl.when(z // 2 == half)
                    def _():
                        for n in range(folds):
                            at = pl.multiple_of(((z - 2 * half) * folds + n) * 256, 256)
                            start = column + n * width
                            outs[2 * p + half][pl.ds(at, 256), :] = chunks[k][:, start : start + width]

    outs = [bf(2 * folds * 256, width) for _, width, folds in pieces for _ in range(2)]
    return _plain(body, name, outs, list(got), [me])


class Chunks:
    def __init__(self, rows, cut, width, places, xs, column, y):
        self.rows, self.cx, self.cy = rows, cut, width - cut
        self.depth = 8 * rows
        self.places = places
        self.column = column
        self.arrays = [xs] + y[0] + y[1]


def _y_rows(places, rows, half, j, k):
    return pl.multiple_of((2 * half + j) * 2 * rows + places[0, k] * rows, rows)


def _copies(w, places, refs, whole):
    xs, y = refs[0], refs[1:9]
    quarter, half_width = w.cx // 4, w.cy // 2
    folds = w.rows // 256
    panels = []
    for k in range(4):
        panel = []
        for z in range(4):
            for yh in range(2):
                for n in range(folds):
                    target = whole.at[pl.ds((2 * z + yh) * w.rows + 256 * n, 256), pl.ds(k * quarter, quarter)]
                    panel.append((xs.at[k, z, yh, :, pl.ds(w.column + n * quarter, quarter)], target))
        panels.append(panel)
    chunks = []
    for k in range(4):
        column = pl.multiple_of(w.cx + places[1, k] * half_width, 128)
        for half in range(2):
            for j in range(2):
                row = _y_rows(places, w.rows, half, j, k)
                chunks.append(
                    (
                        y[4 * half + k].at[pl.ds(j * w.rows, w.rows)],
                        whole.at[pl.ds(row, w.rows), pl.ds(column, half_width)],
                    )
                )
    return panels, chunks


def assemble(w):
    anywhere = pl.BlockSpec(memory_space=pl.ANY)

    def body(places, *refs):
        out, out_matrix, sems = refs[9], refs[10], refs[11]
        panels, chunks = _copies(w, places, refs[:9], out)
        plain = [pltpu.make_async_copy(a, b, sems.at[n]) for n, (a, b) in enumerate(sum(panels, []))]
        for copy in plain:
            copy.start()

        def move(started):
            at = len(plain)
            for k in range(4):
                for half in range(2):
                    for j in range(2):
                        source = refs[1 + 4 * half + k].at[pl.ds(j * 256, 256)]
                        block = 2 * (2 * half + j) + places[0, k]

                        @pl.when(places[1, k] == 0)
                        def _():
                            row = pl.multiple_of(block * 256, 256)
                            target = out.at[pl.ds(row, 256), pl.ds(2 * HALF, HALF)]
                            copy = pltpu.make_async_copy(source, target, sems.at[at])
                            copy.wait() if started else copy.start()

                        @pl.when(places[1, k] == 1)
                        def _():
                            for n in range(2):
                                row = pl.multiple_of(block * HD, HD)
                                target = out_matrix.at[pl.ds(row, HD), pl.ds(n * HALF, HALF)]
                                copy = pltpu.make_async_copy(source.at[pl.ds(n * HD, HD)], target, sems.at[at + n])
                                copy.wait() if started else copy.start()

                        at += 2

        move(False)
        for copy in plain:
            copy.wait()
        move(True)

    return pl.pallas_call(
        body,
        out_shape=[bf(D, 3 * HALF), bf(HALF, D)],
        in_specs=[_smem()] + [anywhere] * 9,
        out_specs=[_vmem()] * 2,
        scratch_shapes=[pltpu.SemaphoreType.DMA((64,))],
        compiler_params=pltpu.CompilerParams(vmem_limit_bytes=48 * 2**20),
        cost_estimate=pl.CostEstimate(flops=0, bytes_accessed=64 * 2**20, transcendentals=0),
        name="assemble",
    )(w.places, *w.arrays)


class Resident:
    def __init__(self, w, panels):
        self.w = w
        self.panels = panels
        step = w.cx // 4 * panels
        self.pieces = [(n * step, step) for n in range(4 // panels)] + [(w.cx, w.cy)]

    def scratch(self):
        w = self.w
        return [pltpu.VMEM((w.depth, w.cx + w.cy), BF), pltpu.SemaphoreType.DMA((80,))]

    def start(self, places, refs, whole, sems):
        panels, chunks = _copies(self.w, places, refs, whole)
        n = self.panels
        pieces = [sum(panels[k : k + n], []) for k in range(0, 4, n)] + [chunks]
        numbers = [sum(len(p) for p in pieces[:n]) for n in range(len(pieces))]
        copies = [
            [pltpu.make_async_copy(a, b, sems.at[first + m]) for m, (a, b) in enumerate(piece)]
            for first, piece in zip(numbers, pieces)
        ]

        def begin(n):
            if n < len(copies):
                for copy in copies[n]:
                    copy.start()

        def arrive(n):
            for copy in copies[n]:
                copy.wait()

        begin(0)
        begin(1)
        return begin, arrive

    def forward(self, places, refs, whole, sems, first, x, tile, finish):
        begin, arrive = self.start(places, refs, whole, sems)
        first()
        for n, (start, width) in enumerate(self.pieces):
            arrive(n)
            begin(n + 2)
            for column in range(start, start + width, tile):
                size = min(tile, start + width - column)
                finish(jnp.dot(x[...], whole[:, column : column + size], preferred_element_type=F32), column)

    def backward(self, places, refs, whole, sems, first, dy, tile, finish):
        begin, arrive = self.start(places, refs, whole, sems)
        first()
        for n, (start, width) in enumerate(self.pieces):
            arrive(n)
            begin(n + 2)
            left = dy[:, start : start + width]
            for row in range(0, self.w.depth, tile):
                finish(lax.dot_general(left, whole[row : row + tile, start : start + width], **NT), row, n)

    def call(self, body, name, ins, outs, flops, scratch=()):
        w = self.w
        anywhere = pl.BlockSpec(memory_space=pl.ANY)
        size = 2 * w.depth * (w.cx + w.cy) + sum(v.size * v.dtype.itemsize for v in ins)
        return pl.pallas_call(
            body,
            out_shape=outs,
            in_specs=[_smem()] + [anywhere] * 9 + [_vmem()] * len(ins),
            out_specs=[_vmem()] * len(outs),
            scratch_shapes=self.scratch() + list(scratch),
            compiler_params=pltpu.CompilerParams(vmem_limit_bytes=60 * 2**20),
            cost_estimate=pl.CostEstimate(flops=flops, bytes_accessed=size, transcendentals=0),
            name=name,
        )(w.places, *w.arrays, *ins)


WIDE = D + 128


def _f32(*shape):
    return jax.ShapeDtypeStruct(shape, F32)


def _pair_up(core, own, other, pair):
    pair[pl.ds(pl.multiple_of(core * ROWS, ROWS), ROWS), :] = own[...]
    pair[pl.ds(pl.multiple_of((1 - core) * ROWS, ROWS), ROWS), :] = other[...]


def _split(core, sums, keep, give):
    keep[...] = sums[pl.ds(pl.multiple_of(core * ROWS, ROWS), ROWS), :]
    give[...] = sums[pl.ds(pl.multiple_of((1 - core) * ROWS, ROWS), ROWS), :].astype(BF)


def _in_group(rows, columns, count):
    row = lax.broadcasted_iota(jnp.int32, (rows, columns), 0) >= ROWS
    column = lax.broadcasted_iota(jnp.int32, (rows, columns), 1) >= count
    return row == column


def _own_group(low, count):
    row = lax.broadcasted_iota(jnp.int32, (low.shape[0], count), 0)
    return jnp.where(row >= ROWS, low[:, count:], low[:, :count])


def _put_low(sums, low):
    count = low.shape[1]
    sums[:, D:] = jnp.zeros((sums.shape[0], WIDE - D), F32)
    sums[:, D : D + count] = low


def gate_and_up(w, own, other, maps_down, maps_up):
    rows = 2 * ROWS
    plan = Resident(w, 1)

    def body(places, *refs):
        weights, (own_ref, other_ref, down_ref, up_ref, gu, mixed, pair, low_ref, whole, sems) = refs[:9], refs[9:]

        def first():
            _pair_up(places[2, 0], own_ref, other_ref, pair)
            low = 2.0 * lax.dot_general(pair[:, :D], down_ref[...], **NT).astype(BF).astype(F32)
            low_ref[...] = jnp.where(_in_group(rows, 4 * RANK, 2 * RANK), low, 0.0).astype(BF)

        def finish(total, column):
            width = total.shape[1]
            total = total + jnp.dot(low_ref[...], up_ref[:, column : column + width], preferred_element_type=F32)
            gu[:, column : column + width] = total.astype(BF)
            unit = column // 2
            for m in range(width // 256):
                g, u = total[:, 256 * m : 256 * m + 128], total[:, 256 * m + 128 : 256 * m + 256]
                mixed[:, unit + 128 * m : unit + 128 * (m + 1)] = (g * jax.nn.sigmoid(g) * u).astype(BF)

        plan.forward(places, weights, whole, sems, first, pair.at[:, pl.ds(0, D)], 768, finish)

    outs = [bf(rows, 2 * FF), bf(rows, FF), bf(rows, WIDE), bf(rows, 4 * RANK)]
    return plan.call(body, "gate_and_up", [own, other, maps_down, maps_up], outs, 2 * rows * D * 2 * FF)


def down(w, x, maps_down):
    rows = x.shape[0]
    plan = Resident(w, 2)

    def body(places, *refs):
        weights, (x_ref, down_ref, keep, give, whole, sems, sums) = refs[:9], refs[9:]

        def first():
            _put_low(sums, _own_group(lax.dot_general(x_ref[...], down_ref[...], **NT), RANK))

        def finish(total, column):
            sums[:, column : column + total.shape[1]] = total

        plan.forward(places, weights, whole, sems, first, x_ref, 512, finish)
        _split(places[2, 0], sums, keep, give)

    outs = [_f32(ROWS, WIDE), bf(ROWS, WIDE)]
    return plan.call(body, "down", [x, maps_down], outs, 2 * rows * D * FF, [pltpu.VMEM((rows, WIDE), F32)])


def down_back(w, own, other, maps_up, maps_down, gu):
    rows = 2 * ROWS
    plan = Resident(w, 4)

    def body(places, *refs):
        weights, (own_ref, other_ref, up_ref, down_ref, gu_ref, out, pair, low_ref, whole, sems, sums) = refs[:9], refs[9:]

        def first():
            _pair_up(places[2, 0], own_ref, other_ref, pair)
            low = 2.0 * lax.dot_general(pair[:, :D], up_ref[...], **NT)
            low_ref[...] = jnp.where(_in_group(rows, 2 * RANK, RANK), low, 0.0).astype(BF)

        def finish(part_sum, row, part):
            units = slice(row, row + part_sum.shape[1])
            if part == 0:
                sums[:, units] = part_sum + jnp.dot(low_ref[...], down_ref[:, units], preferred_element_type=F32)
            else:
                d_mixed = sums[:, units] + part_sum
                column = 2 * row
                for m in range(part_sum.shape[1] // 128):
                    g = gu_ref[:, column + 256 * m : column + 256 * m + 128].astype(F32)
                    u = gu_ref[:, column + 256 * m + 128 : column + 256 * (m + 1)].astype(F32)
                    d = d_mixed[:, 128 * m : 128 * (m + 1)]
                    s = jax.nn.sigmoid(g)
                    out[:, column + 256 * m : column + 256 * m + 128] = (d * u * s * (1.0 + g * (1.0 - s))).astype(BF)
                    out[:, column + 256 * m + 128 : column + 256 * (m + 1)] = (d * g * s).astype(BF)

        plan.backward(places, weights, whole, sems, first, pair, 1024, finish)

    outs = [bf(rows, 2 * FF), bf(rows, WIDE), bf(rows, 2 * RANK)]
    scratch = [pltpu.VMEM((rows, FF), F32)]
    return plan.call(body, "down_back", [own, other, maps_up, maps_down, gu], outs, 2 * rows * D * FF, scratch)


def gate_and_up_back(w, dy, maps_up):
    rows = dy.shape[0]
    plan = Resident(w, 2)

    def body(places, *refs):
        weights, (dy_ref, up_ref, keep, give, whole, sems, sums) = refs[:9], refs[9:]

        def first():
            _put_low(sums, _own_group(lax.dot_general(dy_ref[...], up_ref[...], **NT), 2 * RANK))

        def finish(part_sum, row, part):
            units = slice(row, row + part_sum.shape[1])
            if part == 0:
                sums[:, units] = part_sum
            else:
                sums[:, units] += part_sum

        plan.backward(places, weights, whole, sems, first, dy_ref, 1024, finish)
        _split(places[2, 0], sums, keep, give)

    outs = [_f32(ROWS, WIDE), bf(ROWS, WIDE)]
    return plan.call(
        body, "gate_and_up_back", [dy, maps_up], outs, 2 * rows * D * 2 * FF, [pltpu.VMEM((rows, WIDE), F32)]
    )


def project_qkv(x, w, low, maps_up):
    rows, tile = x.shape[0], 512

    def body(x, w, low, up, out, squares):
        i = pl.program_id(0)

        @pl.when(i == 0)
        def _():
            squares[...] = jnp.zeros_like(squares)

        total = jnp.dot(x[...], w[...], preferred_element_type=F32)
        total = total + jnp.dot(low[...], up[...], preferred_element_type=F32)
        out[...] = total
        here = lax.broadcasted_iota(jnp.int32, squares.shape, 1) == i // 2
        squares[...] += jnp.where(here, jnp.sum(total * total, axis=1, keepdims=True), 0.0)

    whole = lambda v: pl.BlockSpec(v.shape, lambda i: (0, 0))
    column = lambda n: pl.BlockSpec((n, tile), lambda i: (0, i))
    return pl.pallas_call(
        body,
        grid=(3 * HALF // tile,),
        out_shape=[_f32(rows, 3 * HALF), _f32(rows, 128)],
        in_specs=[whole(x), column(D), whole(low), column(maps_up.shape[0])],
        out_specs=[column(rows), pl.BlockSpec((rows, 128), lambda i: (0, 0))],
        compiler_params=pltpu.CompilerParams(vmem_limit_bytes=32 * 2**20),
        cost_estimate=pl.CostEstimate(flops=2 * rows * D * 3 * HALF, bytes_accessed=18_000_000, transcendentals=0),
        name="project_qkv",
    )(x, w, low, maps_up)


def project_out(me, heads, w, maps_down):
    rows = 2 * ROWS

    def body(me, heads, w, down, keep, give, flat, sums):
        flat[...] = jnp.concatenate([heads[h] for h in range(8)], axis=1)
        for n in range(0, D, 512):
            sums[:, n : n + 512] = jnp.dot(flat[...], w[:, n : n + 512], preferred_element_type=F32)
        _put_low(sums, _own_group(lax.dot_general(flat[...], down[...], **NT), RANK))
        _split(me[CORE], sums, keep, give)

    outs = [_f32(ROWS, WIDE), bf(ROWS, WIDE), bf(rows, HALF)]
    return _plain(body, "project_out", outs, [heads, w, maps_down], [me], [pltpu.VMEM((rows, WIDE), F32)])


def _low_and_sum(me, keep, got, maps, count, factor):
    total = keep[...] + got[...].astype(F32)
    low = (factor * total[:, D : D + count]).astype(BF)
    start = pl.multiple_of(me[CORE] * count, count)
    return total[:, :D], low, jnp.dot(low, maps[pl.ds(start, count), :], preferred_element_type=F32)


def _send(out, value, low):
    out[:, :D] = value.astype(BF)
    out[:, D:] = jnp.zeros((ROWS, WIDE - D), BF)
    out[:, D : D + low.shape[1]] = low


def _inverse(field):
    return lax.rsqrt(jnp.mean(field * field, axis=1, keepdims=True) + EPS)


def combine_attention(me, keep, got, tokens, gains, maps_up):
    def body(me, keep, got, tokens, gains, up, pre, hidden, out):
        total, low, raised = _low_and_sum(me, keep, got, up, RANK, 1.0)
        field = total + 2.0 * raised
        pre[...] = field
        value = tokens[...].astype(F32) + field * _inverse(field) * gains[2:3]
        hidden[...] = value
        _send(out, value, low)

    outs = [_f32(ROWS, D), _f32(ROWS, D), bf(ROWS, WIDE)]
    return _plain(body, "combine_attention", outs, [keep, got, tokens, gains, maps_up], [me])


def combine_output(me, keep, got, hidden, cotangent, gains, maps_up):
    def body(me, keep, got, hidden, cotangent, gains, up, output, out):
        total, low, raised = _low_and_sum(me, keep, got, up, RANK, 1.0)
        field = total + 2.0 * raised
        inverse = _inverse(field)
        output[...] = (hidden[...] + field * inverse * gains[3:4]).astype(BF)
        _send(out, normalize_back(field, inverse, gains[3:4], cotangent[...].astype(F32)), low)

    outs = [bf(ROWS, D), bf(ROWS, WIDE)]
    return _plain(body, "combine_output", outs, [keep, got, hidden, cotangent, gains, maps_up], [me])


def combine_hidden(me, keep, got, cotangent, pre, gains, maps_down):
    def body(me, keep, got, cotangent, pre, gains, down, hidden, out):
        total, low, lowered = _low_and_sum(me, keep, got, down, 2 * RANK, 2.0)
        value = cotangent[...].astype(F32) + total + lowered
        hidden[...] = value
        field = pre[...]
        _send(out, normalize_back(field, _inverse(field), gains[2:3], value), low)

    outs = [_f32(ROWS, D), bf(ROWS, WIDE)]
    return _plain(body, "combine_hidden", outs, [keep, got, cotangent, pre, gains, maps_down], [me])


def combine_tokens(me, keep, got, hidden, maps_down):
    def body(me, keep, got, hidden, down, out, low_out):
        total, low, lowered = _low_and_sum(me, keep, got, down, 3 * RANK, 2.0)
        out[...] = (hidden[...] + total + lowered).astype(BF)
        low_out[...] = jnp.zeros_like(low_out)
        low_out[:, : 3 * RANK] = low

    outs = [bf(ROWS, D), bf(ROWS, 128)]
    return _plain(body, "combine_tokens", outs, [keep, got, hidden, maps_down], [me])


def project_out_back(me, own, other, w, maps_up, maps_down):
    rows = 2 * ROWS

    def body(me, own, other, w, up, down, heads, pair, low_ref):
        _pair_up(me[CORE], own, other, pair)
        low = 2.0 * lax.dot_general(pair[:, :D], up[...], **NT)
        low_ref[...] = jnp.where(_in_group(rows, 2 * RANK, RANK), low, 0.0).astype(BF)
        for n in range(0, HALF, 512):
            total = lax.dot_general(pair[:, :D], w[n : n + 512, :], **NT)
            total = total + jnp.dot(low_ref[...], down[:, n : n + 512], preferred_element_type=F32)
            for h in range(4):
                heads[n // HD + h] = total[:, h * HD : (h + 1) * HD].astype(BF)

    outs = [bf(8, rows, HD), bf(rows, WIDE), bf(rows, 2 * RANK)]
    return _plain(body, "project_out_back", outs, [own, other, w, maps_up, maps_down], [me])


def project_qkv_back(me, weighted, value_grad, qkv, squares, sums, w, maps_up):
    rows, tile = 2 * ROWS, 512

    def body(me, wq, wk, dv, q, k, sq, sq_other, su, su_other, w, up, d_qkv, keep, give, acc):
        i = pl.program_id(0)

        @pl.when(i == 0)
        def _():
            inverse = lax.rsqrt((sq[...] + sq_other[...]) / D + EPS)
            mean = (su[...] + su_other[...]) / D
            for n, (weight, field) in enumerate(((wq, q), (wk, k))):
                r, m = inverse[:, n : n + 1], mean[:, n : n + 1]
                d_qkv[:, n * HALF : (n + 1) * HALF] = (r * weight[...] - field[...] * (r * r * r * m)).astype(BF)
            d_qkv[:, 2 * HALF :] = dv[...]
            _put_low(acc, _own_group(lax.dot_general(d_qkv[...], up[...], **NT), 3 * RANK))

        acc[:, pl.ds(pl.multiple_of(i * tile, tile), tile)] = lax.dot_general(d_qkv[...], w[...], **NT)

        @pl.when(i == D // tile - 1)
        def _():
            _split(me[CORE], acc, keep, give)

    once = lambda v: pl.BlockSpec(v.shape, lambda i: (0, 0), pipeline_mode=pl.Buffered(1))
    third = lambda n: pl.BlockSpec((rows, HALF), lambda i: (0, n), pipeline_mode=pl.Buffered(1))
    ins = [*weighted, value_grad]
    return pl.pallas_call(
        body,
        grid=(D // tile,),
        out_shape=[bf(rows, 3 * HALF), _f32(ROWS, WIDE), bf(ROWS, WIDE)],
        in_specs=[_smem()]
        + [once(v) for v in ins]
        + [third(0), third(1)]
        + [once(v) for v in (*squares, *sums)]
        + [pl.BlockSpec((tile, 3 * HALF), lambda i: (i, 0)), once(maps_up)],
        out_specs=[once(jax.ShapeDtypeStruct((rows, 3 * HALF), BF))] + [once(_f32(ROWS, WIDE))] * 2,
        scratch_shapes=[pltpu.VMEM((rows, WIDE), F32)],
        compiler_params=pltpu.CompilerParams(vmem_limit_bytes=48 * 2**20),
        cost_estimate=pl.CostEstimate(flops=2 * rows * D * 3 * HALF, bytes_accessed=22_000_000, transcendentals=0),
        name="project_qkv_back",
    )(me, *ins, qkv, qkv, *squares, *sums, w, maps_up)


class Gather:
    def __init__(self):
        core = lax.axis_index("c")
        x, z = lax.axis_index("x"), lax.axis_index("z")
        yl, yh = lax.axis_index("yl"), lax.axis_index("yh")
        y = 2 * yh + yl
        sign = 1 - 2 * core
        ys = [lax.rem(y - sign * k + 8, 4) for k in range(4)]
        zs = [lax.rem(z - sign * k + 8, 4) for k in range(4)]
        self.yh = yh
        self.me = jnp.stack([core, x, yl, yh] + zs).astype(jnp.int32)
        self.places = jnp.stack([jnp.stack([v // 2 for v in ys]), jnp.stack([v % 2 for v in ys]), self.me[:4]]).astype(jnp.int32)
        self.lanes = {"y0": Lane(), "y1": Lane(), "z": Lane(), "cross": Lane()}

    def across(self, own):
        return self.lanes["cross"].send(own, "cross")

    def over_xz(self, own, other, *before):
        other = after(other, *before)
        both = jnp.where(self.yh == 0, jnp.stack([own, other]), jnp.stack([other, own]))
        return lax.all_gather(both, ("x", "z")).reshape(4, 4, 2, *own.shape)

    def small(self, own):
        got = [own]
        for _ in range(3):
            got.append(self.lanes["z"].send(got[-1], "z"))
        return got

    def round(self, rings, *before):
        for n in range(2):
            value = after(rings[n][-1], *before) if before else rings[n][-1]
            rings[n].append(self.lanes["y%d" % n].send(value, "y"))


def turn(value, cosine, sine):
    return value * cosine + pltpu.roll(value, 64, 1) * sine


def _pack_body(me, q, k, v, squares, other, gains, cosine, sine, out):
    scales = lax.rsqrt((squares[...] + other[...]) / D + EPS)
    c, s = cosine[...], sine[...]
    out[0, :, 0:HD] = turn(q[...] * scales[:, 0:1] * gains[0:1], c, s).astype(BF)
    out[0, :, HD : 2 * HD] = turn(k[...] * scales[:, 1:2] * gains[1:2], c, s).astype(BF)
    out[0, :, 2 * HD :] = v[...].astype(BF)


def pack_heads(me, qkv, squares, other, gains, cosine, sine):
    rows = qkv.shape[0]
    whole = lambda shape: pl.BlockSpec(shape, lambda i, me: (0, 0))
    return pl.pallas_call(
        _pack_body,
        out_shape=jax.ShapeDtypeStruct((8, rows, 3 * HD), BF),
        grid_spec=pltpu.PrefetchScalarGridSpec(
            num_scalar_prefetch=1,
            grid=(8,),
            in_specs=[
            pl.BlockSpec((rows, HD), lambda i, me: (0, i)),
            pl.BlockSpec((rows, HD), lambda i, me: (0, 8 + i)),
            pl.BlockSpec((rows, HD), lambda i, me: (0, 16 + i)),
            whole((rows, 128)),
            whole((rows, 128)),
            pl.BlockSpec((4, HD), lambda i, me: (0, 2 * i + me[CORE])),
            whole((rows, HD)),
            whole((rows, HD)),
        ],
            out_specs=pl.BlockSpec((1, rows, 3 * HD), lambda i, me: (i, 0, 0)),
        ),
        name="pack_heads",
    )(me, qkv, qkv, qkv, squares, other, gains, cosine, sine)


def _unpack_body(me, d, q, k, gains, cosine, sine, wq, wk, dv, sums):
    c, s = cosine[...], -sine[...]
    i = pl.program_id(0)
    gq = turn(d[0, :, 0:HD].astype(F32), c, s) * gains[0:1]
    gk = turn(d[0, :, HD : 2 * HD].astype(F32), c, s) * gains[1:2]
    wq[...] = gq
    wk[...] = gk
    dv[...] = d[0, :, 2 * HD :]

    @pl.when(i == 0)
    def _():
        sums[...] = jnp.zeros_like(sums)

    lane = lax.broadcasted_iota(jnp.int32, sums.shape, 1)
    of_q = jnp.sum(gq * q[...], axis=1, keepdims=True)
    of_k = jnp.sum(gk * k[...], axis=1, keepdims=True)
    sums[...] += jnp.where(lane == 0, of_q, jnp.where(lane == 1, of_k, 0.0))


def unpack_heads(me, d, qkv, gains, cosine, sine):
    rows = qkv.shape[0]
    whole = lambda shape: pl.BlockSpec(shape, lambda i, me: (0, 0))
    column = pl.BlockSpec((rows, HD), lambda i, me: (0, i))
    return pl.pallas_call(
        _unpack_body,
        out_shape=[
            jax.ShapeDtypeStruct((rows, HALF), F32),
            jax.ShapeDtypeStruct((rows, HALF), F32),
            jax.ShapeDtypeStruct((rows, HALF), BF),
            jax.ShapeDtypeStruct((rows, HD), F32),
        ],
        grid_spec=pltpu.PrefetchScalarGridSpec(
            num_scalar_prefetch=1,
            grid=(8,),
            in_specs=[
            pl.BlockSpec((1, rows, 3 * HD), lambda i, me: (i, 0, 0)),
            pl.BlockSpec((rows, HD), lambda i, me: (0, i)),
            pl.BlockSpec((rows, HD), lambda i, me: (0, 8 + i)),
            pl.BlockSpec((4, HD), lambda i, me: (0, 2 * i + me[CORE])),
            whole((rows, HD)),
            whole((rows, HD)),
        ],
            out_specs=[column, column, column, whole((rows, HD))],
        ),
        name="unpack_heads",
    )(me, d, qkv, qkv, gains, cosine, sine)


TILE = 128
def hidden_pairs(t, bound):
    query = t * TILE + lax.broadcasted_iota(jnp.int32, (TILE, TILE), 0)
    key = t * TILE + lax.broadcasted_iota(jnp.int32, (TILE, TILE), 1)
    hidden = key > query
    if t * TILE >= PROMPT:
        hidden = hidden | ((query >= bound) & (key < bound))
    return hidden


def tile_scores(q, k, t, bound):
    n = (t + 1) * TILE
    s = lax.dot_general(q[t * TILE : n], k[:n], **NT) * SCALE
    last = jnp.where(hidden_pairs(t, bound), -1e30, s[:, n - TILE :])
    return last if t == 0 else jnp.concatenate([s[:, : n - TILE], last], axis=1)


def _attend_body(bounds, qkv, out, exact, total):
    bound = bounds[pl.program_id(0)]
    q = qkv[:, 0, :, 0:HD].reshape(TOTAL, HD)
    k = qkv[:, 0, :, HD : 2 * HD].reshape(TOTAL, HD)
    v = qkv[:, 0, :, 2 * HD :].reshape(TOTAL, HD)
    for t in range(TOTAL // TILE):
        n = (t + 1) * TILE
        s = tile_scores(q, k, t, bound)
        top = jnp.max(s, axis=1, keepdims=True)
        p = jnp.exp(s - top)
        denom = jnp.sum(p, axis=1, keepdims=True)
        o = jnp.dot(p.astype(BF), v[:n], preferred_element_type=F32) / denom
        exact[0, t * TILE : n] = o
        total[0, t * TILE : n] = top + jnp.log(denom)
    out[:, 0] = exact[0].reshape(8, ROWS, HD).astype(BF)


def attend(bounds, qkv):
    return pl.pallas_call(
        _attend_body,
        grid=(2,),
        out_shape=[
            jax.ShapeDtypeStruct((8, 2, ROWS, HD), BF),
            jax.ShapeDtypeStruct((2, TOTAL, HD), F32),
            jax.ShapeDtypeStruct((2, TOTAL, 1), F32),
        ],
        in_specs=[
            pl.BlockSpec(memory_space=pltpu.SMEM),
            pl.BlockSpec((8, 1, ROWS, 3 * HD), lambda g: (0, g, 0, 0)),
        ],
        out_specs=[
            pl.BlockSpec((8, 1, ROWS, HD), lambda g: (0, g, 0, 0)),
            pl.BlockSpec((1, TOTAL, HD), lambda g: (g, 0, 0)),
            pl.BlockSpec((1, TOTAL, 1), lambda g: (g, 0, 0)),
        ],
        compiler_params=pltpu.CompilerParams(vmem_limit_bytes=40 * 2**20),
        cost_estimate=pl.CostEstimate(flops=900_000_000, bytes_accessed=5_000_000, transcendentals=1_500_000),
        name="attend",
    )(bounds, qkv)


def _attend_back_body(bounds, qkv, grad, exact, total, out, dk, dv, dq):
    bound = bounds[pl.program_id(0)]
    q = qkv[:, 0, :, 0:HD].reshape(TOTAL, HD)
    k = qkv[:, 0, :, HD : 2 * HD].reshape(TOTAL, HD)
    v = qkv[:, 0, :, 2 * HD :].reshape(TOTAL, HD)
    g = grad[:, 0].reshape(TOTAL, HD)
    dk[...] = jnp.zeros_like(dk)
    dv[...] = jnp.zeros_like(dv)
    for t in range(TOTAL // TILE):
        n = (t + 1) * TILE
        here = slice(t * TILE, n)
        s = tile_scores(q, k, t, bound)
        p = jnp.exp(s - total[0, here])
        delta = jnp.sum(g[here].astype(F32) * exact[0, here], axis=1, keepdims=True)
        dp = lax.dot_general(g[here], v[:n], **NT)
        ds = (p * (dp - delta)).astype(BF)
        dq[here] = jnp.dot(ds, k[:n], preferred_element_type=F32) * SCALE
        dk[:n] += lax.dot_general(ds, q[here], **TN) * SCALE
        dv[:n] += lax.dot_general(p.astype(BF), g[here], **TN)
    out[:, 0, :, 0:HD] = dq[...].reshape(8, ROWS, HD).astype(BF)
    out[:, 0, :, HD : 2 * HD] = dk[...].reshape(8, ROWS, HD).astype(BF)
    out[:, 0, :, 2 * HD :] = dv[...].reshape(8, ROWS, HD).astype(BF)


def attend_back(bounds, qkv, grad, exact, total):
    return pl.pallas_call(
        _attend_back_body,
        grid=(2,),
        out_shape=jax.ShapeDtypeStruct((8, 2, ROWS, 3 * HD), BF),
        in_specs=[
            pl.BlockSpec(memory_space=pltpu.SMEM),
            pl.BlockSpec((8, 1, ROWS, 3 * HD), lambda g: (0, g, 0, 0)),
            pl.BlockSpec((8, 1, ROWS, HD), lambda g: (0, g, 0, 0)),
            pl.BlockSpec((1, TOTAL, HD), lambda g: (g, 0, 0)),
            pl.BlockSpec((1, TOTAL, 1), lambda g: (g, 0, 0)),
        ],
        out_specs=pl.BlockSpec((8, 1, ROWS, 3 * HD), lambda g: (0, g, 0, 0)),
        scratch_shapes=[pltpu.VMEM((TOTAL, HD), F32)] * 3,
        compiler_params=pltpu.CompilerParams(vmem_limit_bytes=40 * 2**20),
        cost_estimate=pl.CostEstimate(flops=2_300_000_000, bytes_accessed=8_000_000, transcendentals=1_500_000),
        name="attend_back",
    )(bounds, qkv, grad, exact, total)


def dot(a, b):
    return jnp.dot(a, b, preferred_element_type=F32)


def dot_nt(a, b):
    return lax.dot_general(a, b, **NT)


def dot_tn(a, b):
    return lax.dot_general(a, b, **TN)


def normalize_back(field, inverse, gain, grad):
    weighted = grad * gain
    return inverse * weighted - field * inverse**3 * jnp.mean(weighted * field, axis=-1, keepdims=True)


def choose_adapters(slots, down_in, down_ff, up_model, up_hidden):
    def body(slots, down_in, down_ff, up_model, up_hidden, qkv_down, gu_down, out_down, ff_down, qkv_up, out_up, ff_up, gu_up):
        core = slots[2]
        qkv_down[...] = down_in[0, :3].reshape(3 * RANK, D)
        gu_down[...] = down_in[0, 4:].reshape(2 * RANK, D)
        out_up[...] = up_model[0, 3]
        ff_up[...] = up_model[0, 4]
        qkv_up[...] = jnp.zeros_like(qkv_up)
        gu_up[...] = jnp.zeros_like(gu_up)
        for h in range(8):
            head = pl.ds(pl.multiple_of((2 * h + core) * HD, HD), HD)
            out_down[:, HD * h : HD * (h + 1)] = down_in[0, 3, :, head]
            for n in range(3):
                here = slice(n * HALF + HD * h, n * HALF + HD * (h + 1))
                qkv_up[n * RANK : (n + 1) * RANK, here] = up_model[0, n, :, head]
        for m in range(FF // 128):
            start = (2 * (m // 4) + core) * 512 + (m % 4) * 128
            units = pl.ds(pl.multiple_of(start, 128), 128)
            ff_down[:, 128 * m : 128 * (m + 1)] = down_ff[0, :, units]
            for n in range(2):
                here = slice(256 * m + 128 * n, 256 * m + 128 * (n + 1))
                gu_up[n * RANK : (n + 1) * RANK, here] = up_hidden[0, n, :, units]

    def chosen(shape):
        return pl.BlockSpec((1,) + shape[1:], lambda g, slots: (slots[g],) + (0,) * (len(shape) - 1))

    shapes = [(48, D), (32, D), (16, HALF), (16, FF), (48, 3 * HALF), (16, D), (16, D), (32, 2 * FF)]
    maps = [down_in, down_ff, up_model, up_hidden]
    return pl.pallas_call(
        body,
        out_shape=[bf(2 * r, c) for r, c in shapes],
        grid_spec=pltpu.PrefetchScalarGridSpec(
            num_scalar_prefetch=1,
            grid=(2,),
            in_specs=[chosen(m.shape) for m in maps],
            out_specs=[pl.BlockSpec(shape, lambda g, slots: (g, 0)) for shape in shapes],
        ),
        cost_estimate=pl.CostEstimate(flops=0, bytes_accessed=7_000_000, transcendentals=0),
        name="choose_adapters",
    )(slots, *maps)


def rank_gradients(lows, acts, core, name, plan, width):
    count = len(lows)

    def body(core, *refs):
        lows, acts, out = refs[:count], refs[count:-1], refs[-1]
        at = 0
        for low, act, columns, factor, starts in plan:
            picked = [lows[low][:, c : c + RANK] for c in columns]
            picked = jnp.concatenate(picked, axis=1)
            if columns[0] == columns[1]:
                picked = jnp.where(_in_group(2 * ROWS, 2 * RANK, RANK), picked, jnp.zeros_like(picked))
            if factor != 1:
                picked = picked * factor
            for start in starts(core[0]):
                right = acts[act][:, start if isinstance(start, slice) else pl.ds(pl.multiple_of(start, 128), 128)]
                n = right.shape[1]
                grad = lax.dot_general(picked, right, **TN).astype(BF)
                for b in range(n // 128):
                    block, slot = divmod(at, width // 128)
                    out[block, :, 128 * slot : 128 * (slot + 1)] = grad[:, 128 * b : 128 * (b + 1)]
                    at += 1

    return _plain(body, name, [bf(8, 2 * RANK, width)], list(lows) + list(acts), [core])[0]


def adapter_outputs(core, halves, others, count, shapes, name, write):
    def body(core, *refs):
        own, other, outs = refs[:count], refs[count : 2 * count], refs[2 * count :]

        def place(start):
            return pl.ds(pl.multiple_of(start, 128), 128)

        for side, group in ((core[0], own), (1 - core[0], other)):

            def piece(n, at):
                block, slot = divmod(at, group[n].shape[3] // 128)
                return group[n][block, 0, :, 128 * slot : 128 * (slot + 1)].astype(F32)

            write(side, piece, place, outs)

    arrays = halves + others
    size = sum(v.size * 2 for v in arrays)
    return pl.pallas_call(
        body,
        grid=(8,),
        out_shape=[jax.ShapeDtypeStruct(s, F32) for s in shapes],
        in_specs=[_smem()] + [pl.BlockSpec((v.shape[0], 1) + v.shape[2:], lambda i: (0, i, 0, 0)) for v in arrays],
        out_specs=[pl.BlockSpec((1,) + s[1:], lambda i, n=len(s): (i,) + (0,) * (n - 1)) for s in shapes],
        compiler_params=pltpu.CompilerParams(vmem_limit_bytes=40 * 2**20),
        cost_estimate=pl.CostEstimate(flops=0, bytes_accessed=size, transcendentals=0),
        name=name,
    )(core, *arrays)


def write_early(side, piece, place, outs):
    up_hidden, down_ff = outs
    for m in range(FF // 128):
        units = place((2 * (m // 4) + side) * 512 + (m % 4) * 128)
        up_hidden[0, 0, :, units] = piece(0, m)
        up_hidden[0, 1, :, units] = piece(0, 32 + m)
        down_ff[0, :, units] = piece(0, 64 + m)


def write_late(side, piece, place, outs):
    down_in, up_model = outs
    for m in range(8):
        whole, head = place(side * HALF + 128 * m), place((2 * m + side) * HD)
        for n in range(3):
            down_in[0, n, :, whole] = piece(0, 8 * n + m)
            up_model[0, n, :, head] = piece(0, 24 + 8 * n + m)
        down_in[0, 4, :, whole] = piece(0, 48 + m)
        down_in[0, 5, :, whole] = piece(0, 56 + m)
        down_in[0, 3, :, head] = piece(0, 64 + m)
        up_model[0, 3, :, whole] = piece(0, 72 + m)
        up_model[0, 4, :, whole] = piece(1, EARLY // 128 - 8 + m)


def on_device(
    tokens,
    cotangent,
    query_matrix,
    key_matrix,
    value_matrix,
    output_matrix,
    gate_matrix,
    upward_matrix,
    down_matrix,
    gains,
    adapter_down_inputs,
    adapter_down_feedforward,
    adapter_up_model_maps,
    adapter_up_hidden_maps,
    group_adapter_index,
    continuation_lengths,
):
    core = lax.axis_index("c")
    first = core == 0
    ctx = lax.axis_index("yl") * 4 + lax.axis_index("x")
    tokens, cotangent = tokens[0], cotangent[0]

    def both(own, other):
        return jnp.where(first, jnp.stack([own, other]), jnp.stack([other, own]))

    def rows_of_both(own):
        return both(own, swap(own)).reshape(2 * own.shape[0], own.shape[1])

    plan = Gather()
    me, places = plan.me, plan.places
    keep_a, give_a = split_a(me, query_matrix, key_matrix, value_matrix)
    keep_g, give_g = split_g(me, gate_matrix, upward_matrix)
    got_a, got_g = swap(give_a), swap(give_g)
    xs_a, ys_a = parts_a(me, keep_a, got_a, output_matrix)
    xs_m, ys_g, ys_d = parts_m(me, keep_g, got_g, down_matrix)
    crossed = plan.across(xs_a)
    small_a = plan.small(ys_a)
    small_g = plan.small(ys_g)
    xs_a = plan.over_xz(xs_a, crossed, small_a[1])
    crossed = plan.across(after(xs_m, small_a[2]))
    y_a = spread(me, small_a, [(0, HALF, 1)], "spread_a")
    rings_a = [[v] for v in y_a]
    for _ in range(3):
        plan.round(rings_a)
    xs_m = plan.over_xz(xs_m, crossed, rings_a[0][1], rings_a[1][1])
    small_d = plan.small(ys_d)
    y_g = spread(me, small_g, [(0, FF - CUT_G // 2, 1)], "spread_g")
    rings_g = [[v] for v in y_g]
    plan.round(rings_g)
    w_qkv, w_out = assemble(Chunks(256, CUT_A, 4 * HALF, places, xs_a, 0, rings_a))

    facts = jnp.concatenate([group_adapter_index[0], continuation_lengths[0]]).astype(F32)
    facts = jnp.broadcast_to(jnp.pad(facts, (0, 125))[None], (8, 128))
    pair_facts = both(facts, swap(facts))[:, 0, :2].astype(jnp.int32)
    slots = pair_facts[:, 0]
    bounds = PROMPT + pair_facts[:, 1]
    (qkv_down, gu_down, out_down, ff_down, qkv_up, out_up2, ff_up2, gu_up) = choose_adapters(
        jnp.concatenate([slots, me[:1]]),
        adapter_down_inputs,
        adapter_down_feedforward,
        adapter_up_model_maps,
        adapter_up_hidden_maps,
    )

    group_row = lax.broadcasted_iota(jnp.int32, (2 * ROWS, 1), 0) // ROWS

    def own_columns(low, count):
        group_column = lax.broadcasted_iota(jnp.int32, (1, 2 * count), 1) // count
        return jnp.where(group_row == group_column, low, jnp.zeros_like(low))

    shard = ("z", "yh")

    def spread_over(value, axes):
        return lax.all_to_all(jnp.broadcast_to(value[None], (8,) + value.shape), axes, 0, 0, tiled=True)

    place = ctx * ROWS + lax.broadcasted_iota(jnp.int32, (2, ROWS), 1)
    position = jnp.where(place >= bounds[:, None], PROMPT + place - bounds[:, None], place)
    freq = BASE ** (-(jnp.arange(HD // 2, dtype=F32) * 2.0 / HD))
    angle = position.reshape(2 * ROWS, 1).astype(F32) * freq[None]
    cosine = jnp.concatenate([jnp.cos(angle)] * 2, axis=1)
    sine = jnp.concatenate([-jnp.sin(angle), jnp.sin(angle)], axis=1)

    def whole(n):
        return lambda core: [slice(0, n)]

    def half(core):
        return [core * HALF + 128 * m for m in range(8)]

    def turns(n):
        return lambda core: [slice(256 * m + 128 * n, 256 * m + 128 * (n + 1)) for m in range(FF // 128)]

    def third(n):
        return lambda core: [slice(n * HALF, (n + 1) * HALF)]

    x2 = rows_of_both(tokens)
    qkv_low = own_columns((2.0 * dot_nt(x2, qkv_down).astype(BF)).astype(BF), 3 * RANK)
    qkv, squares = project_qkv(x2, w_qkv, qkv_low, qkv_up)
    squares = (squares, swap(squares))
    qkv = after(qkv, small_d[1])
    packed = pack_heads(me, qkv, *squares, gains, cosine, sine)
    heads = lax.all_to_all(packed, CTX, 0, 0, tiled=True).reshape(8, 2, ROWS, 3 * HD)
    heads = after(heads, rings_g[0][-1], rings_g[1][-1], small_d[2])
    plan.round(rings_g, qkv)
    out_heads, exact, log_total = attend(bounds, heads)
    attended = lax.all_to_all(out_heads, CTX, 0, 0, tiled=True).reshape(8, 2 * ROWS, HD)
    y_d = spread(me, small_d, [(0, HALF - CUT_D // 2, 2)], "spread_d")
    attended = after(attended, rings_g[0][-1], rings_g[1][-1], y_d[0])
    keep, give, attended = project_out(me, attended, w_out, out_down)
    attn_pre, hidden, sent = combine_attention(me, keep, swap(give), tokens, gains, out_up2)

    plan.round(rings_g, out_heads)
    wg = Chunks(256, CUT_G, 2 * FF, places, xs_m, 0, rings_g)
    rings_d = [[v] for v in y_d]
    plan.round(rings_d)
    gu, mixed, h2, gu_low = gate_and_up(wg, sent, swap(sent), gu_down, gu_up)
    plan.round(rings_d)
    plan.round(rings_d)
    wd = Chunks(512, CUT_D, D, places, xs_m, CUT_G // 4, rings_d)
    keep, give = down(wd, mixed, ff_down)
    output, sent = combine_output(me, keep, swap(give), hidden, cotangent, gains, ff_up2)

    d_gu, d_mlp, ff_grad_low = down_back(wd, sent, swap(sent), ff_up2, ff_down, gu)
    early = rank_gradients(
        [gu_low, ff_grad_low, d_mlp],
        [d_gu, mixed, d_mlp],
        me,
        "early_gradients",
        [
            (0, 0, (0, 2 * RANK), 1, turns(0)),
            (0, 0, (RANK, 3 * RANK), 1, turns(1)),
            (1, 1, (0, RANK), 1, whole(FF)),
            (2, 2, (D, D), 2, half),
        ],
        EARLY,
    )
    d_gu, early = lax.optimization_barrier((d_gu, early))
    early = lax.all_to_all(early, CTX, 0, 0, tiled=True)
    keep, give = gate_and_up_back(wg, d_gu, gu_up)
    give, early = lax.optimization_barrier((give, early))
    d_hidden, sent = combine_hidden(me, keep, swap(give), cotangent, attn_pre, gains, gu_down)

    d_out_heads, d_attn, out_grad_low = project_out_back(me, sent, swap(sent), w_out, out_up2, out_down)
    d_out_heads = lax.all_to_all(d_out_heads, CTX, 0, 0, tiled=True).reshape(8, 2, ROWS, HD)
    own = jnp.sum(early.astype(F32), axis=0).astype(BF)
    own_slot = jnp.repeat(slots, RANK)[:, None] == lax.broadcasted_iota(jnp.int32, (1, 128), 1)
    own = jnp.concatenate([own, own_slot.astype(BF)], axis=1)
    d_out_heads, own = lax.optimization_barrier((d_out_heads, own))
    groups = spread_over(own, shard).reshape(16, RANK, EARLY + 128)
    d_heads = attend_back(bounds, heads, d_out_heads, exact, log_total)
    d_heads, groups = lax.optimization_barrier((d_heads, groups))
    picker = groups[:, 0, EARLY : EARLY + 8]
    d_heads = lax.all_to_all(d_heads, CTX, 0, 0, tiled=True).reshape(8, 2 * ROWS, 3 * HD)
    w_q, w_k, d_v, sums = unpack_heads(me, d_heads, qkv, gains, cosine, sine)

    def by_slot(groups):
        flat = groups.reshape(16, -1)
        return lax.dot_general(picker, flat, **TN).astype(BF).reshape(8 * RANK, -1)

    early, w_q = lax.optimization_barrier((by_slot(groups[:, :, :EARLY]), w_q))
    early = lax.all_gather(early, CTX)
    d_qkv, keep, give = project_qkv_back(me, (w_q, w_k), d_v, qkv, squares, (sums, swap(sums)), w_qkv, qkv_up)
    grad_tokens, low = combine_tokens(me, keep, swap(give), d_hidden, qkv_down)
    low = both(low, swap(low)).reshape(2 * ROWS, 128)

    late = rank_gradients(
        [low, qkv_low, d_attn, out_grad_low, h2],
        [x2, d_qkv, h2, attended, d_attn],
        me,
        "late_gradients",
        [(0, 0, (n * RANK, n * RANK), 1, half) for n in range(3)]
        + [(1, 1, (n * RANK, (3 + n) * RANK), 1, third(n)) for n in range(3)]
        + [
            (2, 2, (D, D), 1, half),
            (2, 2, (D + RANK, D + RANK), 1, half),
            (3, 3, (0, RANK), 1, whole(HALF)),
            (4, 4, (D, D), 2, half),
        ],
        LATE,
    )
    late = lax.all_to_all(late, CTX, 0, 0, tiled=True)
    late = jnp.sum(late.astype(F32), axis=0).astype(BF)
    late = spread_over(late, shard)
    early, late = lax.optimization_barrier((early, late))
    late = spread_over(by_slot(late.reshape(16, RANK, LATE)), CTX)
    shape = (8, 8, RANK, -1)
    early = early.reshape(shape)
    early_other = swap(early)
    grad_up_hidden, grad_down_ff = adapter_outputs(
        me,
        [early],
        [early_other],
        1,
        [(8, 2, RANK, 2 * FF), (8, RANK, 2 * FF)],
        "early_outputs",
        write_early,
    )
    late, grad_up_hidden = lax.optimization_barrier((late, grad_up_hidden))
    late_other = swap(late)
    late, late_other = late.reshape(shape), late_other.reshape(shape)
    grad_down_in, grad_up_model = adapter_outputs(
        me,
        [late, early[7:]],
        [late_other, early_other[7:]],
        2,
        [(8, 6, RANK, D), (8, 5, RANK, D)],
        "late_outputs",
        write_late,
    )
    return (output[None], grad_tokens[None], grad_down_in, grad_down_ff, grad_up_model, grad_up_hidden)


def solution(mesh):
    fine = Mesh(mesh.devices.reshape(2, 4, 4, 2, 2), ALL)
    shard = ("z", "yh", "c")
    rows = P(shard, None)
    per_token = P(shard, CTX, None)
    return jax.shard_map(
        on_device,
        mesh=fine,
        in_specs=(per_token, per_token) + (rows,) * 7 + (P(),) * 5 + (rows, rows),
        out_specs=(per_token, per_token, P(), P(), P(), P()),
        check_vma=False,
    )
```

```python
import jax
import jax.numpy as jnp
from jax import lax
from jax.experimental import pallas as pl
from jax.experimental.pallas import tpu as pltpu
from jax.sharding import Mesh, PartitionSpec as P

HD = 128
PROMPT = 1024
ROWS = 144
TOTAL = 1152
D = 2048
HALF = 1024
FF = 4096
RANK = 16
SCALE = HD**-0.5
EPS = 1e-06
BASE = 500000.0
ALL = ("yl", "x", "z", "yh", "c")
CTX = ("yl", "x")
BF = jnp.bfloat16
F32 = jnp.float32
CUT_A, CUT_G = 2048, 4096
EARLY, MIDDLE, LATE = 1664, 512, 768


NT = dict(dimension_numbers=(((1,), (1,)), ((), ())), preferred_element_type=F32)
TN = dict(dimension_numbers=(((0,), (0,)), ((), ())), preferred_element_type=F32)


CORE, X, YL, YH, Z0 = 0, 1, 2, 3, 4


def _place(yl, x, z, yh, c):
    return (((yl * 4 + x) * 4 + z) * 2 + yh) * 2 + c


def _permutation(move):
    pairs = []
    for yl in range(2):
        for x in range(4):
            for z in range(4):
                for yh in range(2):
                    for c in range(2):
                        nx, ny, nz, nc = move(x, 2 * yh + yl, z, c)
                        pairs.append(
                            (_place(yl, x, z, yh, c), _place(ny % 2, nx % 4, nz % 4, (ny % 4) // 2, nc))
                        )
    return pairs


STEPS = {
    "y": _permutation(lambda x, y, z, c: (x, (y + 1 - 2 * c) % 4, z, c)),
    "z": _permutation(lambda x, y, z, c: (x, y, z + 1 - 2 * c, c)),
    "cross": _permutation(lambda x, y, z, c: (x, 3 - y, z, c)),
    "core": _permutation(lambda x, y, z, c: (x, y, z, 1 - c)),
}


def swap(value):
    return lax.ppermute(value, ALL, STEPS["core"])


class Lane:
    def __init__(self):
        self.last = None

    def send(self, value, how):
        if self.last is not None:
            value, _ = lax.optimization_barrier((value, self.last))
        self.last = lax.ppermute(value, ALL, STEPS[how])
        return self.last


def after(value, *others):
    return lax.optimization_barrier((value, *others))[0]


def _smem():
    return pl.BlockSpec(memory_space=pltpu.SMEM)


def _vmem():
    return pl.BlockSpec(memory_space=pltpu.VMEM)


def _plain(body, name, outs, ins, scalars, scratch=(), limit=48):
    size = sum(v.size * v.dtype.itemsize for v in list(ins) + list(outs))
    return pl.pallas_call(
        body,
        out_shape=outs,
        in_specs=[_smem()] * len(scalars) + [_vmem()] * len(ins),
        out_specs=[_vmem()] * len(outs),
        scratch_shapes=list(scratch),
        compiler_params=pltpu.CompilerParams(vmem_limit_bytes=limit * 2**20),
        cost_estimate=pl.CostEstimate(flops=0, bytes_accessed=size, transcendentals=0),
        name=name,
    )(*scalars, *ins)


def bf(*shape):
    return jax.ShapeDtypeStruct(shape, BF)


def split_a(core, q, k, v):
    def body(core, q, k, v, keep, give):
        for n, w in enumerate((q, k, v)):
            for h in range(8):
                here = slice(n * HALF + HD * h, n * HALF + HD * (h + 1))
                keep[:, here] = w[:, pl.ds(pl.multiple_of((2 * h + core[0]) * HD, HD), HD)]
                give[:, here] = w[:, pl.ds(pl.multiple_of((2 * h + 1 - core[0]) * HD, HD), HD)]

    return _plain(body, "split_a", [bf(HD, 3 * HALF)] * 2, [q, k, v], [core])


def split_g(core, gate, upward):
    def body(core, gate, upward, keep, give):
        for m in range(FF // 128):
            for n, w in enumerate((gate, upward)):
                here = slice(256 * m + 128 * n, 256 * m + 128 * (n + 1))
                for side, out in ((core[0], keep), (1 - core[0], give)):
                    start = (2 * (m // 4) + side) * 512 + (m % 4) * 128
                    out[:, here] = w[:, pl.ds(pl.multiple_of(start, 128), 128)]

    return _plain(body, "split_g", [bf(HD, 2 * FF)] * 2, [gate, upward], [core])


def parts_a(me, keep, got, out):
    quarter = CUT_A // 4

    def body(me, keep, got, out, xs, ys):
        for side, w in ((me[CORE], keep), (1 - me[CORE], got)):
            rows = pl.ds(pl.multiple_of(side * HD, HD), HD)
            xs[rows, :] = w[:, pl.ds(pl.multiple_of(me[X] * quarter, 128), quarter)]

            @pl.when(me[YL] == 0)
            def _():
                ys[rows, :] = w[:, 2 * HALF :]

        @pl.when(me[YL] == 1)
        def _():
            ys[:HD, :] = out[:, :HALF]
            ys[HD:, :] = out[:, HALF:]

    return _plain(body, "parts_a", [bf(256, quarter), bf(256, HALF)], [keep, got, out], [me])


def parts_m(me, keep, got, down):
    gx, dx, gy = CUT_G // 4, D // 4, FF - CUT_G // 2

    def body(me, keep, got, down, xs, ys):
        for side, w in ((me[CORE], keep), (1 - me[CORE], got)):
            rows = pl.ds(pl.multiple_of(side * HD, HD), HD)
            xs[rows, :gx] = w[:, pl.ds(pl.multiple_of(me[X] * gx, 128), gx)]
            ys[rows, :] = w[:, pl.ds(pl.multiple_of(CUT_G + me[YL] * gy, 128), gy)]
        for n in range(2):
            rows = slice(256 * n, 256 * (n + 1))
            xs[:, gx + n * dx : gx + (n + 1) * dx] = down[rows, pl.ds(pl.multiple_of(me[X] * dx, 128), dx)]

    return _plain(body, "parts_m", [bf(256, gx + 2 * dx), bf(256, gy)], [keep, got, down], [me])


def spread(me, got, pieces, name):
    def body(me, *refs):
        chunks, outs = refs[:4], refs[4:]
        for k in range(4):
            z = me[Z0 + k]
            for p, (column, width, folds) in enumerate(pieces):
                for half in range(2):

                    @pl.when(z // 2 == half)
                    def _():
                        for n in range(folds):
                            at = pl.multiple_of(((z - 2 * half) * folds + n) * 256, 256)
                            start = column + n * width
                            outs[2 * p + half][pl.ds(at, 256), :] = chunks[k][:, start : start + width]

    outs = [bf(2 * folds * 256, width) for _, width, folds in pieces for _ in range(2)]
    return _plain(body, name, outs, list(got), [me])


class Chunks:
    def __init__(self, rows, cut, width, places, xs, column, y):
        self.rows, self.cx, self.cy = rows, cut, width - cut
        self.depth = 8 * rows
        self.places = places
        self.column = column
        self.arrays = [xs] + (y[0] + y[1] if y else [])


def _y_rows(places, rows, half, j, k):
    return pl.multiple_of((2 * half + j) * 2 * rows + places[0, k] * rows, rows)


def _panel_copies(rows, width, column, xs, whole, panels):
    copies = []
    for at, k in enumerate(panels):
        for z in range(4):
            for yh in range(2):
                for n in range(rows // 256):
                    target = whole.at[pl.ds((2 * z + yh) * rows + 256 * n, 256), pl.ds(at * width, width)]
                    copies.append((xs.at[k, z, yh, :, pl.ds(column + n * width, width)], target))
    return copies


def _y_copies(places, y, whole, k, column, width):
    copies = []
    for half in range(2):
        for j in range(2):
            row = _y_rows(places, 256, half, j, k)
            copies.append((y[4 * half + k].at[pl.ds(j * 256, 256)], whole.at[pl.ds(row, 256), pl.ds(column, width)]))
    return copies


def assemble(w):
    anywhere = pl.BlockSpec(memory_space=pl.ANY)

    def body(places, *refs):
        out, out_matrix, sems = refs[9], refs[10], refs[11]
        panels = _panel_copies(256, w.cx // 4, 0, refs[0], out, range(4))
        plain = [pltpu.make_async_copy(a, b, sems.at[n]) for n, (a, b) in enumerate(panels)]
        for copy in plain:
            copy.start()

        def move(started):
            at = len(plain)
            for k in range(4):
                for half in range(2):
                    for j in range(2):
                        source = refs[1 + 4 * half + k].at[pl.ds(j * 256, 256)]
                        block = 2 * (2 * half + j) + places[0, k]

                        @pl.when(places[1, k] == 0)
                        def _():
                            row = pl.multiple_of(block * 256, 256)
                            target = out.at[pl.ds(row, 256), pl.ds(2 * HALF, HALF)]
                            copy = pltpu.make_async_copy(source, target, sems.at[at])
                            copy.wait() if started else copy.start()

                        @pl.when(places[1, k] == 1)
                        def _():
                            for n in range(2):
                                row = pl.multiple_of(block * HD, HD)
                                target = out_matrix.at[pl.ds(row, HD), pl.ds(n * HALF, HALF)]
                                copy = pltpu.make_async_copy(source.at[pl.ds(n * HD, HD)], target, sems.at[at + n])
                                copy.wait() if started else copy.start()

                        at += 2

        move(False)
        for copy in plain:
            copy.wait()
        move(True)

    return pl.pallas_call(
        body,
        out_shape=[bf(D, 3 * HALF), bf(HALF, D)],
        in_specs=[_smem()] + [anywhere] * 9,
        out_specs=[_vmem()] * 2,
        scratch_shapes=[pltpu.SemaphoreType.DMA((64,))],
        compiler_params=pltpu.CompilerParams(vmem_limit_bytes=48 * 2**20),
        cost_estimate=pl.CostEstimate(flops=0, bytes_accessed=64 * 2**20, transcendentals=0),
        name="assemble",
    )(w.places, *w.arrays)


WIDE = D + 128


def _f32(*shape):
    return jax.ShapeDtypeStruct(shape, F32)


def _pair_up(core, own, other, pair):
    pair[pl.ds(pl.multiple_of(core * ROWS, ROWS), ROWS), :] = own[...]
    pair[pl.ds(pl.multiple_of((1 - core) * ROWS, ROWS), ROWS), :] = other[...]


def _split(core, sums, keep, give):
    keep[...] = sums[pl.ds(pl.multiple_of(core * ROWS, ROWS), ROWS), :]
    give[...] = sums[pl.ds(pl.multiple_of((1 - core) * ROWS, ROWS), ROWS), :].astype(BF)


def _in_group(rows, columns, count):
    row = lax.broadcasted_iota(jnp.int32, (rows, columns), 0) >= ROWS
    column = lax.broadcasted_iota(jnp.int32, (rows, columns), 1) >= count
    return row == column


def _own_group(low, count):
    row = lax.broadcasted_iota(jnp.int32, (low.shape[0], count), 0)
    return jnp.where(row >= ROWS, low[:, count:], low[:, :count])


def _put_low(sums, low):
    count = low.shape[1]
    sums[:, D:] = jnp.zeros((sums.shape[0], WIDE - D), F32)
    sums[:, D : D + count] = low


SLOT = D
SLOTS = 4


class Stream:
    def __init__(self, w):
        self.w = w

    def gate_up(self, places, refs, n):
        xs, y, quarter = refs[0], refs[1:9], CUT_G // 4
        if n < 2:
            return n * SLOT, lambda slot: _panel_copies(256, quarter, 0, xs, slot, range(2 * n, 2 * n + 2))
        column = pl.multiple_of(CUT_G + places[1, n - 2] * SLOT, SLOT)
        return column, lambda slot: [
            copy for k in (n - 2, n) for copy in _y_copies(places, y, slot, k, 0, SLOT)
        ]

    def down(self, refs, n):
        xs, quarter = refs[0], D // 4

        def copies(slot):
            made = []
            for k in range(4):
                for block in range(4 * n, 4 * n + 4):
                    for m in range(2):
                        source = xs.at[k, block // 2, block % 2, :, pl.ds(CUT_G // 4 + m * quarter, quarter)]
                        row = (block - 4 * n) * 512 + 256 * m
                        made.append((source, slot.at[pl.ds(row, 256), pl.ds(k * quarter, quarter)]))
            return made

        return n * SLOT, copies

    def run(self, pieces, slots, sems, first, use):
        copies = []
        for n, (_, made) in enumerate(pieces):
            slot = n % SLOTS
            pairs = made(slots.at[slot])
            copies.append([pltpu.make_async_copy(a, b, sems.at[slot, m]) for m, (a, b) in enumerate(pairs)])

        def begin(n):
            if n < len(copies):
                for copy in copies[n]:
                    copy.start()

        for n in range(SLOTS - 1):
            begin(n)
        first()
        for n, (at, _) in enumerate(pieces):
            for copy in copies[n]:
                copy.wait()
            use(n, at, slots.at[n % SLOTS])
            begin(n + SLOTS - 1)

    def call(self, body, name, ins, outs, scratch=()):
        w = self.w
        anywhere = pl.BlockSpec(memory_space=pl.ANY)
        size = 6 * D * FF + sum(v.size * v.dtype.itemsize for v in ins)
        return pl.pallas_call(
            body,
            out_shape=outs,
            in_specs=[_smem()] + [anywhere] * 9 + [_vmem()] * len(ins),
            out_specs=[_vmem()] * len(outs),
            scratch_shapes=[pltpu.VMEM((SLOTS, SLOT, SLOT), BF), pltpu.SemaphoreType.DMA((SLOTS, 32)), *scratch],
            compiler_params=pltpu.CompilerParams(vmem_limit_bytes=60 * 2**20),
            cost_estimate=pl.CostEstimate(flops=4 * ROWS * D * 3 * FF, bytes_accessed=size, transcendentals=0),
            name=name,
        )(w.places, *w.arrays, *ins)


def feed_forward(w, own, other, maps_down, maps_up, ff_down):
    rows = 2 * ROWS
    stream = Stream(w)

    def body(places, *refs):
        weights, (own_ref, other_ref, down_ref, up_ref, ff_ref) = refs[:9], refs[9:14]
        gu, mixed, pair, low_ref, keep, give, slots, sems, sums = refs[14:]

        def first():
            _pair_up(places[2, 0], own_ref, other_ref, pair)
            low = 2.0 * lax.dot_general(pair[:, :D], down_ref[...], **NT).astype(BF).astype(F32)
            low_ref[...] = jnp.where(_in_group(rows, 4 * RANK, 2 * RANK), low, 0.0).astype(BF)

        def use(n, at, slot):
            tile = SLOT // 2
            if n < 4:
                for t in range(2):
                    column = at + t * tile
                    unit = column // 2
                    if not isinstance(at, int):
                        column, unit = pl.multiple_of(column, tile), pl.multiple_of(unit, tile // 2)
                    total = jnp.dot(pair[:, :D], slot[:, t * tile : (t + 1) * tile], preferred_element_type=F32)
                    total = total + jnp.dot(low_ref[...], up_ref[:, pl.ds(column, tile)], preferred_element_type=F32)
                    gu[:, pl.ds(column, tile)] = total.astype(BF)
                    for m in range(tile // 256):
                        g, u = total[:, 256 * m : 256 * m + 128], total[:, 256 * m + 128 : 256 * m + 256]
                        mixed[:, pl.ds(unit + 128 * m, 128)] = (g * jax.nn.sigmoid(g) * u).astype(BF)
                return
            left = mixed[:, at : at + SLOT]
            for t in range(2):
                here = slice(t * tile, (t + 1) * tile)
                part = jnp.dot(left, slot[:, here], preferred_element_type=F32)
                if n == 4:
                    sums[:, here] = part
                else:
                    sums[:, here] += part

        pieces = [stream.gate_up(places, weights, n) for n in range(4)] + [stream.down(weights, n) for n in range(2)]
        stream.run(pieces, slots, sems, first, use)
        _put_low(sums, _own_group(lax.dot_general(mixed[...], ff_ref[...], **NT), RANK))
        _split(places[2, 0], sums, keep, give)

    outs = [bf(rows, 2 * FF), bf(rows, FF), bf(rows, WIDE), bf(rows, 4 * RANK), _f32(ROWS, WIDE), bf(ROWS, WIDE)]
    ins = [own, other, maps_down, maps_up, ff_down]
    return stream.call(body, "feed_forward", ins, outs, [pltpu.VMEM((rows, WIDE), F32)])


def feed_forward_back(w, own, other, ff_up, ff_down, gu, maps_up):
    rows = 2 * ROWS
    stream = Stream(w)

    def body(places, *refs):
        weights, (own_ref, other_ref, ff_up_ref, ff_down_ref, gu_ref, up_ref) = refs[:9], refs[9:15]
        out, pair, low_ref, keep, give, slots, sems, sums, lows = refs[15:]

        def first():
            _pair_up(places[2, 0], own_ref, other_ref, pair)
            low = 2.0 * lax.dot_general(pair[:, :D], ff_up_ref[...], **NT)
            low_ref[...] = jnp.where(_in_group(rows, 2 * RANK, RANK), low, 0.0).astype(BF)

        def use(n, at, slot):
            tile = SLOT // 2
            if n < 2:
                for t in range(2):
                    units = slice(at + t * tile, at + (t + 1) * tile)
                    d_mixed = lax.dot_general(pair[:, :D], slot[t * tile : (t + 1) * tile, :], **NT)
                    d_mixed = d_mixed + jnp.dot(low_ref[...], ff_down_ref[:, units], preferred_element_type=F32)
                    for m in range(tile // 128):
                        column = 2 * (at + t * tile) + 256 * m
                        g = gu_ref[:, column : column + 128].astype(F32)
                        u = gu_ref[:, column + 128 : column + 256].astype(F32)
                        d = d_mixed[:, 128 * m : 128 * (m + 1)]
                        s = jax.nn.sigmoid(g)
                        out[:, column : column + 128] = (d * u * s * (1.0 + g * (1.0 - s))).astype(BF)
                        out[:, column + 128 : column + 256] = (d * g * s).astype(BF)
                return
            left = out[:, pl.ds(at, SLOT)]
            low = lax.dot_general(left, up_ref[:, pl.ds(at, SLOT)], **NT)
            for t in range(2):
                here = slice(t * tile, (t + 1) * tile)
                part = lax.dot_general(left, slot[here, :], **NT)
                if n == 2:
                    sums[:, here] = part
                else:
                    sums[:, here] += part
            if n == 2:
                lows[...] = low
            else:
                lows[...] += low

        pieces = [stream.down(weights, n) for n in range(2)] + [stream.gate_up(places, weights, n) for n in range(4)]
        stream.run(pieces, slots, sems, first, use)
        _put_low(sums, _own_group(lows[...], 2 * RANK))
        _split(places[2, 0], sums, keep, give)

    outs = [bf(rows, 2 * FF), bf(rows, WIDE), bf(rows, 2 * RANK), _f32(ROWS, WIDE), bf(ROWS, WIDE)]
    ins = [own, other, ff_up, ff_down, gu, maps_up]
    scratch = [pltpu.VMEM((rows, WIDE), F32), pltpu.VMEM((rows, 4 * RANK), F32)]
    return stream.call(body, "feed_forward_back", ins, outs, scratch)


def project_qkv(x, w, low, maps_up):
    rows, tile = x.shape[0], 512

    def body(x, w, low, up, out, squares):
        i = pl.program_id(0)

        @pl.when(i == 0)
        def _():
            squares[...] = jnp.zeros_like(squares)

        total = jnp.dot(x[...], w[...], preferred_element_type=F32)
        total = total + jnp.dot(low[...], up[...], preferred_element_type=F32)
        out[...] = total
        here = lax.broadcasted_iota(jnp.int32, squares.shape, 1) == i // 2
        squares[...] += jnp.where(here, jnp.sum(total * total, axis=1, keepdims=True), 0.0)

    whole = lambda v: pl.BlockSpec(v.shape, lambda i: (0, 0))
    column = lambda n: pl.BlockSpec((n, tile), lambda i: (0, i))
    return pl.pallas_call(
        body,
        grid=(3 * HALF // tile,),
        out_shape=[_f32(rows, 3 * HALF), _f32(rows, 128)],
        in_specs=[whole(x), column(D), whole(low), column(maps_up.shape[0])],
        out_specs=[column(rows), pl.BlockSpec((rows, 128), lambda i: (0, 0))],
        compiler_params=pltpu.CompilerParams(vmem_limit_bytes=32 * 2**20),
        cost_estimate=pl.CostEstimate(flops=2 * rows * D * 3 * HALF, bytes_accessed=18_000_000, transcendentals=0),
        name="project_qkv",
    )(x, w, low, maps_up)


def project_out(me, heads, w, maps_down):
    rows = 2 * ROWS

    def body(me, heads, w, down, keep, give, flat, sums):
        flat[...] = jnp.concatenate([heads[h] for h in range(8)], axis=1)
        for n in range(0, D, 512):
            sums[:, n : n + 512] = jnp.dot(flat[...], w[:, n : n + 512], preferred_element_type=F32)
        _put_low(sums, _own_group(lax.dot_general(flat[...], down[...], **NT), RANK))
        _split(me[CORE], sums, keep, give)

    outs = [_f32(ROWS, WIDE), bf(ROWS, WIDE), bf(rows, HALF)]
    return _plain(body, "project_out", outs, [heads, w, maps_down], [me], [pltpu.VMEM((rows, WIDE), F32)])


def _low_and_sum(me, keep, got, maps, count, factor):
    total = keep[...] + got[...].astype(F32)
    low = (factor * total[:, D : D + count]).astype(BF)
    start = pl.multiple_of(me[CORE] * count, count)
    return total[:, :D], low, jnp.dot(low, maps[pl.ds(start, count), :], preferred_element_type=F32)


def _send(out, value, low):
    out[:, :D] = value.astype(BF)
    out[:, D:] = jnp.zeros((ROWS, WIDE - D), BF)
    out[:, D : D + low.shape[1]] = low


def _inverse(field):
    return lax.rsqrt(jnp.mean(field * field, axis=1, keepdims=True) + EPS)


def combine_attention(me, keep, got, tokens, gains, maps_up):
    def body(me, keep, got, tokens, gains, up, pre, hidden, out):
        total, low, raised = _low_and_sum(me, keep, got, up, RANK, 1.0)
        field = total + 2.0 * raised
        pre[...] = field
        value = tokens[...].astype(F32) + field * _inverse(field) * gains[2:3]
        hidden[...] = value
        _send(out, value, low)

    outs = [_f32(ROWS, D), _f32(ROWS, D), bf(ROWS, WIDE)]
    return _plain(body, "combine_attention", outs, [keep, got, tokens, gains, maps_up], [me])


def combine_output(me, keep, got, hidden, cotangent, gains, maps_up):
    def body(me, keep, got, hidden, cotangent, gains, up, output, out):
        total, low, raised = _low_and_sum(me, keep, got, up, RANK, 1.0)
        field = total + 2.0 * raised
        inverse = _inverse(field)
        output[...] = (hidden[...] + field * inverse * gains[3:4]).astype(BF)
        _send(out, normalize_back(field, inverse, gains[3:4], cotangent[...].astype(F32)), low)

    outs = [bf(ROWS, D), bf(ROWS, WIDE)]
    return _plain(body, "combine_output", outs, [keep, got, hidden, cotangent, gains, maps_up], [me])


def combine_hidden(me, keep, got, cotangent, pre, gains, maps_down):
    def body(me, keep, got, cotangent, pre, gains, down, hidden, out):
        total, low, lowered = _low_and_sum(me, keep, got, down, 2 * RANK, 2.0)
        value = cotangent[...].astype(F32) + total + lowered
        hidden[...] = value
        field = pre[...]
        _send(out, normalize_back(field, _inverse(field), gains[2:3], value), low)

    outs = [_f32(ROWS, D), bf(ROWS, WIDE)]
    return _plain(body, "combine_hidden", outs, [keep, got, cotangent, pre, gains, maps_down], [me])


def combine_tokens(me, keep, got, hidden, maps_down):
    def body(me, keep, got, hidden, down, out, low_out):
        total, low, lowered = _low_and_sum(me, keep, got, down, 3 * RANK, 2.0)
        out[...] = (hidden[...] + total + lowered).astype(BF)
        low_out[...] = jnp.zeros_like(low_out)
        low_out[:, : 3 * RANK] = low

    outs = [bf(ROWS, D), bf(ROWS, 128)]
    return _plain(body, "combine_tokens", outs, [keep, got, hidden, maps_down], [me])


def project_out_back(me, own, other, w, maps_up, maps_down, h2, attended):
    rows = 2 * ROWS

    def body(me, own, other, w, up, down, h2, attended, out, low_ref, pair):
        _pair_up(me[CORE], own, other, pair)
        low = 2.0 * lax.dot_general(pair[:, :D], up[...], **NT)
        low_ref[...] = jnp.where(_in_group(rows, 2 * RANK, RANK), low, 0.0).astype(BF)
        for n in range(0, HALF, 512):
            total = lax.dot_general(pair[:, :D], w[n : n + 512, :], **NT)
            total = total + jnp.dot(low_ref[...], down[:, n : n + 512], preferred_element_type=F32)
            for h in range(4):
                out[n // HD + h, :rows] = total[:, h * HD : (h + 1) * HD].astype(BF)

        def shared(columns, start):
            picked = jnp.concatenate([columns[:, start : start + RANK]] * 2, axis=1)
            return jnp.where(_in_group(rows, 2 * RANK, RANK), picked, jnp.zeros_like(picked))

        here = pl.ds(pl.multiple_of(me[CORE] * HALF, HALF), HALF)
        pieces = [
            (shared(pair, D), h2[:, here]),
            (shared(pair, D + RANK), h2[:, here]),
            (low_ref[...], attended[...]),
            (2 * shared(h2, D), pair[:, here]),
        ]
        for p, (picked, act) in enumerate(pieces):
            grad = lax.dot_general(picked, act, **TN).astype(BF)
            at = slice(rows + 2 * RANK * p, rows + 2 * RANK * (p + 1))
            for b in range(8):
                out[b, at] = grad[:, HD * b : HD * (b + 1)]

    outs = [bf(8, rows + 8 * RANK, HD), bf(rows, 2 * RANK)]
    ins = [own, other, w, maps_up, maps_down, h2, attended]
    return _plain(body, "project_out_back", outs, ins, [me], [pltpu.VMEM((rows, WIDE), BF)])


def project_qkv_back(me, weighted, value_grad, qkv, squares, sums, w, maps_up):
    rows, tile = 2 * ROWS, 512

    def body(me, wq, wk, dv, q, k, sq, sq_other, su, su_other, w, up, d_qkv, keep, give, acc):
        i = pl.program_id(0)

        @pl.when(i == 0)
        def _():
            inverse = lax.rsqrt((sq[...] + sq_other[...]) / D + EPS)
            mean = (su[...] + su_other[...]) / D
            for n, (weight, field) in enumerate(((wq, q), (wk, k))):
                r, m = inverse[:, n : n + 1], mean[:, n : n + 1]
                d_qkv[:, n * HALF : (n + 1) * HALF] = (r * weight[...] - field[...] * (r * r * r * m)).astype(BF)
            d_qkv[:, 2 * HALF :] = dv[...]
            _put_low(acc, _own_group(lax.dot_general(d_qkv[...], up[...], **NT), 3 * RANK))

        acc[:, pl.ds(pl.multiple_of(i * tile, tile), tile)] = lax.dot_general(d_qkv[...], w[...], **NT)

        @pl.when(i == D // tile - 1)
        def _():
            _split(me[CORE], acc, keep, give)

    once = lambda v: pl.BlockSpec(v.shape, lambda i: (0, 0), pipeline_mode=pl.Buffered(1))
    third = lambda n: pl.BlockSpec((rows, HALF), lambda i: (0, n), pipeline_mode=pl.Buffered(1))
    ins = [*weighted, value_grad]
    return pl.pallas_call(
        body,
        grid=(D // tile,),
        out_shape=[bf(rows, 3 * HALF), _f32(ROWS, WIDE), bf(ROWS, WIDE)],
        in_specs=[_smem()]
        + [once(v) for v in ins]
        + [third(0), third(1)]
        + [once(v) for v in (*squares, *sums)]
        + [pl.BlockSpec((tile, 3 * HALF), lambda i: (i, 0)), once(maps_up)],
        out_specs=[once(jax.ShapeDtypeStruct((rows, 3 * HALF), BF))] + [once(_f32(ROWS, WIDE))] * 2,
        scratch_shapes=[pltpu.VMEM((rows, WIDE), F32)],
        compiler_params=pltpu.CompilerParams(vmem_limit_bytes=48 * 2**20),
        cost_estimate=pl.CostEstimate(flops=2 * rows * D * 3 * HALF, bytes_accessed=22_000_000, transcendentals=0),
        name="project_qkv_back",
    )(me, *ins, qkv, qkv, *squares, *sums, w, maps_up)


class Gather:
    def __init__(self):
        core = lax.axis_index("c")
        x, z = lax.axis_index("x"), lax.axis_index("z")
        yl, yh = lax.axis_index("yl"), lax.axis_index("yh")
        y = 2 * yh + yl
        sign = 1 - 2 * core
        ys = [lax.rem(y - sign * k + 8, 4) for k in range(4)]
        zs = [lax.rem(z - sign * k + 8, 4) for k in range(4)]
        self.yh = yh
        self.me = jnp.stack([core, x, yl, yh] + zs).astype(jnp.int32)
        self.places = jnp.stack([jnp.stack([v // 2 for v in ys]), jnp.stack([v % 2 for v in ys]), self.me[:4]]).astype(jnp.int32)
        self.lanes = {"y0": Lane(), "y1": Lane(), "z": Lane(), "cross": Lane()}

    def across(self, own):
        return self.lanes["cross"].send(own, "cross")

    def over_xz(self, own, other, *before):
        other = after(other, *before)
        both = jnp.where(self.yh == 0, jnp.stack([own, other]), jnp.stack([other, own]))
        return lax.all_gather(both, ("x", "z")).reshape(4, 4, 2, *own.shape)

    def small(self, own):
        got = [own]
        for _ in range(3):
            got.append(self.lanes["z"].send(got[-1], "z"))
        return got

    def round(self, rings, *before):
        for n in range(2):
            value = after(rings[n][-1], *before) if before else rings[n][-1]
            rings[n].append(self.lanes["y%d" % n].send(value, "y"))


def turn(value, cosine, sine):
    return value * cosine + pltpu.roll(value, 64, 1) * sine


def _gain(gains, n, h, core):
    return gains[n : n + 1, pl.ds(pl.multiple_of((2 * h + core) * HD, HD), HD)]


def _pack_body(me, q, k, v, squares, other, gains, cosine, sine, out):
    scales = lax.rsqrt((squares[...] + other[...]) / D + EPS)
    c, s = cosine[...], sine[...]
    for h in range(4):
        here = slice(h * HD, (h + 1) * HD)
        out[h, :, 0:HD] = turn(q[:, here] * scales[:, 0:1] * _gain(gains, 0, h, me[CORE]), c, s).astype(BF)
        out[h, :, HD : 2 * HD] = turn(k[:, here] * scales[:, 1:2] * _gain(gains, 1, h, me[CORE]), c, s).astype(BF)
        out[h, :, 2 * HD :] = v[:, here].astype(BF)


def _head_specs(rows):
    whole = pl.BlockSpec((rows, HD), lambda i: (0, 0))
    columns = [pl.BlockSpec((rows, 4 * HD), lambda i, n=n: (0, 2 * n + i)) for n in range(3)]
    heads = pl.BlockSpec((4, rows, 3 * HD), lambda i: (i, 0, 0))
    gains = pl.BlockSpec((4, 8 * HD), lambda i: (0, i))
    return whole, columns, heads, gains


def pack_heads(me, qkv, squares, other, gains, cosine, sine):
    rows = qkv.shape[0]
    whole, columns, heads, gain = _head_specs(rows)
    return pl.pallas_call(
        _pack_body,
        grid=(2,),
        out_shape=bf(8, rows, 3 * HD),
        in_specs=[_smem(), *columns, whole, whole, gain, whole, whole],
        out_specs=heads,
        name="pack_heads",
    )(me, qkv, qkv, qkv, squares, other, gains, cosine, sine)


def _unpack_body(me, d, q, k, gains, cosine, sine, wq, wk, dv, sums):
    c, s = cosine[...], -sine[...]

    @pl.when(pl.program_id(0) == 0)
    def _():
        sums[...] = jnp.zeros_like(sums)

    lane = lax.broadcasted_iota(jnp.int32, sums.shape, 1)
    of_q, of_k = 0.0, 0.0
    for h in range(4):
        here = slice(h * HD, (h + 1) * HD)
        gq = turn(d[h, :, 0:HD].astype(F32), c, s) * _gain(gains, 0, h, me[CORE])
        gk = turn(d[h, :, HD : 2 * HD].astype(F32), c, s) * _gain(gains, 1, h, me[CORE])
        wq[:, here] = gq
        wk[:, here] = gk
        dv[:, here] = d[h, :, 2 * HD :]
        of_q += gq * q[:, here]
        of_k += gk * k[:, here]
    of_q, of_k = jnp.sum(of_q, axis=1, keepdims=True), jnp.sum(of_k, axis=1, keepdims=True)
    sums[...] += jnp.where(lane == 0, of_q, jnp.where(lane == 1, of_k, 0.0))


def unpack_heads(me, d, qkv, gains, cosine, sine):
    rows = qkv.shape[0]
    whole, columns, heads, gain = _head_specs(rows)
    return pl.pallas_call(
        _unpack_body,
        grid=(2,),
        out_shape=[_f32(rows, HALF), _f32(rows, HALF), bf(rows, HALF), _f32(rows, HD)],
        in_specs=[_smem(), heads, *columns[:2], gain, whole, whole],
        out_specs=[columns[0], columns[0], columns[0], whole],
        name="unpack_heads",
    )(me, d, qkv, qkv, gains, cosine, sine)


TILE = 128
def hidden_pairs(t, bound):
    query = t * TILE + lax.broadcasted_iota(jnp.int32, (TILE, TILE), 0)
    key = t * TILE + lax.broadcasted_iota(jnp.int32, (TILE, TILE), 1)
    hidden = key > query
    if t * TILE >= PROMPT:
        hidden = hidden | ((query >= bound) & (key < bound))
    return hidden


def tile_scores(q, k, t, bound):
    n = (t + 1) * TILE
    s = lax.dot_general(q[t * TILE : n], k[:n], **NT) * SCALE
    last = jnp.where(hidden_pairs(t, bound), -1e30, s[:, n - TILE :])
    return last if t == 0 else jnp.concatenate([s[:, : n - TILE], last], axis=1)


def _attend_body(bounds, qkv, out, exact, total):
    bound = bounds[pl.program_id(0)]
    q = qkv[:, 0, :, 0:HD].reshape(TOTAL, HD)
    k = qkv[:, 0, :, HD : 2 * HD].reshape(TOTAL, HD)
    v = qkv[:, 0, :, 2 * HD :].reshape(TOTAL, HD)
    for t in range(TOTAL // TILE):
        n = (t + 1) * TILE
        s = tile_scores(q, k, t, bound)
        top = jnp.max(s, axis=1, keepdims=True)
        p = jnp.exp(s - top)
        denom = jnp.sum(p, axis=1, keepdims=True)
        o = jnp.dot(p.astype(BF), v[:n], preferred_element_type=F32) / denom
        exact[0, t * TILE : n] = o
        total[0, t * TILE : n] = top + jnp.log(denom)
    out[:, 0] = exact[0].reshape(8, ROWS, HD).astype(BF)


def attend(bounds, qkv):
    return pl.pallas_call(
        _attend_body,
        grid=(2,),
        out_shape=[
            jax.ShapeDtypeStruct((8, 2, ROWS, HD), BF),
            jax.ShapeDtypeStruct((2, TOTAL, HD), F32),
            jax.ShapeDtypeStruct((2, TOTAL, 1), F32),
        ],
        in_specs=[
            pl.BlockSpec(memory_space=pltpu.SMEM),
            pl.BlockSpec((8, 1, ROWS, 3 * HD), lambda g: (0, g, 0, 0)),
        ],
        out_specs=[
            pl.BlockSpec((8, 1, ROWS, HD), lambda g: (0, g, 0, 0)),
            pl.BlockSpec((1, TOTAL, HD), lambda g: (g, 0, 0)),
            pl.BlockSpec((1, TOTAL, 1), lambda g: (g, 0, 0)),
        ],
        compiler_params=pltpu.CompilerParams(vmem_limit_bytes=40 * 2**20),
        cost_estimate=pl.CostEstimate(flops=900_000_000, bytes_accessed=5_000_000, transcendentals=1_500_000),
        name="attend",
    )(bounds, qkv)


def _attend_back_body(bounds, qkv, grad, exact, total, out, dk, dv, dq):
    bound = bounds[pl.program_id(0)]
    q = qkv[:, 0, :, 0:HD].reshape(TOTAL, HD)
    k = qkv[:, 0, :, HD : 2 * HD].reshape(TOTAL, HD)
    v = qkv[:, 0, :, 2 * HD :].reshape(TOTAL, HD)
    g = grad[...].reshape(TOTAL, HD)
    dk[...] = jnp.zeros_like(dk)
    dv[...] = jnp.zeros_like(dv)
    for t in range(TOTAL // TILE):
        n = (t + 1) * TILE
        here = slice(t * TILE, n)
        s = tile_scores(q, k, t, bound)
        p = jnp.exp(s - total[0, here])
        delta = jnp.sum(g[here].astype(F32) * exact[0, here], axis=1, keepdims=True)
        dp = lax.dot_general(g[here], v[:n], **NT)
        ds = (p * (dp - delta)).astype(BF)
        dq[here] = jnp.dot(ds, k[:n], preferred_element_type=F32) * SCALE
        dk[:n] += lax.dot_general(ds, q[here], **TN) * SCALE
        dv[:n] += lax.dot_general(p.astype(BF), g[here], **TN)
    out[:, 0, :, 0:HD] = dq[...].reshape(8, ROWS, HD).astype(BF)
    out[:, 0, :, HD : 2 * HD] = dk[...].reshape(8, ROWS, HD).astype(BF)
    out[:, 0, :, 2 * HD :] = dv[...].reshape(8, ROWS, HD).astype(BF)


def attend_back(bounds, qkv, grad, exact, total):
    return pl.pallas_call(
        _attend_back_body,
        grid=(2,),
        out_shape=jax.ShapeDtypeStruct((8, 2, ROWS, 3 * HD), BF),
        in_specs=[
            pl.BlockSpec(memory_space=pltpu.SMEM),
            pl.BlockSpec((8, 1, ROWS, 3 * HD), lambda g: (0, g, 0, 0)),
            pl.BlockSpec((8, ROWS, HD), lambda g: (0, g, 0)),
            pl.BlockSpec((1, TOTAL, HD), lambda g: (g, 0, 0)),
            pl.BlockSpec((1, TOTAL, 1), lambda g: (g, 0, 0)),
        ],
        out_specs=pl.BlockSpec((8, 1, ROWS, 3 * HD), lambda g: (0, g, 0, 0)),
        scratch_shapes=[pltpu.VMEM((TOTAL, HD), F32)] * 3,
        compiler_params=pltpu.CompilerParams(vmem_limit_bytes=40 * 2**20),
        cost_estimate=pl.CostEstimate(flops=2_300_000_000, bytes_accessed=8_000_000, transcendentals=1_500_000),
        name="attend_back",
    )(bounds, qkv, grad, exact, total)


def dot(a, b):
    return jnp.dot(a, b, preferred_element_type=F32)


def dot_nt(a, b):
    return lax.dot_general(a, b, **NT)


def dot_tn(a, b):
    return lax.dot_general(a, b, **TN)


def normalize_back(field, inverse, gain, grad):
    weighted = grad * gain
    return inverse * weighted - field * inverse**3 * jnp.mean(weighted * field, axis=-1, keepdims=True)


def choose_adapters(slots, down_in, down_ff, up_model, up_hidden):
    def body(slots, down_in, down_ff, up_model, up_hidden, qkv_down, gu_down, out_down, ff_down, qkv_up, out_up, ff_up, gu_up):
        core = slots[2]
        qkv_down[...] = down_in[0, :3].reshape(3 * RANK, D)
        gu_down[...] = down_in[0, 4:].reshape(2 * RANK, D)
        out_up[...] = up_model[0, 3]
        ff_up[...] = up_model[0, 4]
        qkv_up[...] = jnp.zeros_like(qkv_up)
        gu_up[...] = jnp.zeros_like(gu_up)
        for h in range(8):
            head = pl.ds(pl.multiple_of((2 * h + core) * HD, HD), HD)
            out_down[:, HD * h : HD * (h + 1)] = down_in[0, 3, :, head]
            for n in range(3):
                here = slice(n * HALF + HD * h, n * HALF + HD * (h + 1))
                qkv_up[n * RANK : (n + 1) * RANK, here] = up_model[0, n, :, head]
        for m in range(FF // 128):
            start = (2 * (m // 4) + core) * 512 + (m % 4) * 128
            units = pl.ds(pl.multiple_of(start, 128), 128)
            ff_down[:, 128 * m : 128 * (m + 1)] = down_ff[0, :, units]
            for n in range(2):
                here = slice(256 * m + 128 * n, 256 * m + 128 * (n + 1))
                gu_up[n * RANK : (n + 1) * RANK, here] = up_hidden[0, n, :, units]

    def chosen(shape):
        return pl.BlockSpec((1,) + shape[1:], lambda g, slots: (slots[g],) + (0,) * (len(shape) - 1))

    shapes = [(48, D), (32, D), (16, HALF), (16, FF), (48, 3 * HALF), (16, D), (16, D), (32, 2 * FF)]
    maps = [down_in, down_ff, up_model, up_hidden]
    return pl.pallas_call(
        body,
        out_shape=[bf(2 * r, c) for r, c in shapes],
        grid_spec=pltpu.PrefetchScalarGridSpec(
            num_scalar_prefetch=1,
            grid=(2,),
            in_specs=[chosen(m.shape) for m in maps],
            out_specs=[pl.BlockSpec(shape, lambda g, slots: (g, 0)) for shape in shapes],
        ),
        cost_estimate=pl.CostEstimate(flops=0, bytes_accessed=7_000_000, transcendentals=0),
        name="choose_adapters",
    )(slots, *maps)


def rank_gradients(lows, acts, core, name, plan, width):
    count = len(lows)

    def body(core, *refs):
        lows, acts, out = refs[:count], refs[count:-1], refs[-1]
        at = 0
        for low, act, columns, factor, starts in plan:
            picked = [lows[low][:, c : c + RANK] for c in columns]
            picked = jnp.concatenate(picked, axis=1)
            if columns[0] == columns[1]:
                picked = jnp.where(_in_group(2 * ROWS, 2 * RANK, RANK), picked, jnp.zeros_like(picked))
            if factor != 1:
                picked = picked * factor
            for start in starts(core[0]):
                right = acts[act][:, start if isinstance(start, slice) else pl.ds(pl.multiple_of(start, 128), 128)]
                n = right.shape[1]
                grad = lax.dot_general(picked, right, **TN).astype(BF)
                for b in range(n // 128):
                    block, slot = divmod(at, width // 128)
                    out[block, :, 128 * slot : 128 * (slot + 1)] = grad[:, 128 * b : 128 * (b + 1)]
                    at += 1

    return _plain(body, name, [bf(8, 2 * RANK, width)], list(lows) + list(acts), [core])[0]


def adapter_outputs(core, halves, others, shapes, name, write, done=()):
    count = len(halves)

    def body(core, *refs):
        own, other = refs[:count], refs[count : 2 * count]
        ready, outs = refs[2 * count : 2 * count + len(done)], refs[2 * count + len(done) :]

        def place(start):
            return pl.ds(pl.multiple_of(start, 128), 128)

        for side, group in ((core[0], own), (1 - core[0], other)):

            def block(n, b, t):
                return group[n][b, 0, :, 128 * t : 128 * (t + 1)].astype(F32)

            write(side, block, place, outs, *ready)

    arrays = halves + others
    size = sum(v.size * 2 for v in arrays)
    return pl.pallas_call(
        body,
        grid=(8,),
        out_shape=[jax.ShapeDtypeStruct(s, F32) for s in shapes],
        in_specs=[_smem()] + [pl.BlockSpec((8, 1) + v.shape[2:], lambda i: (0, i, 0, 0)) for v in arrays]
        + [pl.BlockSpec((1,) + v.shape[1:], lambda i: (i, 0, 0, 0)) for v in done],
        out_specs=[pl.BlockSpec((1,) + s[1:], lambda i, n=len(s): (i,) + (0,) * (n - 1)) for s in shapes],
        compiler_params=pltpu.CompilerParams(vmem_limit_bytes=40 * 2**20),
        cost_estimate=pl.CostEstimate(flops=0, bytes_accessed=size, transcendentals=0),
        name=name,
    )(core, *arrays, *done)


def write_early(side, block, place, outs):
    up_hidden, down_ff, middle = outs
    slots = EARLY // 128
    for m in range(FF // 128):
        units = place((2 * (m // 4) + side) * 512 + (m % 4) * 128)
        up_hidden[0, 0, :, units] = block(0, *divmod(m, slots))
        up_hidden[0, 1, :, units] = block(0, *divmod(32 + m, slots))
        down_ff[0, :, units] = block(0, *divmod(64 + m, slots))
    for m in range(8):
        whole, head = place(side * HALF + 128 * m), place((2 * m + side) * HD)
        for n in range(2):
            middle[0, n, :, whole] = block(0, m, slots + n)
        middle[0, 2, :, head] = block(0, m, slots + 2)
        middle[0, 3, :, whole] = block(0, m, slots + 3)
        middle[0, 4, :, whole] = block(0, *divmod(96 + m, slots))


def write_late(side, block, place, outs, middle):
    down_in, up_model = outs
    for n, m in ((4, 0), (5, 1), (3, 2)):
        down_in[0, n] = middle[0, m]
    for n in (3, 4):
        up_model[0, n] = middle[0, n]
    slots = LATE // 128
    for m in range(8):
        whole, head = place(side * HALF + 128 * m), place((2 * m + side) * HD)
        for n in range(3):
            down_in[0, n, :, whole] = block(0, *divmod(8 * n + m, slots))
            up_model[0, n, :, head] = block(0, *divmod(24 + 8 * n + m, slots))


def on_device(
    tokens,
    cotangent,
    query_matrix,
    key_matrix,
    value_matrix,
    output_matrix,
    gate_matrix,
    upward_matrix,
    down_matrix,
    gains,
    adapter_down_inputs,
    adapter_down_feedforward,
    adapter_up_model_maps,
    adapter_up_hidden_maps,
    group_adapter_index,
    continuation_lengths,
):
    core = lax.axis_index("c")
    first = core == 0
    ctx = lax.axis_index("yl") * 4 + lax.axis_index("x")
    tokens, cotangent = tokens[0], cotangent[0]

    def both(own, other):
        return jnp.where(first, jnp.stack([own, other]), jnp.stack([other, own]))

    def rows_of_both(own):
        return both(own, swap(own)).reshape(2 * own.shape[0], own.shape[1])

    plan = Gather()
    me, places = plan.me, plan.places
    keep_a, give_a = split_a(me, query_matrix, key_matrix, value_matrix)
    keep_g, give_g = split_g(me, gate_matrix, upward_matrix)
    got_a, got_g = swap(give_a), swap(give_g)
    xs_a, ys_a = parts_a(me, keep_a, got_a, output_matrix)
    xs_m, ys_g = parts_m(me, keep_g, got_g, down_matrix)
    crossed = plan.across(xs_a)
    small_a = plan.small(ys_a)
    small_g = plan.small(ys_g)
    xs_a = plan.over_xz(xs_a, crossed, small_a[1])
    crossed = plan.across(after(xs_m, small_a[2]))
    y_a = spread(me, small_a, [(0, HALF, 1)], "spread_a")
    rings_a = [[v] for v in y_a]
    for _ in range(3):
        plan.round(rings_a)
    xs_m = plan.over_xz(xs_m, crossed, rings_a[0][1], rings_a[1][1])
    w_qkv, w_out = assemble(Chunks(256, CUT_A, 4 * HALF, places, xs_a, 0, rings_a))
    small_g[3] = after(small_g[3], w_qkv)
    rings_g = [[v] for v in spread(me, small_g, [(0, FF - CUT_G // 2, 1)], "spread_g")]
    plan.round(rings_g)

    facts = jnp.concatenate([group_adapter_index[0], continuation_lengths[0]]).astype(F32)
    facts = jnp.broadcast_to(jnp.pad(facts, (0, 125))[None], (8, 128))
    pair_facts = both(facts, swap(facts))[:, 0, :2].astype(jnp.int32)
    slots = pair_facts[:, 0]
    bounds = PROMPT + pair_facts[:, 1]
    (qkv_down, gu_down, out_down, ff_down, qkv_up, out_up2, ff_up2, gu_up) = choose_adapters(
        jnp.concatenate([slots, me[:1]]),
        adapter_down_inputs,
        adapter_down_feedforward,
        adapter_up_model_maps,
        adapter_up_hidden_maps,
    )

    group_row = lax.broadcasted_iota(jnp.int32, (2 * ROWS, 1), 0) // ROWS

    def own_columns(low, count):
        group_column = lax.broadcasted_iota(jnp.int32, (1, 2 * count), 1) // count
        return jnp.where(group_row == group_column, low, jnp.zeros_like(low))

    shard = ("z", "yh")

    def spread_over(value, axes):
        return lax.all_to_all(jnp.broadcast_to(value[None], (8,) + value.shape), axes, 0, 0, tiled=True)

    place = ctx * ROWS + lax.broadcasted_iota(jnp.int32, (2, ROWS), 1)
    position = jnp.where(place >= bounds[:, None], PROMPT + place - bounds[:, None], place)
    freq = BASE ** (-(jnp.arange(HD // 2, dtype=F32) * 2.0 / HD))
    angle = position.reshape(2 * ROWS, 1).astype(F32) * freq[None]
    cosine = jnp.concatenate([jnp.cos(angle)] * 2, axis=1)
    sine = jnp.concatenate([-jnp.sin(angle), jnp.sin(angle)], axis=1)

    def whole(n):
        return lambda core: [slice(0, n)]

    def half(core):
        return [core * HALF + 128 * m for m in range(8)]

    def turns(n):
        return lambda core: [slice(256 * m + 128 * n, 256 * m + 128 * (n + 1)) for m in range(FF // 128)]

    def third(n):
        return lambda core: [slice(n * HALF, (n + 1) * HALF)]

    x2 = rows_of_both(tokens)
    qkv_low = own_columns((2.0 * dot_nt(x2, qkv_down).astype(BF)).astype(BF), 3 * RANK)
    qkv, squares = project_qkv(x2, w_qkv, qkv_low, qkv_up)
    squares = (squares, swap(squares))
    packed = pack_heads(me, qkv, *squares, gains, cosine, sine)
    heads = lax.all_to_all(packed, CTX, 0, 0, tiled=True).reshape(8, 2, ROWS, 3 * HD)
    heads = after(heads, rings_g[0][-1], rings_g[1][-1])
    plan.round(rings_g, heads)
    out_heads, exact, log_total = attend(bounds, heads)
    attended = lax.all_to_all(out_heads, CTX, 0, 0, tiled=True).reshape(8, 2 * ROWS, HD)
    keep, give, attended = project_out(me, attended, w_out, out_down)
    attn_pre, hidden, sent = combine_attention(me, keep, swap(give), tokens, gains, out_up2)

    sent = after(sent, rings_g[0][-1], rings_g[1][-1])
    plan.round(rings_g, attended)
    wg = Chunks(256, CUT_G, 2 * FF, places, xs_m, 0, rings_g)
    gu, mixed, h2, gu_low, keep, give = feed_forward(wg, sent, swap(sent), gu_down, gu_up, ff_down)
    output, sent = combine_output(me, keep, swap(give), hidden, cotangent, gains, ff_up2)

    d_gu, d_mlp, ff_grad_low, keep, give = feed_forward_back(wg, sent, swap(sent), ff_up2, ff_down, gu, gu_up)
    early = rank_gradients(
        [gu_low, ff_grad_low, d_mlp],
        [d_gu, mixed, d_mlp],
        me,
        "early_gradients",
        [
            (0, 0, (0, 2 * RANK), 1, turns(0)),
            (0, 0, (RANK, 3 * RANK), 1, turns(1)),
            (1, 1, (0, RANK), 1, whole(FF)),
            (2, 2, (D, D), 2, half),
        ],
        EARLY,
    )
    d_hidden, sent = combine_hidden(me, keep, swap(give), cotangent, attn_pre, gains, gu_down)
    sent, early = lax.optimization_barrier((sent, early))
    early = lax.all_to_all(early, CTX, 0, 0, tiled=True)

    d_out_heads, _ = project_out_back(me, sent, swap(sent), w_out, out_up2, out_down, h2, attended)
    d_out_heads = lax.all_to_all(d_out_heads, CTX, 0, 0, tiled=True)
    own = jnp.sum(early.astype(F32), axis=0).astype(BF)
    middle = jnp.sum(d_out_heads[:, 2 * ROWS :].astype(F32), axis=0).astype(BF).reshape(4, 2 * RANK, HD)
    own = jnp.concatenate([own, *middle], axis=1)
    own_slot = jnp.repeat(slots, RANK)[:, None] == lax.broadcasted_iota(jnp.int32, (1, 128), 1)
    own = jnp.concatenate([own, own_slot.astype(BF)], axis=1)
    d_out_heads, own = lax.optimization_barrier((d_out_heads, own))
    groups = spread_over(own, shard).reshape(16, RANK, EARLY + MIDDLE + 128)
    d_heads = attend_back(bounds, heads, d_out_heads, exact, log_total)
    d_heads = lax.all_to_all(d_heads, CTX, 0, 0, tiled=True).reshape(8, 2 * ROWS, 3 * HD)
    w_q, w_k, d_v, sums = unpack_heads(me, d_heads, qkv, gains, cosine, sine)

    def by_slot(groups):
        flat = groups.reshape(16, -1)
        return lax.dot_general(picker, flat, **TN).astype(BF).reshape(8 * RANK, -1)

    picker = groups[:, 0, EARLY + MIDDLE : EARLY + MIDDLE + 8]
    early, w_q = lax.optimization_barrier((by_slot(groups[:, :, : EARLY + MIDDLE]), w_q))
    early = lax.all_gather(early, CTX)
    d_qkv, keep, give = project_qkv_back(me, (w_q, w_k), d_v, qkv, squares, (sums, swap(sums)), w_qkv, qkv_up)
    grad_tokens, low = combine_tokens(me, keep, swap(give), d_hidden, qkv_down)
    low = both(low, swap(low)).reshape(2 * ROWS, 128)

    late = rank_gradients(
        [low, qkv_low],
        [x2, d_qkv],
        me,
        "late_gradients",
        [(0, 0, (n * RANK, n * RANK), 1, half) for n in range(3)]
        + [(1, 1, (n * RANK, (3 + n) * RANK), 1, third(n)) for n in range(3)],
        LATE,
    )
    late = lax.all_to_all(late, CTX, 0, 0, tiled=True)
    late = jnp.sum(late.astype(F32), axis=0).astype(BF)
    late = spread_over(late, shard)
    early, late = lax.optimization_barrier((early, late))
    late = spread_over(by_slot(late.reshape(16, RANK, LATE)), CTX)
    shape = (8, 8, RANK, -1)
    early = early.reshape(shape)
    early_other = swap(early)
    grad_up_hidden, grad_down_ff, middle = adapter_outputs(
        me,
        [early],
        [early_other],
        [(8, 2, RANK, 2 * FF), (8, RANK, 2 * FF), (8, 5, RANK, D)],
        "early_outputs",
        write_early,
    )
    late, middle = lax.optimization_barrier((late, middle))
    late_other = swap(late)
    late, late_other = late.reshape(shape), late_other.reshape(shape)
    shapes = [(8, 6, RANK, D), (8, 5, RANK, D)]
    grad_down_in, grad_up_model = adapter_outputs(
        me, [late], [late_other], shapes, "late_outputs", write_late, [middle]
    )
    return (output[None], grad_tokens[None], grad_down_in, grad_down_ff, grad_up_model, grad_up_hidden)


def solution(mesh):
    fine = Mesh(mesh.devices.reshape(2, 4, 4, 2, 2), ALL)
    shard = ("z", "yh", "c")
    rows = P(shard, None)
    per_token = P(shard, CTX, None)
    return jax.shard_map(
        on_device,
        mesh=fine,
        in_specs=(per_token, per_token) + (rows,) * 7 + (P(),) * 5 + (rows, rows),
        out_specs=(per_token, per_token, P(), P(), P(), P()),
        check_vma=False,
    )
```

```python
import jax
import jax.numpy as jnp
from jax import lax
from jax.experimental import pallas as pl
from jax.experimental.pallas import tpu as pltpu
from jax.sharding import Mesh, PartitionSpec as P

HD = 128
PROMPT = 1024
ROWS = 144
TOTAL = 1152
D = 2048
HALF = 1024
FF = 4096
RANK = 16
SCALE = HD**-0.5
EPS = 1e-06
BASE = 500000.0
ALL = ("yl", "x", "z", "yh", "c")
CTX = ("yl", "x")
BF = jnp.bfloat16
F32 = jnp.float32
CUT_A, CUT_G = 2048, 4096
EARLY, MIDDLE, LATE = 1664, 512, 768


NT = dict(dimension_numbers=(((1,), (1,)), ((), ())), preferred_element_type=F32)
TN = dict(dimension_numbers=(((0,), (0,)), ((), ())), preferred_element_type=F32)


CORE, X, YL, YH, Z0 = 0, 1, 2, 3, 4


def _place(yl, x, z, yh, c):
    return (((yl * 4 + x) * 4 + z) * 2 + yh) * 2 + c


def _permutation(move):
    pairs = []
    for yl in range(2):
        for x in range(4):
            for z in range(4):
                for yh in range(2):
                    for c in range(2):
                        nx, ny, nz, nc = move(x, 2 * yh + yl, z, c)
                        pairs.append(
                            (_place(yl, x, z, yh, c), _place(ny % 2, nx % 4, nz % 4, (ny % 4) // 2, nc))
                        )
    return pairs


STEPS = {
    "y": _permutation(lambda x, y, z, c: (x, (y + 1 - 2 * c) % 4, z, c)),
    "z": _permutation(lambda x, y, z, c: (x, y, z + 1 - 2 * c, c)),
    "cross": _permutation(lambda x, y, z, c: (x, 3 - y, z, c)),
    "core": _permutation(lambda x, y, z, c: (x, y, z, 1 - c)),
}


def swap(value):
    return lax.ppermute(value, ALL, STEPS["core"])


class Lane:
    def __init__(self):
        self.last = None

    def send(self, value, how):
        if self.last is not None:
            value, _ = lax.optimization_barrier((value, self.last))
        self.last = lax.ppermute(value, ALL, STEPS[how])
        return self.last


def after(value, *others):
    return lax.optimization_barrier((value, *others))[0]


def _smem():
    return pl.BlockSpec(memory_space=pltpu.SMEM)


def _vmem():
    return pl.BlockSpec(memory_space=pltpu.VMEM)


def _plain(body, name, outs, ins, scalars, scratch=(), limit=48):
    size = sum(v.size * v.dtype.itemsize for v in list(ins) + list(outs))
    return pl.pallas_call(
        body,
        out_shape=outs,
        in_specs=[_smem()] * len(scalars) + [_vmem()] * len(ins),
        out_specs=[_vmem()] * len(outs),
        scratch_shapes=list(scratch),
        compiler_params=pltpu.CompilerParams(vmem_limit_bytes=limit * 2**20),
        cost_estimate=pl.CostEstimate(flops=0, bytes_accessed=size, transcendentals=0),
        name=name,
    )(*scalars, *ins)


def bf(*shape):
    return jax.ShapeDtypeStruct(shape, BF)


def split_a(core, q, k, v):
    def body(core, q, k, v, keep, give):
        for n, w in enumerate((q, k, v)):
            for h in range(8):
                here = slice(n * HALF + HD * h, n * HALF + HD * (h + 1))
                keep[:, here] = w[:, pl.ds(pl.multiple_of((2 * h + core[0]) * HD, HD), HD)]
                give[:, here] = w[:, pl.ds(pl.multiple_of((2 * h + 1 - core[0]) * HD, HD), HD)]

    return _plain(body, "split_a", [bf(HD, 3 * HALF)] * 2, [q, k, v], [core])


def split_g(core, gate, upward):
    def body(core, gate, upward, keep, give):
        for m in range(FF // 128):
            for n, w in enumerate((gate, upward)):
                here = slice(256 * m + 128 * n, 256 * m + 128 * (n + 1))
                for side, out in ((core[0], keep), (1 - core[0], give)):
                    start = (2 * (m // 4) + side) * 512 + (m % 4) * 128
                    out[:, here] = w[:, pl.ds(pl.multiple_of(start, 128), 128)]

    return _plain(body, "split_g", [bf(HD, 2 * FF)] * 2, [gate, upward], [core])


def parts_a(me, keep, got, out):
    quarter = CUT_A // 4

    def body(me, keep, got, out, xs, ys):
        for side, w in ((me[CORE], keep), (1 - me[CORE], got)):
            rows = pl.ds(pl.multiple_of(side * HD, HD), HD)
            xs[rows, :] = w[:, pl.ds(pl.multiple_of(me[X] * quarter, 128), quarter)]

            @pl.when(me[YL] == 0)
            def _():
                ys[rows, :] = w[:, 2 * HALF :]

        @pl.when(me[YL] == 1)
        def _():
            ys[:HD, :] = out[:, :HALF]
            ys[HD:, :] = out[:, HALF:]

    return _plain(body, "parts_a", [bf(256, quarter), bf(256, HALF)], [keep, got, out], [me])


def parts_m(me, keep, got, down):
    gx, dx, gy = CUT_G // 4, D // 4, FF - CUT_G // 2

    def body(me, keep, got, down, xs, ys):
        for side, w in ((me[CORE], keep), (1 - me[CORE], got)):
            rows = pl.ds(pl.multiple_of(side * HD, HD), HD)
            xs[rows, :gx] = w[:, pl.ds(pl.multiple_of(me[X] * gx, 128), gx)]
            ys[rows, :] = w[:, pl.ds(pl.multiple_of(CUT_G + me[YL] * gy, 128), gy)]
        for n in range(2):
            rows = slice(256 * n, 256 * (n + 1))
            xs[:, gx + n * dx : gx + (n + 1) * dx] = down[rows, pl.ds(pl.multiple_of(me[X] * dx, 128), dx)]

    return _plain(body, "parts_m", [bf(256, gx + 2 * dx), bf(256, gy)], [keep, got, down], [me])


def spread(me, got, pieces, name):
    def body(me, *refs):
        chunks, outs = refs[:4], refs[4:]
        for k in range(4):
            z = me[Z0 + k]
            for p, (column, width, folds) in enumerate(pieces):
                for half in range(2):

                    @pl.when(z // 2 == half)
                    def _():
                        for n in range(folds):
                            at = pl.multiple_of(((z - 2 * half) * folds + n) * 256, 256)
                            start = column + n * width
                            outs[2 * p + half][pl.ds(at, 256), :] = chunks[k][:, start : start + width]

    outs = [bf(2 * folds * 256, width) for _, width, folds in pieces for _ in range(2)]
    return _plain(body, name, outs, list(got), [me])


class Chunks:
    def __init__(self, rows, cut, width, places, xs, column, y):
        self.rows, self.cx, self.cy = rows, cut, width - cut
        self.depth = 8 * rows
        self.places = places
        self.column = column
        self.arrays = [xs] + (y[0] + y[1] if y else [])


def _y_rows(places, rows, half, j, k):
    return pl.multiple_of((2 * half + j) * 2 * rows + places[0, k] * rows, rows)


def _panel_copies(rows, width, column, xs, whole, panels):
    copies = []
    for at, k in enumerate(panels):
        for z in range(4):
            for yh in range(2):
                for n in range(rows // 256):
                    target = whole.at[pl.ds((2 * z + yh) * rows + 256 * n, 256), pl.ds(at * width, width)]
                    copies.append((xs.at[k, z, yh, :, pl.ds(column + n * width, width)], target))
    return copies


def _y_copies(places, y, whole, k, column, width):
    copies = []
    for half in range(2):
        for j in range(2):
            row = _y_rows(places, 256, half, j, k)
            copies.append((y[4 * half + k].at[pl.ds(j * 256, 256)], whole.at[pl.ds(row, 256), pl.ds(column, width)]))
    return copies


def assemble(w):
    anywhere = pl.BlockSpec(memory_space=pl.ANY)

    def body(places, *refs):
        out, out_matrix, sems = refs[9], refs[10], refs[11]
        panels = _panel_copies(256, w.cx // 4, 0, refs[0], out, range(4))
        plain = [pltpu.make_async_copy(a, b, sems.at[n]) for n, (a, b) in enumerate(panels)]
        for copy in plain:
            copy.start()

        def move(started):
            at = len(plain)
            for k in range(4):
                for half in range(2):
                    for j in range(2):
                        source = refs[1 + 4 * half + k].at[pl.ds(j * 256, 256)]
                        block = 2 * (2 * half + j) + places[0, k]

                        @pl.when(places[1, k] == 0)
                        def _():
                            row = pl.multiple_of(block * 256, 256)
                            target = out.at[pl.ds(row, 256), pl.ds(2 * HALF, HALF)]
                            copy = pltpu.make_async_copy(source, target, sems.at[at])
                            copy.wait() if started else copy.start()

                        @pl.when(places[1, k] == 1)
                        def _():
                            for n in range(2):
                                row = pl.multiple_of(block * HD, HD)
                                target = out_matrix.at[pl.ds(row, HD), pl.ds(n * HALF, HALF)]
                                copy = pltpu.make_async_copy(source.at[pl.ds(n * HD, HD)], target, sems.at[at + n])
                                copy.wait() if started else copy.start()

                        at += 2

        move(False)
        for copy in plain:
            copy.wait()
        move(True)

    return pl.pallas_call(
        body,
        out_shape=[bf(D, 3 * HALF), bf(HALF, D)],
        in_specs=[_smem()] + [anywhere] * 9,
        out_specs=[_vmem()] * 2,
        scratch_shapes=[pltpu.SemaphoreType.DMA((64,))],
        compiler_params=pltpu.CompilerParams(vmem_limit_bytes=48 * 2**20),
        cost_estimate=pl.CostEstimate(flops=0, bytes_accessed=64 * 2**20, transcendentals=0),
        name="assemble",
    )(w.places, *w.arrays)


WIDE = D + 128


def _f32(*shape):
    return jax.ShapeDtypeStruct(shape, F32)


def _pair_up(core, own, other, pair):
    pair[pl.ds(pl.multiple_of(core * ROWS, ROWS), ROWS), :] = own[...]
    pair[pl.ds(pl.multiple_of((1 - core) * ROWS, ROWS), ROWS), :] = other[...]


def _split(core, sums, keep, give):
    keep[...] = sums[pl.ds(pl.multiple_of(core * ROWS, ROWS), ROWS), :]
    give[...] = sums[pl.ds(pl.multiple_of((1 - core) * ROWS, ROWS), ROWS), :].astype(BF)


def _in_group(rows, columns, count):
    row = lax.broadcasted_iota(jnp.int32, (rows, columns), 0) >= ROWS
    column = lax.broadcasted_iota(jnp.int32, (rows, columns), 1) >= count
    return row == column


def _own_group(low, count):
    row = lax.broadcasted_iota(jnp.int32, (low.shape[0], count), 0)
    return jnp.where(row >= ROWS, low[:, count:], low[:, :count])


def _put_low(sums, low):
    count = low.shape[1]
    sums[:, D:] = jnp.zeros((sums.shape[0], WIDE - D), F32)
    sums[:, D : D + count] = low


SLOT = D
SLOTS = 4


class Stream:
    def __init__(self, w):
        self.w = w

    def gate_up(self, places, refs, n):
        xs, y, quarter = refs[0], refs[1:9], CUT_G // 4
        if n < 2:
            return n * SLOT, lambda slot: _panel_copies(256, quarter, 0, xs, slot, range(2 * n, 2 * n + 2))
        column = pl.multiple_of(CUT_G + places[1, n - 2] * SLOT, SLOT)
        return column, lambda slot: [
            copy for k in (n - 2, n) for copy in _y_copies(places, y, slot, k, 0, SLOT)
        ]

    def down(self, refs, n):
        xs, quarter = refs[0], D // 4

        def copies(slot):
            made = []
            for k in range(4):
                for block in range(4 * n, 4 * n + 4):
                    for m in range(2):
                        source = xs.at[k, block // 2, block % 2, :, pl.ds(CUT_G // 4 + m * quarter, quarter)]
                        row = (block - 4 * n) * 512 + 256 * m
                        made.append((source, slot.at[pl.ds(row, 256), pl.ds(k * quarter, quarter)]))
            return made

        return n * SLOT, copies

    def run(self, pieces, slots, sems, first, use):
        copies = []
        for n, (_, made) in enumerate(pieces):
            slot = n % SLOTS
            pairs = made(slots.at[slot])
            copies.append([pltpu.make_async_copy(a, b, sems.at[slot, m]) for m, (a, b) in enumerate(pairs)])

        def begin(n):
            if n < len(copies):
                for copy in copies[n]:
                    copy.start()

        for n in range(SLOTS - 1):
            begin(n)
        first()
        for n, (at, _) in enumerate(pieces):
            for copy in copies[n]:
                copy.wait()
            use(n, at, slots.at[n % SLOTS])
            begin(n + SLOTS - 1)

    def call(self, body, name, ins, outs, scratch=()):
        w = self.w
        anywhere = pl.BlockSpec(memory_space=pl.ANY)
        size = 6 * D * FF + sum(v.size * v.dtype.itemsize for v in ins)
        return pl.pallas_call(
            body,
            out_shape=outs,
            in_specs=[_smem()] + [anywhere] * 9 + [_vmem()] * len(ins),
            out_specs=[_vmem()] * len(outs),
            scratch_shapes=[pltpu.VMEM((SLOTS, SLOT, SLOT), BF), pltpu.SemaphoreType.DMA((SLOTS, 32)), *scratch],
            compiler_params=pltpu.CompilerParams(vmem_limit_bytes=60 * 2**20),
            cost_estimate=pl.CostEstimate(flops=4 * ROWS * D * 3 * FF, bytes_accessed=size, transcendentals=0),
            name=name,
        )(w.places, *w.arrays, *ins)


def feed_forward(w, own, other, maps_down, maps_up, ff_down):
    rows = 2 * ROWS
    stream = Stream(w)

    def body(places, *refs):
        weights, (own_ref, other_ref, down_ref, up_ref, ff_ref) = refs[:9], refs[9:14]
        gu, mixed, pair, low_ref, keep, give, slots, sems, sums = refs[14:]

        def first():
            _pair_up(places[2, 0], own_ref, other_ref, pair)
            low = 2.0 * lax.dot_general(pair[:, :D], down_ref[...], **NT).astype(BF).astype(F32)
            low_ref[...] = jnp.where(_in_group(rows, 4 * RANK, 2 * RANK), low, 0.0).astype(BF)

        def use(n, at, slot):
            tile = SLOT // 2
            if n < 4:
                for t in range(2):
                    column = at + t * tile
                    unit = column // 2
                    if not isinstance(at, int):
                        column, unit = pl.multiple_of(column, tile), pl.multiple_of(unit, tile // 2)
                    total = jnp.dot(pair[:, :D], slot[:, t * tile : (t + 1) * tile], preferred_element_type=F32)
                    total = total + jnp.dot(low_ref[...], up_ref[:, pl.ds(column, tile)], preferred_element_type=F32)
                    gu[:, pl.ds(column, tile)] = total.astype(BF)
                    for m in range(tile // 256):
                        g, u = total[:, 256 * m : 256 * m + 128], total[:, 256 * m + 128 : 256 * m + 256]
                        mixed[:, pl.ds(unit + 128 * m, 128)] = (g * jax.nn.sigmoid(g) * u).astype(BF)
                return
            left = mixed[:, at : at + SLOT]
            for t in range(2):
                here = slice(t * tile, (t + 1) * tile)
                part = jnp.dot(left, slot[:, here], preferred_element_type=F32)
                if n == 4:
                    sums[:, here] = part
                else:
                    sums[:, here] += part

        pieces = [stream.gate_up(places, weights, n) for n in range(4)] + [stream.down(weights, n) for n in range(2)]
        stream.run(pieces, slots, sems, first, use)
        _put_low(sums, _own_group(lax.dot_general(mixed[...], ff_ref[...], **NT), RANK))
        _split(places[2, 0], sums, keep, give)

    outs = [bf(rows, 2 * FF), bf(rows, FF), bf(rows, WIDE), bf(rows, 4 * RANK), _f32(ROWS, WIDE), bf(ROWS, WIDE)]
    ins = [own, other, maps_down, maps_up, ff_down]
    return stream.call(body, "feed_forward", ins, outs, [pltpu.VMEM((rows, WIDE), F32)])


def feed_forward_back(w, own, other, ff_up, ff_down, gu, maps_up):
    rows = 2 * ROWS
    stream = Stream(w)

    def body(places, *refs):
        weights, (own_ref, other_ref, ff_up_ref, ff_down_ref, gu_ref, up_ref) = refs[:9], refs[9:15]
        out, pair, low_ref, keep, give, slots, sems, sums, lows = refs[15:]

        def first():
            _pair_up(places[2, 0], own_ref, other_ref, pair)
            low = 2.0 * lax.dot_general(pair[:, :D], ff_up_ref[...], **NT)
            low_ref[...] = jnp.where(_in_group(rows, 2 * RANK, RANK), low, 0.0).astype(BF)

        def use(n, at, slot):
            tile = SLOT // 2
            if n < 2:
                for t in range(2):
                    units = slice(at + t * tile, at + (t + 1) * tile)
                    d_mixed = lax.dot_general(pair[:, :D], slot[t * tile : (t + 1) * tile, :], **NT)
                    d_mixed = d_mixed + jnp.dot(low_ref[...], ff_down_ref[:, units], preferred_element_type=F32)
                    for m in range(tile // 128):
                        column = 2 * (at + t * tile) + 256 * m
                        g = gu_ref[:, column : column + 128].astype(F32)
                        u = gu_ref[:, column + 128 : column + 256].astype(F32)
                        d = d_mixed[:, 128 * m : 128 * (m + 1)]
                        s = jax.nn.sigmoid(g)
                        out[:, column : column + 128] = (d * u * s * (1.0 + g * (1.0 - s))).astype(BF)
                        out[:, column + 128 : column + 256] = (d * g * s).astype(BF)
                return
            left = out[:, pl.ds(at, SLOT)]
            low = lax.dot_general(left, up_ref[:, pl.ds(at, SLOT)], **NT)
            for t in range(2):
                here = slice(t * tile, (t + 1) * tile)
                part = lax.dot_general(left, slot[here, :], **NT)
                if n == 2:
                    sums[:, here] = part
                else:
                    sums[:, here] += part
            if n == 2:
                lows[...] = low
            else:
                lows[...] += low

        pieces = [stream.down(weights, n) for n in range(2)] + [stream.gate_up(places, weights, n) for n in range(4)]
        stream.run(pieces, slots, sems, first, use)
        _put_low(sums, _own_group(lows[...], 2 * RANK))
        _split(places[2, 0], sums, keep, give)

    outs = [bf(rows, 2 * FF), bf(rows, WIDE), bf(rows, 2 * RANK), _f32(ROWS, WIDE), bf(ROWS, WIDE)]
    ins = [own, other, ff_up, ff_down, gu, maps_up]
    scratch = [pltpu.VMEM((rows, WIDE), F32), pltpu.VMEM((rows, 4 * RANK), F32)]
    return stream.call(body, "feed_forward_back", ins, outs, scratch)


def project_qkv(x, w, low, maps_up):
    rows, tile = x.shape[0], 512

    def body(x, w, low, up, out, squares):
        i = pl.program_id(0)

        @pl.when(i == 0)
        def _():
            squares[...] = jnp.zeros_like(squares)

        total = jnp.dot(x[...], w[...], preferred_element_type=F32)
        total = total + jnp.dot(low[...], up[...], preferred_element_type=F32)
        out[...] = total
        here = lax.broadcasted_iota(jnp.int32, squares.shape, 1) == i // 2
        squares[...] += jnp.where(here, jnp.sum(total * total, axis=1, keepdims=True), 0.0)

    whole = lambda v: pl.BlockSpec(v.shape, lambda i: (0, 0))
    column = lambda n: pl.BlockSpec((n, tile), lambda i: (0, i))
    return pl.pallas_call(
        body,
        grid=(3 * HALF // tile,),
        out_shape=[_f32(rows, 3 * HALF), _f32(rows, 128)],
        in_specs=[whole(x), column(D), whole(low), column(maps_up.shape[0])],
        out_specs=[column(rows), pl.BlockSpec((rows, 128), lambda i: (0, 0))],
        compiler_params=pltpu.CompilerParams(vmem_limit_bytes=32 * 2**20),
        cost_estimate=pl.CostEstimate(flops=2 * rows * D * 3 * HALF, bytes_accessed=18_000_000, transcendentals=0),
        name="project_qkv",
    )(x, w, low, maps_up)


def project_out(me, heads, w, maps_down):
    rows = 2 * ROWS

    def body(me, heads, w, down, keep, give, flat, sums):
        flat[...] = jnp.concatenate([heads[h] for h in range(8)], axis=1)
        for n in range(0, D, 512):
            sums[:, n : n + 512] = jnp.dot(flat[...], w[:, n : n + 512], preferred_element_type=F32)
        _put_low(sums, _own_group(lax.dot_general(flat[...], down[...], **NT), RANK))
        _split(me[CORE], sums, keep, give)

    outs = [_f32(ROWS, WIDE), bf(ROWS, WIDE), bf(rows, HALF)]
    return _plain(body, "project_out", outs, [heads, w, maps_down], [me], [pltpu.VMEM((rows, WIDE), F32)])


def _low_and_sum(me, keep, got, maps, count, factor):
    total = keep[...] + got[...].astype(F32)
    low = (factor * total[:, D : D + count]).astype(BF)
    start = pl.multiple_of(me[CORE] * count, count)
    return total[:, :D], low, jnp.dot(low, maps[pl.ds(start, count), :], preferred_element_type=F32)


def _send(out, value, low):
    out[:, :D] = value.astype(BF)
    out[:, D:] = jnp.zeros((ROWS, WIDE - D), BF)
    out[:, D : D + low.shape[1]] = low


def _inverse(field):
    return lax.rsqrt(jnp.mean(field * field, axis=1, keepdims=True) + EPS)


def combine_attention(me, keep, got, tokens, gains, maps_up):
    def body(me, keep, got, tokens, gains, up, pre, hidden, out):
        total, low, raised = _low_and_sum(me, keep, got, up, RANK, 1.0)
        field = total + 2.0 * raised
        pre[...] = field
        value = tokens[...].astype(F32) + field * _inverse(field) * gains[2:3]
        hidden[...] = value
        _send(out, value, low)

    outs = [_f32(ROWS, D), _f32(ROWS, D), bf(ROWS, WIDE)]
    return _plain(body, "combine_attention", outs, [keep, got, tokens, gains, maps_up], [me])


def combine_output(me, keep, got, hidden, cotangent, gains, maps_up):
    def body(me, keep, got, hidden, cotangent, gains, up, output, out):
        total, low, raised = _low_and_sum(me, keep, got, up, RANK, 1.0)
        field = total + 2.0 * raised
        inverse = _inverse(field)
        output[...] = (hidden[...] + field * inverse * gains[3:4]).astype(BF)
        _send(out, normalize_back(field, inverse, gains[3:4], cotangent[...].astype(F32)), low)

    outs = [bf(ROWS, D), bf(ROWS, WIDE)]
    return _plain(body, "combine_output", outs, [keep, got, hidden, cotangent, gains, maps_up], [me])


def combine_hidden(me, keep, got, cotangent, pre, gains, maps_down):
    def body(me, keep, got, cotangent, pre, gains, down, hidden, out):
        total, low, lowered = _low_and_sum(me, keep, got, down, 2 * RANK, 2.0)
        value = cotangent[...].astype(F32) + total + lowered
        hidden[...] = value
        field = pre[...]
        _send(out, normalize_back(field, _inverse(field), gains[2:3], value), low)

    outs = [_f32(ROWS, D), bf(ROWS, WIDE)]
    return _plain(body, "combine_hidden", outs, [keep, got, cotangent, pre, gains, maps_down], [me])


def combine_tokens(me, keep, got, hidden, maps_down):
    def body(me, keep, got, hidden, down, out, low_out):
        total, low, lowered = _low_and_sum(me, keep, got, down, 3 * RANK, 2.0)
        out[...] = (hidden[...] + total + lowered).astype(BF)
        low_out[...] = jnp.zeros_like(low_out)
        low_out[:, : 3 * RANK] = low

    outs = [bf(ROWS, D), bf(ROWS, 128)]
    return _plain(body, "combine_tokens", outs, [keep, got, hidden, maps_down], [me])


def project_out_back(me, own, other, w, maps_up, maps_down, h2, attended):
    rows = 2 * ROWS

    def body(me, own, other, w, up, down, h2, attended, out, low_ref, pair):
        _pair_up(me[CORE], own, other, pair)
        low = 2.0 * lax.dot_general(pair[:, :D], up[...], **NT)
        low_ref[...] = jnp.where(_in_group(rows, 2 * RANK, RANK), low, 0.0).astype(BF)
        for n in range(0, HALF, 512):
            total = lax.dot_general(pair[:, :D], w[n : n + 512, :], **NT)
            total = total + jnp.dot(low_ref[...], down[:, n : n + 512], preferred_element_type=F32)
            for h in range(4):
                out[n // HD + h, :rows] = total[:, h * HD : (h + 1) * HD].astype(BF)

        def shared(columns, start):
            picked = jnp.concatenate([columns[:, start : start + RANK]] * 2, axis=1)
            return jnp.where(_in_group(rows, 2 * RANK, RANK), picked, jnp.zeros_like(picked))

        here = pl.ds(pl.multiple_of(me[CORE] * HALF, HALF), HALF)
        pieces = [
            (shared(pair, D), h2[:, here]),
            (shared(pair, D + RANK), h2[:, here]),
            (low_ref[...], attended[...]),
            (2 * shared(h2, D), pair[:, here]),
        ]
        for p, (picked, act) in enumerate(pieces):
            grad = lax.dot_general(picked, act, **TN).astype(BF)
            at = slice(rows + 2 * RANK * p, rows + 2 * RANK * (p + 1))
            for b in range(8):
                out[b, at] = grad[:, HD * b : HD * (b + 1)]

    outs = [bf(8, rows + 8 * RANK, HD), bf(rows, 2 * RANK)]
    ins = [own, other, w, maps_up, maps_down, h2, attended]
    return _plain(body, "project_out_back", outs, ins, [me], [pltpu.VMEM((rows, WIDE), BF)])


def project_qkv_back(me, weighted, value_grad, qkv, squares, sums, w, maps_up):
    rows, tile = 2 * ROWS, 512

    def body(me, wq, wk, dv, q, k, sq, sq_other, su, su_other, w, up, d_qkv, keep, give, acc):
        i = pl.program_id(0)

        @pl.when(i == 0)
        def _():
            inverse = lax.rsqrt((sq[...] + sq_other[...]) / D + EPS)
            mean = (su[...] + su_other[...]) / D
            for n, (weight, field) in enumerate(((wq, q), (wk, k))):
                r, m = inverse[:, n : n + 1], mean[:, n : n + 1]
                d_qkv[:, n * HALF : (n + 1) * HALF] = (r * weight[...] - field[...] * (r * r * r * m)).astype(BF)
            d_qkv[:, 2 * HALF :] = dv[...]
            _put_low(acc, _own_group(lax.dot_general(d_qkv[...], up[...], **NT), 3 * RANK))

        acc[:, pl.ds(pl.multiple_of(i * tile, tile), tile)] = lax.dot_general(d_qkv[...], w[...], **NT)

        @pl.when(i == D // tile - 1)
        def _():
            _split(me[CORE], acc, keep, give)

    once = lambda v: pl.BlockSpec(v.shape, lambda i: (0, 0), pipeline_mode=pl.Buffered(1))
    third = lambda n: pl.BlockSpec((rows, HALF), lambda i: (0, n), pipeline_mode=pl.Buffered(1))
    ins = [*weighted, value_grad]
    return pl.pallas_call(
        body,
        grid=(D // tile,),
        out_shape=[bf(rows, 3 * HALF), _f32(ROWS, WIDE), bf(ROWS, WIDE)],
        in_specs=[_smem()]
        + [once(v) for v in ins]
        + [third(0), third(1)]
        + [once(v) for v in (*squares, *sums)]
        + [pl.BlockSpec((tile, 3 * HALF), lambda i: (i, 0)), once(maps_up)],
        out_specs=[once(jax.ShapeDtypeStruct((rows, 3 * HALF), BF))] + [once(_f32(ROWS, WIDE))] * 2,
        scratch_shapes=[pltpu.VMEM((rows, WIDE), F32)],
        compiler_params=pltpu.CompilerParams(vmem_limit_bytes=48 * 2**20),
        cost_estimate=pl.CostEstimate(flops=2 * rows * D * 3 * HALF, bytes_accessed=22_000_000, transcendentals=0),
        name="project_qkv_back",
    )(me, *ins, qkv, qkv, *squares, *sums, w, maps_up)


class Gather:
    def __init__(self):
        core = lax.axis_index("c")
        x, z = lax.axis_index("x"), lax.axis_index("z")
        yl, yh = lax.axis_index("yl"), lax.axis_index("yh")
        y = 2 * yh + yl
        sign = 1 - 2 * core
        ys = [lax.rem(y - sign * k + 8, 4) for k in range(4)]
        zs = [lax.rem(z - sign * k + 8, 4) for k in range(4)]
        self.yh = yh
        self.me = jnp.stack([core, x, yl, yh] + zs).astype(jnp.int32)
        self.places = jnp.stack([jnp.stack([v // 2 for v in ys]), jnp.stack([v % 2 for v in ys]), self.me[:4]]).astype(jnp.int32)
        self.lanes = {"y0": Lane(), "y1": Lane(), "z": Lane(), "cross": Lane()}

    def across(self, own):
        return self.lanes["cross"].send(own, "cross")

    def over_xz(self, own, other, *before):
        other = after(other, *before)
        both = jnp.where(self.yh == 0, jnp.stack([own, other]), jnp.stack([other, own]))
        return lax.all_gather(both, ("x", "z")).reshape(4, 4, 2, *own.shape)

    def small(self, own):
        got = [own]
        for _ in range(3):
            got.append(self.lanes["z"].send(got[-1], "z"))
        return got

    def round(self, rings, *before):
        for n in range(2):
            value = after(rings[n][-1], *before) if before else rings[n][-1]
            rings[n].append(self.lanes["y%d" % n].send(value, "y"))


def turn(value, cosine, sine):
    return value * cosine + pltpu.roll(value, 64, 1) * sine


def _gain(gains, n, h, core):
    return gains[n : n + 1, pl.ds(pl.multiple_of((2 * h + core) * HD, HD), HD)]


def _pack_body(me, q, k, v, squares, other, gains, cosine, sine, out):
    scales = lax.rsqrt((squares[...] + other[...]) / D + EPS)
    c, s = cosine[...], sine[...]
    for h in range(4):
        here = slice(h * HD, (h + 1) * HD)
        out[h, :, 0:HD] = turn(q[:, here] * scales[:, 0:1] * _gain(gains, 0, h, me[CORE]), c, s).astype(BF)
        out[h, :, HD : 2 * HD] = turn(k[:, here] * scales[:, 1:2] * _gain(gains, 1, h, me[CORE]), c, s).astype(BF)
        out[h, :, 2 * HD :] = v[:, here].astype(BF)


def _head_specs(rows):
    whole = pl.BlockSpec((rows, HD), lambda i: (0, 0))
    columns = [pl.BlockSpec((rows, 4 * HD), lambda i, n=n: (0, 2 * n + i)) for n in range(3)]
    heads = pl.BlockSpec((4, rows, 3 * HD), lambda i: (i, 0, 0))
    gains = pl.BlockSpec((4, 8 * HD), lambda i: (0, i))
    return whole, columns, heads, gains


def pack_heads(me, qkv, squares, other, gains, cosine, sine):
    rows = qkv.shape[0]
    whole, columns, heads, gain = _head_specs(rows)
    return pl.pallas_call(
        _pack_body,
        grid=(2,),
        out_shape=bf(8, rows, 3 * HD),
        in_specs=[_smem(), *columns, whole, whole, gain, whole, whole],
        out_specs=heads,
        name="pack_heads",
    )(me, qkv, qkv, qkv, squares, other, gains, cosine, sine)


def _unpack_body(me, d, q, k, gains, cosine, sine, wq, wk, dv, sums):
    c, s = cosine[...], -sine[...]

    @pl.when(pl.program_id(0) == 0)
    def _():
        sums[...] = jnp.zeros_like(sums)

    lane = lax.broadcasted_iota(jnp.int32, sums.shape, 1)
    of_q, of_k = 0.0, 0.0
    for h in range(4):
        here = slice(h * HD, (h + 1) * HD)
        gq = turn(d[h, :, 0:HD].astype(F32), c, s) * _gain(gains, 0, h, me[CORE])
        gk = turn(d[h, :, HD : 2 * HD].astype(F32), c, s) * _gain(gains, 1, h, me[CORE])
        wq[:, here] = gq
        wk[:, here] = gk
        dv[:, here] = d[h, :, 2 * HD :]
        of_q += gq * q[:, here]
        of_k += gk * k[:, here]
    of_q, of_k = jnp.sum(of_q, axis=1, keepdims=True), jnp.sum(of_k, axis=1, keepdims=True)
    sums[...] += jnp.where(lane == 0, of_q, jnp.where(lane == 1, of_k, 0.0))


def unpack_heads(me, d, qkv, gains, cosine, sine):
    rows = qkv.shape[0]
    whole, columns, heads, gain = _head_specs(rows)
    return pl.pallas_call(
        _unpack_body,
        grid=(2,),
        out_shape=[_f32(rows, HALF), _f32(rows, HALF), bf(rows, HALF), _f32(rows, HD)],
        in_specs=[_smem(), heads, *columns[:2], gain, whole, whole],
        out_specs=[columns[0], columns[0], columns[0], whole],
        name="unpack_heads",
    )(me, d, qkv, qkv, gains, cosine, sine)


TILE = 128
def hidden_pairs(t, bound):
    query = t * TILE + lax.broadcasted_iota(jnp.int32, (TILE, TILE), 0)
    key = t * TILE + lax.broadcasted_iota(jnp.int32, (TILE, TILE), 1)
    hidden = key > query
    if t * TILE >= PROMPT:
        hidden = hidden | ((query >= bound) & (key < bound))
    return hidden


def tile_scores(q, k, t, bound):
    n = (t + 1) * TILE
    s = lax.dot_general(q[t * TILE : n], k[:n], **NT) * SCALE
    last = jnp.where(hidden_pairs(t, bound), -1e30, s[:, n - TILE :])
    return last if t == 0 else jnp.concatenate([s[:, : n - TILE], last], axis=1)


def _attend_body(bounds, qkv, out, exact, total):
    bound = bounds[pl.program_id(0)]
    q = qkv[:, 0, :, 0:HD].reshape(TOTAL, HD)
    k = qkv[:, 0, :, HD : 2 * HD].reshape(TOTAL, HD)
    v = qkv[:, 0, :, 2 * HD :].reshape(TOTAL, HD)
    for t in range(TOTAL // TILE):
        n = (t + 1) * TILE
        s = tile_scores(q, k, t, bound)
        top = jnp.max(s, axis=1, keepdims=True)
        p = jnp.exp(s - top)
        denom = jnp.sum(p, axis=1, keepdims=True)
        o = jnp.dot(p.astype(BF), v[:n], preferred_element_type=F32) / denom
        exact[0, t * TILE : n] = o
        total[0, t * TILE : n] = top + jnp.log(denom)
    out[:, 0] = exact[0].reshape(8, ROWS, HD).astype(BF)


def attend(bounds, qkv):
    return pl.pallas_call(
        _attend_body,
        grid=(2,),
        out_shape=[
            jax.ShapeDtypeStruct((8, 2, ROWS, HD), BF),
            jax.ShapeDtypeStruct((2, TOTAL, HD), F32),
            jax.ShapeDtypeStruct((2, TOTAL, 1), F32),
        ],
        in_specs=[
            pl.BlockSpec(memory_space=pltpu.SMEM),
            pl.BlockSpec((8, 1, ROWS, 3 * HD), lambda g: (0, g, 0, 0)),
        ],
        out_specs=[
            pl.BlockSpec((8, 1, ROWS, HD), lambda g: (0, g, 0, 0)),
            pl.BlockSpec((1, TOTAL, HD), lambda g: (g, 0, 0)),
            pl.BlockSpec((1, TOTAL, 1), lambda g: (g, 0, 0)),
        ],
        compiler_params=pltpu.CompilerParams(vmem_limit_bytes=40 * 2**20),
        cost_estimate=pl.CostEstimate(flops=900_000_000, bytes_accessed=5_000_000, transcendentals=1_500_000),
        name="attend",
    )(bounds, qkv)


def _attend_back_body(bounds, qkv, grad, exact, total, out, dk, dv, dq):
    bound = bounds[pl.program_id(0)]
    q = qkv[:, 0, :, 0:HD].reshape(TOTAL, HD)
    k = qkv[:, 0, :, HD : 2 * HD].reshape(TOTAL, HD)
    v = qkv[:, 0, :, 2 * HD :].reshape(TOTAL, HD)
    g = grad[...].reshape(TOTAL, HD)
    dk[...] = jnp.zeros_like(dk)
    dv[...] = jnp.zeros_like(dv)
    for t in range(TOTAL // TILE):
        n = (t + 1) * TILE
        here = slice(t * TILE, n)
        s = tile_scores(q, k, t, bound)
        p = jnp.exp(s - total[0, here])
        delta = jnp.sum(g[here].astype(F32) * exact[0, here], axis=1, keepdims=True)
        dp = lax.dot_general(g[here], v[:n], **NT)
        ds = (p * (dp - delta)).astype(BF)
        dq[here] = jnp.dot(ds, k[:n], preferred_element_type=F32) * SCALE
        dk[:n] += lax.dot_general(ds, q[here], **TN) * SCALE
        dv[:n] += lax.dot_general(p.astype(BF), g[here], **TN)
    out[:, 0, :, 0:HD] = dq[...].reshape(8, ROWS, HD).astype(BF)
    out[:, 0, :, HD : 2 * HD] = dk[...].reshape(8, ROWS, HD).astype(BF)
    out[:, 0, :, 2 * HD :] = dv[...].reshape(8, ROWS, HD).astype(BF)


def attend_back(bounds, qkv, grad, exact, total):
    return pl.pallas_call(
        _attend_back_body,
        grid=(2,),
        out_shape=jax.ShapeDtypeStruct((8, 2, ROWS, 3 * HD), BF),
        in_specs=[
            pl.BlockSpec(memory_space=pltpu.SMEM),
            pl.BlockSpec((8, 1, ROWS, 3 * HD), lambda g: (0, g, 0, 0)),
            pl.BlockSpec((8, ROWS, HD), lambda g: (0, g, 0)),
            pl.BlockSpec((1, TOTAL, HD), lambda g: (g, 0, 0)),
            pl.BlockSpec((1, TOTAL, 1), lambda g: (g, 0, 0)),
        ],
        out_specs=pl.BlockSpec((8, 1, ROWS, 3 * HD), lambda g: (0, g, 0, 0)),
        scratch_shapes=[pltpu.VMEM((TOTAL, HD), F32)] * 3,
        compiler_params=pltpu.CompilerParams(vmem_limit_bytes=40 * 2**20),
        cost_estimate=pl.CostEstimate(flops=2_300_000_000, bytes_accessed=8_000_000, transcendentals=1_500_000),
        name="attend_back",
    )(bounds, qkv, grad, exact, total)


def dot(a, b):
    return jnp.dot(a, b, preferred_element_type=F32)


def dot_nt(a, b):
    return lax.dot_general(a, b, **NT)


def dot_tn(a, b):
    return lax.dot_general(a, b, **TN)


def normalize_back(field, inverse, gain, grad):
    weighted = grad * gain
    return inverse * weighted - field * inverse**3 * jnp.mean(weighted * field, axis=-1, keepdims=True)


def choose_adapters(slots, down_in, down_ff, up_model, up_hidden):
    def body(slots, down_in, down_ff, up_model, up_hidden, qkv_down, gu_down, out_down, ff_down, qkv_up, out_up, ff_up, gu_up):
        core = slots[2]
        qkv_down[...] = down_in[0, :3].reshape(3 * RANK, D)
        gu_down[...] = down_in[0, 4:].reshape(2 * RANK, D)
        out_up[...] = up_model[0, 3]
        ff_up[...] = up_model[0, 4]
        qkv_up[...] = jnp.zeros_like(qkv_up)
        gu_up[...] = jnp.zeros_like(gu_up)
        for h in range(8):
            head = pl.ds(pl.multiple_of((2 * h + core) * HD, HD), HD)
            out_down[:, HD * h : HD * (h + 1)] = down_in[0, 3, :, head]
            for n in range(3):
                here = slice(n * HALF + HD * h, n * HALF + HD * (h + 1))
                qkv_up[n * RANK : (n + 1) * RANK, here] = up_model[0, n, :, head]
        for m in range(FF // 128):
            start = (2 * (m // 4) + core) * 512 + (m % 4) * 128
            units = pl.ds(pl.multiple_of(start, 128), 128)
            ff_down[:, 128 * m : 128 * (m + 1)] = down_ff[0, :, units]
            for n in range(2):
                here = slice(256 * m + 128 * n, 256 * m + 128 * (n + 1))
                gu_up[n * RANK : (n + 1) * RANK, here] = up_hidden[0, n, :, units]

    def chosen(shape):
        return pl.BlockSpec((1,) + shape[1:], lambda g, slots: (slots[g],) + (0,) * (len(shape) - 1))

    shapes = [(48, D), (32, D), (16, HALF), (16, FF), (48, 3 * HALF), (16, D), (16, D), (32, 2 * FF)]
    maps = [down_in, down_ff, up_model, up_hidden]
    return pl.pallas_call(
        body,
        out_shape=[bf(2 * r, c) for r, c in shapes],
        grid_spec=pltpu.PrefetchScalarGridSpec(
            num_scalar_prefetch=1,
            grid=(2,),
            in_specs=[chosen(m.shape) for m in maps],
            out_specs=[pl.BlockSpec(shape, lambda g, slots: (g, 0)) for shape in shapes],
        ),
        cost_estimate=pl.CostEstimate(flops=0, bytes_accessed=7_000_000, transcendentals=0),
        name="choose_adapters",
    )(slots, *maps)


def rank_gradients(lows, acts, core, name, plan, width):
    count = len(lows)

    def body(core, *refs):
        lows, acts, out = refs[:count], refs[count:-1], refs[-1]
        at = 0
        for low, act, columns, factor, starts in plan:
            picked = [lows[low][:, c : c + RANK] for c in columns]
            picked = jnp.concatenate(picked, axis=1)
            if columns[0] == columns[1]:
                picked = jnp.where(_in_group(2 * ROWS, 2 * RANK, RANK), picked, jnp.zeros_like(picked))
            if factor != 1:
                picked = picked * factor
            for start in starts(core[0]):
                right = acts[act][:, start if isinstance(start, slice) else pl.ds(pl.multiple_of(start, 128), 128)]
                n = right.shape[1]
                grad = lax.dot_general(picked, right, **TN).astype(BF)
                for b in range(n // 128):
                    block, slot = divmod(at, width // 128)
                    out[block, :, 128 * slot : 128 * (slot + 1)] = grad[:, 128 * b : 128 * (b + 1)]
                    at += 1

    return _plain(body, name, [bf(8, 2 * RANK, width)], list(lows) + list(acts), [core])[0]


def adapter_outputs(core, halves, others, shapes, name, write, done=()):
    count = len(halves)

    def body(core, *refs):
        own, other = refs[:count], refs[count : 2 * count]
        ready, outs = refs[2 * count : 2 * count + len(done)], refs[2 * count + len(done) :]

        def place(start):
            return pl.ds(pl.multiple_of(start, 128), 128)

        for side, group in ((core[0], own), (1 - core[0], other)):

            def block(n, b, t):
                return group[n][b, 0, :, 128 * t : 128 * (t + 1)].astype(F32)

            write(side, block, place, outs, *ready)

    arrays = halves + others
    size = sum(v.size * 2 for v in arrays)
    return pl.pallas_call(
        body,
        grid=(8,),
        out_shape=[jax.ShapeDtypeStruct(s, F32) for s in shapes],
        in_specs=[_smem()] + [pl.BlockSpec((8, 1) + v.shape[2:], lambda i: (0, i, 0, 0)) for v in arrays]
        + [pl.BlockSpec((1,) + v.shape[1:], lambda i: (i, 0, 0, 0)) for v in done],
        out_specs=[pl.BlockSpec((1,) + s[1:], lambda i, n=len(s): (i,) + (0,) * (n - 1)) for s in shapes],
        compiler_params=pltpu.CompilerParams(vmem_limit_bytes=40 * 2**20),
        cost_estimate=pl.CostEstimate(flops=0, bytes_accessed=size, transcendentals=0),
        name=name,
    )(core, *arrays, *done)


def write_early(side, block, place, outs):
    up_hidden, down_ff, middle = outs
    slots = EARLY // 128
    for m in range(FF // 128):
        units = place((2 * (m // 4) + side) * 512 + (m % 4) * 128)
        up_hidden[0, 0, :, units] = block(0, *divmod(m, slots))
        up_hidden[0, 1, :, units] = block(0, *divmod(32 + m, slots))
        down_ff[0, :, units] = block(0, *divmod(64 + m, slots))
    for m in range(8):
        whole, head = place(side * HALF + 128 * m), place((2 * m + side) * HD)
        for n in range(2):
            middle[0, n, :, whole] = block(0, m, slots + n)
        middle[0, 2, :, head] = block(0, m, slots + 2)
        middle[0, 3, :, whole] = block(0, m, slots + 3)
        middle[0, 4, :, whole] = block(0, *divmod(96 + m, slots))


def write_late(side, block, place, outs, middle):
    down_in, up_model = outs
    for n, m in ((4, 0), (5, 1), (3, 2)):
        down_in[0, n] = middle[0, m]
    for n in (3, 4):
        up_model[0, n] = middle[0, n]
    slots = LATE // 128
    for m in range(8):
        whole, head = place(side * HALF + 128 * m), place((2 * m + side) * HD)
        for n in range(3):
            down_in[0, n, :, whole] = block(0, *divmod(8 * n + m, slots))
            up_model[0, n, :, head] = block(0, *divmod(24 + 8 * n + m, slots))


def on_device(
    tokens,
    cotangent,
    query_matrix,
    key_matrix,
    value_matrix,
    output_matrix,
    gate_matrix,
    upward_matrix,
    down_matrix,
    gains,
    adapter_down_inputs,
    adapter_down_feedforward,
    adapter_up_model_maps,
    adapter_up_hidden_maps,
    group_adapter_index,
    continuation_lengths,
):
    core = lax.axis_index("c")
    first = core == 0
    ctx = lax.axis_index("yl") * 4 + lax.axis_index("x")
    tokens, cotangent = tokens[0], cotangent[0]

    def both(own, other):
        return jnp.where(first, jnp.stack([own, other]), jnp.stack([other, own]))

    def rows_of_both(own):
        return both(own, swap(own)).reshape(2 * own.shape[0], own.shape[1])

    plan = Gather()
    me, places = plan.me, plan.places
    keep_a, give_a = split_a(me, query_matrix, key_matrix, value_matrix)
    keep_g, give_g = split_g(me, gate_matrix, upward_matrix)
    got_a, got_g = swap(give_a), swap(give_g)
    xs_a, ys_a = parts_a(me, keep_a, got_a, output_matrix)
    xs_m, ys_g = parts_m(me, keep_g, got_g, down_matrix)
    crossed = plan.across(xs_a)
    small_a = plan.small(ys_a)
    small_g = plan.small(ys_g)
    xs_a = plan.over_xz(xs_a, crossed, small_a[1])
    crossed = plan.across(after(xs_m, small_a[2]))
    y_a = spread(me, small_a, [(0, HALF, 1)], "spread_a")
    rings_a = [[v] for v in y_a]
    for _ in range(3):
        plan.round(rings_a)
    xs_m = plan.over_xz(xs_m, crossed, rings_a[0][1], rings_a[1][1])
    w_qkv, w_out = assemble(Chunks(256, CUT_A, 4 * HALF, places, xs_a, 0, rings_a))
    small_g[3] = after(small_g[3], w_qkv)
    rings_g = [[v] for v in spread(me, small_g, [(0, FF - CUT_G // 2, 1)], "spread_g")]
    plan.round(rings_g)

    facts = jnp.concatenate([group_adapter_index[0], continuation_lengths[0]]).astype(F32)
    facts = jnp.broadcast_to(jnp.pad(facts, (0, 125))[None], (8, 128))
    pair_facts = both(facts, swap(facts))[:, 0, :2].astype(jnp.int32)
    slots = pair_facts[:, 0]
    bounds = PROMPT + pair_facts[:, 1]
    (qkv_down, gu_down, out_down, ff_down, qkv_up, out_up2, ff_up2, gu_up) = choose_adapters(
        jnp.concatenate([slots, me[:1]]),
        adapter_down_inputs,
        adapter_down_feedforward,
        adapter_up_model_maps,
        adapter_up_hidden_maps,
    )

    group_row = lax.broadcasted_iota(jnp.int32, (2 * ROWS, 1), 0) // ROWS

    def own_columns(low, count):
        group_column = lax.broadcasted_iota(jnp.int32, (1, 2 * count), 1) // count
        return jnp.where(group_row == group_column, low, jnp.zeros_like(low))

    shard = ("z", "yh")

    def spread_over(value, axes):
        return lax.all_to_all(jnp.broadcast_to(value[None], (8,) + value.shape), axes, 0, 0, tiled=True)

    place = ctx * ROWS + lax.broadcasted_iota(jnp.int32, (2, ROWS), 1)
    position = jnp.where(place >= bounds[:, None], PROMPT + place - bounds[:, None], place)
    freq = BASE ** (-(jnp.arange(HD // 2, dtype=F32) * 2.0 / HD))
    angle = position.reshape(2 * ROWS, 1).astype(F32) * freq[None]
    cosine = jnp.concatenate([jnp.cos(angle)] * 2, axis=1)
    sine = jnp.concatenate([-jnp.sin(angle), jnp.sin(angle)], axis=1)

    def whole(n):
        return lambda core: [slice(0, n)]

    def half(core):
        return [core * HALF + 128 * m for m in range(8)]

    def turns(n):
        return lambda core: [slice(256 * m + 128 * n, 256 * m + 128 * (n + 1)) for m in range(FF // 128)]

    def third(n):
        return lambda core: [slice(n * HALF, (n + 1) * HALF)]

    x2 = rows_of_both(tokens)
    qkv_low = own_columns((2.0 * dot_nt(x2, qkv_down).astype(BF)).astype(BF), 3 * RANK)
    qkv, squares = project_qkv(x2, w_qkv, qkv_low, qkv_up)
    squares = (squares, swap(squares))
    packed = pack_heads(me, qkv, *squares, gains, cosine, sine)
    heads = lax.all_to_all(packed, CTX, 0, 0, tiled=True).reshape(8, 2, ROWS, 3 * HD)
    heads = after(heads, rings_g[0][-1], rings_g[1][-1])
    plan.round(rings_g, heads)
    out_heads, exact, log_total = attend(bounds, heads)
    attended = lax.all_to_all(out_heads, CTX, 0, 0, tiled=True).reshape(8, 2 * ROWS, HD)
    keep, give, attended = project_out(me, attended, w_out, out_down)
    attn_pre, hidden, sent = combine_attention(me, keep, swap(give), tokens, gains, out_up2)

    sent = after(sent, rings_g[0][-1], rings_g[1][-1])
    plan.round(rings_g, attended)
    wg = Chunks(256, CUT_G, 2 * FF, places, xs_m, 0, rings_g)
    gu, mixed, h2, gu_low, keep, give = feed_forward(wg, sent, swap(sent), gu_down, gu_up, ff_down)
    output, sent = combine_output(me, keep, swap(give), hidden, cotangent, gains, ff_up2)

    d_gu, d_mlp, ff_grad_low, keep, give = feed_forward_back(wg, sent, swap(sent), ff_up2, ff_down, gu, gu_up)
    early = rank_gradients(
        [gu_low, ff_grad_low, d_mlp],
        [d_gu, mixed, d_mlp],
        me,
        "early_gradients",
        [
            (0, 0, (0, 2 * RANK), 1, turns(0)),
            (0, 0, (RANK, 3 * RANK), 1, turns(1)),
            (1, 1, (0, RANK), 1, whole(FF)),
            (2, 2, (D, D), 2, half),
        ],
        EARLY,
    )
    d_hidden, sent = combine_hidden(me, keep, swap(give), cotangent, attn_pre, gains, gu_down)
    sent, early = lax.optimization_barrier((sent, early))
    early = lax.all_to_all(early, CTX, 0, 0, tiled=True)

    d_out_heads, _ = project_out_back(me, sent, swap(sent), w_out, out_up2, out_down, h2, attended)
    d_out_heads = lax.all_to_all(d_out_heads, CTX, 0, 0, tiled=True)
    own = jnp.sum(early.astype(F32), axis=0).astype(BF)
    middle = jnp.sum(d_out_heads[:, 2 * ROWS :].astype(F32), axis=0).astype(BF).reshape(4, 2 * RANK, HD)
    own = jnp.concatenate([own, *middle], axis=1)
    own_slot = jnp.repeat(slots, RANK)[:, None] == lax.broadcasted_iota(jnp.int32, (1, 128), 1)
    own = jnp.concatenate([own, own_slot.astype(BF)], axis=1)
    d_out_heads, own = lax.optimization_barrier((d_out_heads, own))
    groups = spread_over(own, shard).reshape(16, RANK, EARLY + MIDDLE + 128)
    d_heads = attend_back(bounds, heads, d_out_heads, exact, log_total)
    d_heads, groups = lax.optimization_barrier((d_heads, groups))
    d_heads = lax.all_to_all(d_heads, CTX, 0, 0, tiled=True).reshape(8, 2 * ROWS, 3 * HD)

    def by_slot(groups):
        flat = groups.reshape(16, -1)
        return lax.dot_general(picker, flat, **TN).astype(BF).reshape(8 * RANK, -1)

    picker = groups[:, 0, EARLY + MIDDLE : EARLY + MIDDLE + 8]
    slot_sums = by_slot(groups[:, :, : EARLY + MIDDLE])
    d_heads = after(d_heads, slot_sums)
    early = lax.all_gather(slot_sums, CTX)
    w_q, w_k, d_v, sums = unpack_heads(me, d_heads, qkv, gains, cosine, sine)
    d_qkv, keep, give = project_qkv_back(me, (w_q, w_k), d_v, qkv, squares, (sums, swap(sums)), w_qkv, qkv_up)
    grad_tokens, low = combine_tokens(me, keep, swap(give), d_hidden, qkv_down)
    low = both(low, swap(low)).reshape(2 * ROWS, 128)

    late = rank_gradients(
        [low, qkv_low],
        [x2, d_qkv],
        me,
        "late_gradients",
        [(0, 0, (n * RANK, n * RANK), 1, half) for n in range(3)]
        + [(1, 1, (n * RANK, (3 + n) * RANK), 1, third(n)) for n in range(3)],
        LATE,
    )
    late = lax.all_to_all(late, CTX, 0, 0, tiled=True)
    late = jnp.sum(late.astype(F32), axis=0).astype(BF)
    late = spread_over(late, shard)
    early, late = lax.optimization_barrier((early, late))
    late = spread_over(by_slot(late.reshape(16, RANK, LATE)), CTX)
    shape = (8, 8, RANK, -1)
    early = early.reshape(shape)
    early_other = swap(early)
    grad_up_hidden, grad_down_ff, middle = adapter_outputs(
        me,
        [early],
        [early_other],
        [(8, 2, RANK, 2 * FF), (8, RANK, 2 * FF), (8, 5, RANK, D)],
        "early_outputs",
        write_early,
    )
    late, middle = lax.optimization_barrier((late, middle))
    late_other = swap(late)
    late, late_other = late.reshape(shape), late_other.reshape(shape)
    shapes = [(8, 6, RANK, D), (8, 5, RANK, D)]
    grad_down_in, grad_up_model = adapter_outputs(
        me, [late], [late_other], shapes, "late_outputs", write_late, [middle]
    )
    return (output[None], grad_tokens[None], grad_down_in, grad_down_ff, grad_up_model, grad_up_hidden)


def solution(mesh):
    fine = Mesh(mesh.devices.reshape(2, 4, 4, 2, 2), ALL)
    shard = ("z", "yh", "c")
    rows = P(shard, None)
    per_token = P(shard, CTX, None)
    return jax.shard_map(
        on_device,
        mesh=fine,
        in_specs=(per_token, per_token) + (rows,) * 7 + (P(),) * 5 + (rows, rows),
        out_specs=(per_token, per_token, P(), P(), P(), P()),
        check_vma=False,
    )
```

```python
import jax
import jax.numpy as jnp
from jax import lax
from jax.experimental import pallas as pl
from jax.experimental.pallas import tpu as pltpu
from jax.sharding import Mesh, PartitionSpec as P

HD = 128
PROMPT = 1024
ROWS = 144
TOTAL = 1152
D = 2048
HALF = 1024
FF = 4096
RANK = 16
SCALE = HD**-0.5
EPS = 1e-06
BASE = 500000.0
ALL = ("yl", "x", "z", "yh", "c")
CTX = ("yl", "x")
BF = jnp.bfloat16
F32 = jnp.float32
CUT_A, CUT_G = 2048, 4096
EARLY, MIDDLE, LATE = 1664, 512, 768


NT = dict(dimension_numbers=(((1,), (1,)), ((), ())), preferred_element_type=F32)
TN = dict(dimension_numbers=(((0,), (0,)), ((), ())), preferred_element_type=F32)


CORE, X, YL, YH, Z0 = 0, 1, 2, 3, 4


def _place(yl, x, z, yh, c):
    return (((yl * 4 + x) * 4 + z) * 2 + yh) * 2 + c


def _permutation(move):
    pairs = []
    for yl in range(2):
        for x in range(4):
            for z in range(4):
                for yh in range(2):
                    for c in range(2):
                        nx, ny, nz, nc = move(x, 2 * yh + yl, z, c)
                        pairs.append(
                            (_place(yl, x, z, yh, c), _place(ny % 2, nx % 4, nz % 4, (ny % 4) // 2, nc))
                        )
    return pairs


STEPS = {
    "y": _permutation(lambda x, y, z, c: (x, (y + 1 - 2 * c) % 4, z, c)),
    "z": _permutation(lambda x, y, z, c: (x, y, z + 1 - 2 * c, c)),
    "cross": _permutation(lambda x, y, z, c: (x, 3 - y, z, c)),
    "core": _permutation(lambda x, y, z, c: (x, y, z, 1 - c)),
}


def swap(value):
    return lax.ppermute(value, ALL, STEPS["core"])


class Lane:
    def __init__(self):
        self.last = None

    def send(self, value, how):
        if self.last is not None:
            value, _ = lax.optimization_barrier((value, self.last))
        self.last = lax.ppermute(value, ALL, STEPS[how])
        return self.last


def after(value, *others):
    return lax.optimization_barrier((value, *others))[0]


def _smem():
    return pl.BlockSpec(memory_space=pltpu.SMEM)


def _vmem():
    return pl.BlockSpec(memory_space=pltpu.VMEM)


def _plain(body, name, outs, ins, scalars, scratch=(), limit=48):
    size = sum(v.size * v.dtype.itemsize for v in list(ins) + list(outs))
    return pl.pallas_call(
        body,
        out_shape=outs,
        in_specs=[_smem()] * len(scalars) + [_vmem()] * len(ins),
        out_specs=[_vmem()] * len(outs),
        scratch_shapes=list(scratch),
        compiler_params=pltpu.CompilerParams(vmem_limit_bytes=limit * 2**20),
        cost_estimate=pl.CostEstimate(flops=0, bytes_accessed=size, transcendentals=0),
        name=name,
    )(*scalars, *ins)


def bf(*shape):
    return jax.ShapeDtypeStruct(shape, BF)


def split_a(core, q, k, v):
    def body(core, q, k, v, keep, give):
        for n, w in enumerate((q, k, v)):
            for h in range(8):
                here = slice(n * HALF + HD * h, n * HALF + HD * (h + 1))
                keep[:, here] = w[:, pl.ds(pl.multiple_of((2 * h + core[0]) * HD, HD), HD)]
                give[:, here] = w[:, pl.ds(pl.multiple_of((2 * h + 1 - core[0]) * HD, HD), HD)]

    return _plain(body, "split_a", [bf(HD, 3 * HALF)] * 2, [q, k, v], [core])


def split_g(core, gate, upward):
    def body(core, gate, upward, keep, give):
        for m in range(FF // 128):
            for n, w in enumerate((gate, upward)):
                here = slice(256 * m + 128 * n, 256 * m + 128 * (n + 1))
                for side, out in ((core[0], keep), (1 - core[0], give)):
                    start = (2 * (m // 4) + side) * 512 + (m % 4) * 128
                    out[:, here] = w[:, pl.ds(pl.multiple_of(start, 128), 128)]

    return _plain(body, "split_g", [bf(HD, 2 * FF)] * 2, [gate, upward], [core])


def parts_a(me, keep, got, out):
    quarter = CUT_A // 4

    def body(me, keep, got, out, xs, ys):
        for side, w in ((me[CORE], keep), (1 - me[CORE], got)):
            rows = pl.ds(pl.multiple_of(side * HD, HD), HD)
            xs[rows, :] = w[:, pl.ds(pl.multiple_of(me[X] * quarter, 128), quarter)]

            @pl.when(me[YL] == 0)
            def _():
                ys[rows, :] = w[:, 2 * HALF :]

        @pl.when(me[YL] == 1)
        def _():
            ys[:HD, :] = out[:, :HALF]
            ys[HD:, :] = out[:, HALF:]

    return _plain(body, "parts_a", [bf(256, quarter), bf(256, HALF)], [keep, got, out], [me])


def parts_m(me, keep, got, down):
    gx, dx, gy = CUT_G // 4, D // 4, FF - CUT_G // 2

    def body(me, keep, got, down, xs, ys):
        for side, w in ((me[CORE], keep), (1 - me[CORE], got)):
            rows = pl.ds(pl.multiple_of(side * HD, HD), HD)
            xs[rows, :gx] = w[:, pl.ds(pl.multiple_of(me[X] * gx, 128), gx)]
            ys[rows, :] = w[:, pl.ds(pl.multiple_of(CUT_G + me[YL] * gy, 128), gy)]
        for n in range(2):
            rows = slice(256 * n, 256 * (n + 1))
            xs[:, gx + n * dx : gx + (n + 1) * dx] = down[rows, pl.ds(pl.multiple_of(me[X] * dx, 128), dx)]

    return _plain(body, "parts_m", [bf(256, gx + 2 * dx), bf(256, gy)], [keep, got, down], [me])


def spread(me, got, pieces, name):
    def body(me, *refs):
        chunks, outs = refs[:4], refs[4:]
        for k in range(4):
            z = me[Z0 + k]
            for p, (column, width, folds) in enumerate(pieces):
                for half in range(2):

                    @pl.when(z // 2 == half)
                    def _():
                        for n in range(folds):
                            at = pl.multiple_of(((z - 2 * half) * folds + n) * 256, 256)
                            start = column + n * width
                            outs[2 * p + half][pl.ds(at, 256), :] = chunks[k][:, start : start + width]

    outs = [bf(2 * folds * 256, width) for _, width, folds in pieces for _ in range(2)]
    return _plain(body, name, outs, list(got), [me])


class Chunks:
    def __init__(self, rows, cut, width, places, xs, column, y):
        self.rows, self.cx, self.cy = rows, cut, width - cut
        self.depth = 8 * rows
        self.places = places
        self.column = column
        self.arrays = [xs] + (y[0] + y[1] if y else [])


def _y_rows(places, rows, half, j, k):
    return pl.multiple_of((2 * half + j) * 2 * rows + places[0, k] * rows, rows)


def _panel_copies(rows, width, column, xs, whole, panels):
    copies = []
    for at, k in enumerate(panels):
        for z in range(4):
            for yh in range(2):
                for n in range(rows // 256):
                    target = whole.at[pl.ds((2 * z + yh) * rows + 256 * n, 256), pl.ds(at * width, width)]
                    copies.append((xs.at[k, z, yh, :, pl.ds(column + n * width, width)], target))
    return copies


def _y_copies(places, y, whole, k, column, width):
    copies = []
    for half in range(2):
        for j in range(2):
            row = _y_rows(places, 256, half, j, k)
            copies.append((y[4 * half + k].at[pl.ds(j * 256, 256)], whole.at[pl.ds(row, 256), pl.ds(column, width)]))
    return copies


def assemble(w):
    anywhere = pl.BlockSpec(memory_space=pl.ANY)

    def body(places, *refs):
        out, out_matrix, sems = refs[9], refs[10], refs[11]
        panels = _panel_copies(256, w.cx // 4, 0, refs[0], out, range(4))
        plain = [pltpu.make_async_copy(a, b, sems.at[n]) for n, (a, b) in enumerate(panels)]
        for copy in plain:
            copy.start()

        def move(started):
            at = len(plain)
            for k in range(4):
                for half in range(2):
                    for j in range(2):
                        source = refs[1 + 4 * half + k].at[pl.ds(j * 256, 256)]
                        block = 2 * (2 * half + j) + places[0, k]

                        @pl.when(places[1, k] == 0)
                        def _():
                            row = pl.multiple_of(block * 256, 256)
                            target = out.at[pl.ds(row, 256), pl.ds(2 * HALF, HALF)]
                            copy = pltpu.make_async_copy(source, target, sems.at[at])
                            copy.wait() if started else copy.start()

                        @pl.when(places[1, k] == 1)
                        def _():
                            for n in range(2):
                                row = pl.multiple_of(block * HD, HD)
                                target = out_matrix.at[pl.ds(row, HD), pl.ds(n * HALF, HALF)]
                                copy = pltpu.make_async_copy(source.at[pl.ds(n * HD, HD)], target, sems.at[at + n])
                                copy.wait() if started else copy.start()

                        at += 2

        move(False)
        for copy in plain:
            copy.wait()
        move(True)

    return pl.pallas_call(
        body,
        out_shape=[bf(D, 3 * HALF), bf(HALF, D)],
        in_specs=[_smem()] + [anywhere] * 9,
        out_specs=[_vmem()] * 2,
        scratch_shapes=[pltpu.SemaphoreType.DMA((64,))],
        compiler_params=pltpu.CompilerParams(vmem_limit_bytes=48 * 2**20),
        cost_estimate=pl.CostEstimate(flops=0, bytes_accessed=64 * 2**20, transcendentals=0),
        name="assemble",
    )(w.places, *w.arrays)


WIDE = D + 128


def _f32(*shape):
    return jax.ShapeDtypeStruct(shape, F32)


def _pair_up(core, own, other, pair):
    pair[pl.ds(pl.multiple_of(core * ROWS, ROWS), ROWS), :] = own[...]
    pair[pl.ds(pl.multiple_of((1 - core) * ROWS, ROWS), ROWS), :] = other[...]


def _split(core, sums, keep, give):
    keep[...] = sums[pl.ds(pl.multiple_of(core * ROWS, ROWS), ROWS), :]
    give[...] = sums[pl.ds(pl.multiple_of((1 - core) * ROWS, ROWS), ROWS), :].astype(BF)


def _in_group(rows, columns, count):
    row = lax.broadcasted_iota(jnp.int32, (rows, columns), 0) >= ROWS
    column = lax.broadcasted_iota(jnp.int32, (rows, columns), 1) >= count
    return row == column


def _own_group(low, count):
    row = lax.broadcasted_iota(jnp.int32, (low.shape[0], count), 0)
    return jnp.where(row >= ROWS, low[:, count:], low[:, :count])


def _put_low(sums, low):
    count = low.shape[1]
    sums[:, D:] = jnp.zeros((sums.shape[0], WIDE - D), F32)
    sums[:, D : D + count] = low


SLOT = D
SLOTS = 4


class Stream:
    def __init__(self, w):
        self.w = w

    def gate_up(self, places, refs, n):
        xs, y, quarter = refs[0], refs[1:9], CUT_G // 4
        if n < 2:
            return n * SLOT, lambda slot: _panel_copies(256, quarter, 0, xs, slot, range(2 * n, 2 * n + 2))
        column = pl.multiple_of(CUT_G + places[1, n - 2] * SLOT, SLOT)
        return column, lambda slot: [
            copy for k in (n - 2, n) for copy in _y_copies(places, y, slot, k, 0, SLOT)
        ]

    def down(self, refs, n):
        xs, quarter = refs[0], D // 4

        def copies(slot):
            made = []
            for k in range(4):
                for block in range(4 * n, 4 * n + 4):
                    for m in range(2):
                        source = xs.at[k, block // 2, block % 2, :, pl.ds(CUT_G // 4 + m * quarter, quarter)]
                        row = (block - 4 * n) * 512 + 256 * m
                        made.append((source, slot.at[pl.ds(row, 256), pl.ds(k * quarter, quarter)]))
            return made

        return n * SLOT, copies

    def run(self, pieces, slots, sems, first, use):
        copies = []
        for n, (_, made) in enumerate(pieces):
            slot = n % SLOTS
            pairs = made(slots.at[slot])
            copies.append([pltpu.make_async_copy(a, b, sems.at[slot, m]) for m, (a, b) in enumerate(pairs)])

        def begin(n):
            if n < len(copies):
                for copy in copies[n]:
                    copy.start()

        for n in range(SLOTS - 1):
            begin(n)
        first()
        for n, (at, _) in enumerate(pieces):
            for copy in copies[n]:
                copy.wait()
            use(n, at, slots.at[n % SLOTS])
            begin(n + SLOTS - 1)

    def call(self, body, name, ins, outs, scratch=()):
        w = self.w
        anywhere = pl.BlockSpec(memory_space=pl.ANY)
        size = 6 * D * FF + sum(v.size * v.dtype.itemsize for v in ins)
        return pl.pallas_call(
            body,
            out_shape=outs,
            in_specs=[_smem()] + [anywhere] * 9 + [_vmem()] * len(ins),
            out_specs=[_vmem()] * len(outs),
            scratch_shapes=[pltpu.VMEM((SLOTS, SLOT, SLOT), BF), pltpu.SemaphoreType.DMA((SLOTS, 32)), *scratch],
            compiler_params=pltpu.CompilerParams(vmem_limit_bytes=60 * 2**20),
            cost_estimate=pl.CostEstimate(flops=4 * ROWS * D * 3 * FF, bytes_accessed=size, transcendentals=0),
            name=name,
        )(w.places, *w.arrays, *ins)


def feed_forward(w, own, other, maps_down, maps_up, ff_down):
    rows = 2 * ROWS
    stream = Stream(w)

    def body(places, *refs):
        weights, (own_ref, other_ref, down_ref, up_ref, ff_ref) = refs[:9], refs[9:14]
        gu, mixed, pair, low_ref, keep, give, slots, sems, sums = refs[14:]

        def first():
            _pair_up(places[2, 0], own_ref, other_ref, pair)
            low = 2.0 * lax.dot_general(pair[:, :D], down_ref[...], **NT).astype(BF).astype(F32)
            low_ref[...] = jnp.where(_in_group(rows, 4 * RANK, 2 * RANK), low, 0.0).astype(BF)

        def use(n, at, slot):
            tile = SLOT // 2
            if n < 4:
                for t in range(2):
                    column = at + t * tile
                    unit = column // 2
                    if not isinstance(at, int):
                        column, unit = pl.multiple_of(column, tile), pl.multiple_of(unit, tile // 2)
                    total = jnp.dot(pair[:, :D], slot[:, t * tile : (t + 1) * tile], preferred_element_type=F32)
                    total = total + jnp.dot(low_ref[...], up_ref[:, pl.ds(column, tile)], preferred_element_type=F32)
                    gu[:, pl.ds(column, tile)] = total.astype(BF)
                    for m in range(tile // 256):
                        g, u = total[:, 256 * m : 256 * m + 128], total[:, 256 * m + 128 : 256 * m + 256]
                        mixed[:, pl.ds(unit + 128 * m, 128)] = (g * jax.nn.sigmoid(g) * u).astype(BF)
                return
            left = mixed[:, at : at + SLOT]
            for t in range(2):
                here = slice(t * tile, (t + 1) * tile)
                part = jnp.dot(left, slot[:, here], preferred_element_type=F32)
                if n == 4:
                    sums[:, here] = part
                else:
                    sums[:, here] += part

        pieces = [stream.gate_up(places, weights, n) for n in range(4)] + [stream.down(weights, n) for n in range(2)]
        stream.run(pieces, slots, sems, first, use)
        _put_low(sums, _own_group(lax.dot_general(mixed[...], ff_ref[...], **NT), RANK))
        _split(places[2, 0], sums, keep, give)

    outs = [bf(rows, 2 * FF), bf(rows, FF), bf(rows, WIDE), bf(rows, 4 * RANK), _f32(ROWS, WIDE), bf(ROWS, WIDE)]
    ins = [own, other, maps_down, maps_up, ff_down]
    return stream.call(body, "feed_forward", ins, outs, [pltpu.VMEM((rows, WIDE), F32)])


def feed_forward_back(w, own, other, ff_up, ff_down, gu, maps_up):
    rows = 2 * ROWS
    stream = Stream(w)

    def body(places, *refs):
        weights, (own_ref, other_ref, ff_up_ref, ff_down_ref, gu_ref, up_ref) = refs[:9], refs[9:15]
        out, pair, low_ref, keep, give, slots, sems, sums, lows = refs[15:]

        def first():
            _pair_up(places[2, 0], own_ref, other_ref, pair)
            low = 2.0 * lax.dot_general(pair[:, :D], ff_up_ref[...], **NT)
            low_ref[...] = jnp.where(_in_group(rows, 2 * RANK, RANK), low, 0.0).astype(BF)

        def use(n, at, slot):
            tile = SLOT // 2
            if n < 2:
                for t in range(2):
                    units = slice(at + t * tile, at + (t + 1) * tile)
                    d_mixed = lax.dot_general(pair[:, :D], slot[t * tile : (t + 1) * tile, :], **NT)
                    d_mixed = d_mixed + jnp.dot(low_ref[...], ff_down_ref[:, units], preferred_element_type=F32)
                    for m in range(tile // 128):
                        column = 2 * (at + t * tile) + 256 * m
                        g = gu_ref[:, column : column + 128].astype(F32)
                        u = gu_ref[:, column + 128 : column + 256].astype(F32)
                        d = d_mixed[:, 128 * m : 128 * (m + 1)]
                        s = jax.nn.sigmoid(g)
                        out[:, column : column + 128] = (d * u * s * (1.0 + g * (1.0 - s))).astype(BF)
                        out[:, column + 128 : column + 256] = (d * g * s).astype(BF)
                return
            left = out[:, pl.ds(at, SLOT)]
            low = lax.dot_general(left, up_ref[:, pl.ds(at, SLOT)], **NT)
            for t in range(2):
                here = slice(t * tile, (t + 1) * tile)
                part = lax.dot_general(left, slot[here, :], **NT)
                if n == 2:
                    sums[:, here] = part
                else:
                    sums[:, here] += part
            if n == 2:
                lows[...] = low
            else:
                lows[...] += low

        pieces = [stream.down(weights, n) for n in range(2)] + [stream.gate_up(places, weights, n) for n in range(4)]
        stream.run(pieces, slots, sems, first, use)
        _put_low(sums, _own_group(lows[...], 2 * RANK))
        _split(places[2, 0], sums, keep, give)

    outs = [bf(rows, 2 * FF), bf(rows, WIDE), bf(rows, 2 * RANK), _f32(ROWS, WIDE), bf(ROWS, WIDE)]
    ins = [own, other, ff_up, ff_down, gu, maps_up]
    scratch = [pltpu.VMEM((rows, WIDE), F32), pltpu.VMEM((rows, 4 * RANK), F32)]
    return stream.call(body, "feed_forward_back", ins, outs, scratch)


def project_qkv(x, w, low, maps_up):
    rows, tile = x.shape[0], 512

    def body(x, w, low, up, out, squares):
        i = pl.program_id(0)

        @pl.when(i == 0)
        def _():
            squares[...] = jnp.zeros_like(squares)

        total = jnp.dot(x[...], w[...], preferred_element_type=F32)
        total = total + jnp.dot(low[...], up[...], preferred_element_type=F32)
        out[...] = total
        here = lax.broadcasted_iota(jnp.int32, squares.shape, 1) == i // 2
        squares[...] += jnp.where(here, jnp.sum(total * total, axis=1, keepdims=True), 0.0)

    whole = lambda v: pl.BlockSpec(v.shape, lambda i: (0, 0))
    column = lambda n: pl.BlockSpec((n, tile), lambda i: (0, i))
    return pl.pallas_call(
        body,
        grid=(3 * HALF // tile,),
        out_shape=[_f32(rows, 3 * HALF), _f32(rows, 128)],
        in_specs=[whole(x), column(D), whole(low), column(maps_up.shape[0])],
        out_specs=[column(rows), pl.BlockSpec((rows, 128), lambda i: (0, 0))],
        compiler_params=pltpu.CompilerParams(vmem_limit_bytes=32 * 2**20),
        cost_estimate=pl.CostEstimate(flops=2 * rows * D * 3 * HALF, bytes_accessed=18_000_000, transcendentals=0),
        name="project_qkv",
    )(x, w, low, maps_up)


def project_out(me, heads, w, maps_down):
    rows = 2 * ROWS

    def body(me, heads, w, down, keep, give, flat, sums):
        flat[...] = jnp.concatenate([heads[h] for h in range(8)], axis=1)
        for n in range(0, D, 512):
            sums[:, n : n + 512] = jnp.dot(flat[...], w[:, n : n + 512], preferred_element_type=F32)
        _put_low(sums, _own_group(lax.dot_general(flat[...], down[...], **NT), RANK))
        _split(me[CORE], sums, keep, give)

    outs = [_f32(ROWS, WIDE), bf(ROWS, WIDE), bf(rows, HALF)]
    return _plain(body, "project_out", outs, [heads, w, maps_down], [me], [pltpu.VMEM((rows, WIDE), F32)])


def _low_and_sum(me, keep, got, maps, count, factor):
    total = keep[...] + got[...].astype(F32)
    low = (factor * total[:, D : D + count]).astype(BF)
    start = pl.multiple_of(me[CORE] * count, count)
    return total[:, :D], low, jnp.dot(low, maps[pl.ds(start, count), :], preferred_element_type=F32)


def _send(out, value, low):
    out[:, :D] = value.astype(BF)
    out[:, D:] = jnp.zeros((ROWS, WIDE - D), BF)
    out[:, D : D + low.shape[1]] = low


def _inverse(field):
    return lax.rsqrt(jnp.mean(field * field, axis=1, keepdims=True) + EPS)


def combine_attention(me, keep, got, tokens, gains, maps_up):
    def body(me, keep, got, tokens, gains, up, pre, hidden, out):
        total, low, raised = _low_and_sum(me, keep, got, up, RANK, 1.0)
        field = total + 2.0 * raised
        pre[...] = field
        value = tokens[...].astype(F32) + field * _inverse(field) * gains[2:3]
        hidden[...] = value
        _send(out, value, low)

    outs = [_f32(ROWS, D), _f32(ROWS, D), bf(ROWS, WIDE)]
    return _plain(body, "combine_attention", outs, [keep, got, tokens, gains, maps_up], [me])


def combine_output(me, keep, got, hidden, cotangent, gains, maps_up):
    def body(me, keep, got, hidden, cotangent, gains, up, output, out):
        total, low, raised = _low_and_sum(me, keep, got, up, RANK, 1.0)
        field = total + 2.0 * raised
        inverse = _inverse(field)
        output[...] = (hidden[...] + field * inverse * gains[3:4]).astype(BF)
        _send(out, normalize_back(field, inverse, gains[3:4], cotangent[...].astype(F32)), low)

    outs = [bf(ROWS, D), bf(ROWS, WIDE)]
    return _plain(body, "combine_output", outs, [keep, got, hidden, cotangent, gains, maps_up], [me])


def combine_hidden(me, keep, got, cotangent, pre, gains, maps_down):
    def body(me, keep, got, cotangent, pre, gains, down, hidden, out):
        total, low, lowered = _low_and_sum(me, keep, got, down, 2 * RANK, 2.0)
        value = cotangent[...].astype(F32) + total + lowered
        hidden[...] = value
        field = pre[...]
        _send(out, normalize_back(field, _inverse(field), gains[2:3], value), low)

    outs = [_f32(ROWS, D), bf(ROWS, WIDE)]
    return _plain(body, "combine_hidden", outs, [keep, got, cotangent, pre, gains, maps_down], [me])


def combine_tokens(me, keep, got, hidden, maps_down):
    def body(me, keep, got, hidden, down, out, low_out):
        total, low, lowered = _low_and_sum(me, keep, got, down, 3 * RANK, 2.0)
        out[...] = (hidden[...] + total + lowered).astype(BF)
        low_out[...] = jnp.zeros_like(low_out)
        low_out[:, : 3 * RANK] = low

    outs = [bf(ROWS, D), bf(ROWS, 128)]
    return _plain(body, "combine_tokens", outs, [keep, got, hidden, maps_down], [me])


def project_out_back(me, own, other, w, maps_up, maps_down, h2, attended):
    rows = 2 * ROWS

    def body(me, own, other, w, up, down, h2, attended, out, low_ref, pair):
        _pair_up(me[CORE], own, other, pair)
        low = 2.0 * lax.dot_general(pair[:, :D], up[...], **NT)
        low_ref[...] = jnp.where(_in_group(rows, 2 * RANK, RANK), low, 0.0).astype(BF)
        for n in range(0, HALF, 512):
            total = lax.dot_general(pair[:, :D], w[n : n + 512, :], **NT)
            total = total + jnp.dot(low_ref[...], down[:, n : n + 512], preferred_element_type=F32)
            for h in range(4):
                out[n // HD + h, :rows] = total[:, h * HD : (h + 1) * HD].astype(BF)

        def shared(columns, start):
            picked = jnp.concatenate([columns[:, start : start + RANK]] * 2, axis=1)
            return jnp.where(_in_group(rows, 2 * RANK, RANK), picked, jnp.zeros_like(picked))

        here = pl.ds(pl.multiple_of(me[CORE] * HALF, HALF), HALF)
        pieces = [
            (shared(pair, D), h2[:, here]),
            (shared(pair, D + RANK), h2[:, here]),
            (low_ref[...], attended[...]),
            (2 * shared(h2, D), pair[:, here]),
        ]
        for p, (picked, act) in enumerate(pieces):
            grad = lax.dot_general(picked, act, **TN).astype(BF)
            at = slice(rows + 2 * RANK * p, rows + 2 * RANK * (p + 1))
            for b in range(8):
                out[b, at] = grad[:, HD * b : HD * (b + 1)]

    outs = [bf(8, rows + 8 * RANK, HD), bf(rows, 2 * RANK)]
    ins = [own, other, w, maps_up, maps_down, h2, attended]
    return _plain(body, "project_out_back", outs, ins, [me], [pltpu.VMEM((rows, WIDE), BF)])


def project_qkv_back(me, weighted, value_grad, qkv, squares, sums, w, maps_up):
    rows, tile = 2 * ROWS, 512

    def body(me, wq, wk, dv, q, k, sq, sq_other, su, su_other, w, up, d_qkv, keep, give, acc):
        i = pl.program_id(0)

        @pl.when(i == 0)
        def _():
            inverse = lax.rsqrt((sq[...] + sq_other[...]) / D + EPS)
            mean = (su[...] + su_other[...]) / D
            for n, (weight, field) in enumerate(((wq, q), (wk, k))):
                r, m = inverse[:, n : n + 1], mean[:, n : n + 1]
                d_qkv[:, n * HALF : (n + 1) * HALF] = (r * weight[...] - field[...] * (r * r * r * m)).astype(BF)
            d_qkv[:, 2 * HALF :] = dv[...]
            _put_low(acc, _own_group(lax.dot_general(d_qkv[...], up[...], **NT), 3 * RANK))

        acc[:, pl.ds(pl.multiple_of(i * tile, tile), tile)] = lax.dot_general(d_qkv[...], w[...], **NT)

        @pl.when(i == D // tile - 1)
        def _():
            _split(me[CORE], acc, keep, give)

    once = lambda v: pl.BlockSpec(v.shape, lambda i: (0, 0), pipeline_mode=pl.Buffered(1))
    third = lambda n: pl.BlockSpec((rows, HALF), lambda i: (0, n), pipeline_mode=pl.Buffered(1))
    ins = [*weighted, value_grad]
    return pl.pallas_call(
        body,
        grid=(D // tile,),
        out_shape=[bf(rows, 3 * HALF), _f32(ROWS, WIDE), bf(ROWS, WIDE)],
        in_specs=[_smem()]
        + [once(v) for v in ins]
        + [third(0), third(1)]
        + [once(v) for v in (*squares, *sums)]
        + [pl.BlockSpec((tile, 3 * HALF), lambda i: (i, 0)), once(maps_up)],
        out_specs=[once(jax.ShapeDtypeStruct((rows, 3 * HALF), BF))] + [once(_f32(ROWS, WIDE))] * 2,
        scratch_shapes=[pltpu.VMEM((rows, WIDE), F32)],
        compiler_params=pltpu.CompilerParams(vmem_limit_bytes=48 * 2**20),
        cost_estimate=pl.CostEstimate(flops=2 * rows * D * 3 * HALF, bytes_accessed=22_000_000, transcendentals=0),
        name="project_qkv_back",
    )(me, *ins, qkv, qkv, *squares, *sums, w, maps_up)


class Gather:
    def __init__(self):
        core = lax.axis_index("c")
        x, z = lax.axis_index("x"), lax.axis_index("z")
        yl, yh = lax.axis_index("yl"), lax.axis_index("yh")
        y = 2 * yh + yl
        sign = 1 - 2 * core
        ys = [lax.rem(y - sign * k + 8, 4) for k in range(4)]
        zs = [lax.rem(z - sign * k + 8, 4) for k in range(4)]
        self.yh = yh
        self.me = jnp.stack([core, x, yl, yh] + zs).astype(jnp.int32)
        self.places = jnp.stack([jnp.stack([v // 2 for v in ys]), jnp.stack([v % 2 for v in ys]), self.me[:4]]).astype(jnp.int32)
        self.lanes = {"y0": Lane(), "y1": Lane(), "z": Lane(), "cross": Lane()}

    def across(self, own):
        return self.lanes["cross"].send(own, "cross")

    def over_xz(self, own, other, *before):
        other = after(other, *before)
        both = jnp.where(self.yh == 0, jnp.stack([own, other]), jnp.stack([other, own]))
        return lax.all_gather(both, ("x", "z")).reshape(4, 4, 2, *own.shape)

    def small(self, own):
        got = [own]
        for _ in range(3):
            got.append(self.lanes["z"].send(got[-1], "z"))
        return got

    def round(self, rings, *before):
        for n in range(2):
            value = after(rings[n][-1], *before) if before else rings[n][-1]
            rings[n].append(self.lanes["y%d" % n].send(value, "y"))


def turn(value, cosine, sine):
    return value * cosine + pltpu.roll(value, 64, 1) * sine


def _gain(gains, n, h, core):
    return gains[n : n + 1, pl.ds(pl.multiple_of((2 * h + core) * HD, HD), HD)]


def _pack_body(me, q, k, v, squares, other, gains, cosine, sine, out):
    scales = lax.rsqrt((squares[...] + other[...]) / D + EPS)
    c, s = cosine[...], sine[...]
    for h in range(4):
        here = slice(h * HD, (h + 1) * HD)
        out[h, :, 0:HD] = turn(q[:, here] * scales[:, 0:1] * _gain(gains, 0, h, me[CORE]), c, s).astype(BF)
        out[h, :, HD : 2 * HD] = turn(k[:, here] * scales[:, 1:2] * _gain(gains, 1, h, me[CORE]), c, s).astype(BF)
        out[h, :, 2 * HD :] = v[:, here].astype(BF)


def _head_specs(rows):
    whole = pl.BlockSpec((rows, HD), lambda i: (0, 0))
    columns = [pl.BlockSpec((rows, 4 * HD), lambda i, n=n: (0, 2 * n + i)) for n in range(3)]
    heads = pl.BlockSpec((4, rows, 3 * HD), lambda i: (i, 0, 0))
    gains = pl.BlockSpec((4, 8 * HD), lambda i: (0, i))
    return whole, columns, heads, gains


def pack_heads(me, qkv, squares, other, gains, cosine, sine):
    rows = qkv.shape[0]
    whole, columns, heads, gain = _head_specs(rows)
    return pl.pallas_call(
        _pack_body,
        grid=(2,),
        out_shape=bf(8, rows, 3 * HD),
        in_specs=[_smem(), *columns, whole, whole, gain, whole, whole],
        out_specs=heads,
        name="pack_heads",
    )(me, qkv, qkv, qkv, squares, other, gains, cosine, sine)


def _unpack_body(me, d, q, k, gains, cosine, sine, wq, wk, dv, sums):
    c, s = cosine[...], -sine[...]

    @pl.when(pl.program_id(0) == 0)
    def _():
        sums[...] = jnp.zeros_like(sums)

    lane = lax.broadcasted_iota(jnp.int32, sums.shape, 1)
    of_q, of_k = 0.0, 0.0
    for h in range(4):
        here = slice(h * HD, (h + 1) * HD)
        gq = turn(d[h, :, 0:HD].astype(F32), c, s) * _gain(gains, 0, h, me[CORE])
        gk = turn(d[h, :, HD : 2 * HD].astype(F32), c, s) * _gain(gains, 1, h, me[CORE])
        wq[:, here] = gq
        wk[:, here] = gk
        dv[:, here] = d[h, :, 2 * HD :]
        of_q += gq * q[:, here]
        of_k += gk * k[:, here]
    of_q, of_k = jnp.sum(of_q, axis=1, keepdims=True), jnp.sum(of_k, axis=1, keepdims=True)
    sums[...] += jnp.where(lane == 0, of_q, jnp.where(lane == 1, of_k, 0.0))


def unpack_heads(me, d, qkv, gains, cosine, sine):
    rows = qkv.shape[0]
    whole, columns, heads, gain = _head_specs(rows)
    return pl.pallas_call(
        _unpack_body,
        grid=(2,),
        out_shape=[_f32(rows, HALF), _f32(rows, HALF), bf(rows, HALF), _f32(rows, HD)],
        in_specs=[_smem(), heads, *columns[:2], gain, whole, whole],
        out_specs=[columns[0], columns[0], columns[0], whole],
        name="unpack_heads",
    )(me, d, qkv, qkv, gains, cosine, sine)


TILE = 128
def hidden_pairs(t, bound):
    query = t * TILE + lax.broadcasted_iota(jnp.int32, (TILE, TILE), 0)
    key = t * TILE + lax.broadcasted_iota(jnp.int32, (TILE, TILE), 1)
    hidden = key > query
    if t * TILE >= PROMPT:
        hidden = hidden | ((query >= bound) & (key < bound))
    return hidden


def tile_scores(q, k, t, bound):
    n = (t + 1) * TILE
    s = lax.dot_general(q[t * TILE : n], k[:n], **NT) * SCALE
    last = jnp.where(hidden_pairs(t, bound), -1e30, s[:, n - TILE :])
    return last if t == 0 else jnp.concatenate([s[:, : n - TILE], last], axis=1)


def _attend_body(bounds, qkv, out, exact, total):
    bound = bounds[pl.program_id(0)]
    q = qkv[:, 0, :, 0:HD].reshape(TOTAL, HD)
    k = qkv[:, 0, :, HD : 2 * HD].reshape(TOTAL, HD)
    v = qkv[:, 0, :, 2 * HD :].reshape(TOTAL, HD)
    for t in range(TOTAL // TILE):
        n = (t + 1) * TILE
        s = tile_scores(q, k, t, bound)
        top = jnp.max(s, axis=1, keepdims=True)
        p = jnp.exp(s - top)
        denom = jnp.sum(p, axis=1, keepdims=True)
        o = jnp.dot(p.astype(BF), v[:n], preferred_element_type=F32) / denom
        exact[0, t * TILE : n] = o
        total[0, t * TILE : n] = top + jnp.log(denom)
    out[:, 0] = exact[0].reshape(8, ROWS, HD).astype(BF)


def attend(bounds, qkv):
    return pl.pallas_call(
        _attend_body,
        grid=(2,),
        out_shape=[
            jax.ShapeDtypeStruct((8, 2, ROWS, HD), BF),
            jax.ShapeDtypeStruct((2, TOTAL, HD), F32),
            jax.ShapeDtypeStruct((2, TOTAL, 1), F32),
        ],
        in_specs=[
            pl.BlockSpec(memory_space=pltpu.SMEM),
            pl.BlockSpec((8, 1, ROWS, 3 * HD), lambda g: (0, g, 0, 0)),
        ],
        out_specs=[
            pl.BlockSpec((8, 1, ROWS, HD), lambda g: (0, g, 0, 0)),
            pl.BlockSpec((1, TOTAL, HD), lambda g: (g, 0, 0)),
            pl.BlockSpec((1, TOTAL, 1), lambda g: (g, 0, 0)),
        ],
        compiler_params=pltpu.CompilerParams(vmem_limit_bytes=40 * 2**20),
        cost_estimate=pl.CostEstimate(flops=900_000_000, bytes_accessed=5_000_000, transcendentals=1_500_000),
        name="attend",
    )(bounds, qkv)


def _attend_back_body(bounds, qkv, grad, exact, total, out, dk, dv, dq):
    bound = bounds[pl.program_id(0)]
    q = qkv[:, 0, :, 0:HD].reshape(TOTAL, HD)
    k = qkv[:, 0, :, HD : 2 * HD].reshape(TOTAL, HD)
    v = qkv[:, 0, :, 2 * HD :].reshape(TOTAL, HD)
    g = grad[...].reshape(TOTAL, HD)
    dk[...] = jnp.zeros_like(dk)
    dv[...] = jnp.zeros_like(dv)
    for t in range(TOTAL // TILE):
        n = (t + 1) * TILE
        here = slice(t * TILE, n)
        s = tile_scores(q, k, t, bound)
        p = jnp.exp(s - total[0, here])
        delta = jnp.sum(g[here].astype(F32) * exact[0, here], axis=1, keepdims=True)
        dp = lax.dot_general(g[here], v[:n], **NT)
        ds = (p * (dp - delta)).astype(BF)
        dq[here] = jnp.dot(ds, k[:n], preferred_element_type=F32) * SCALE
        dk[:n] += lax.dot_general(ds, q[here], **TN) * SCALE
        dv[:n] += lax.dot_general(p.astype(BF), g[here], **TN)
    out[:, 0, :, 0:HD] = dq[...].reshape(8, ROWS, HD).astype(BF)
    out[:, 0, :, HD : 2 * HD] = dk[...].reshape(8, ROWS, HD).astype(BF)
    out[:, 0, :, 2 * HD :] = dv[...].reshape(8, ROWS, HD).astype(BF)


def attend_back(bounds, qkv, grad, exact, total):
    return pl.pallas_call(
        _attend_back_body,
        grid=(2,),
        out_shape=jax.ShapeDtypeStruct((8, 2, ROWS, 3 * HD), BF),
        in_specs=[
            pl.BlockSpec(memory_space=pltpu.SMEM),
            pl.BlockSpec((8, 1, ROWS, 3 * HD), lambda g: (0, g, 0, 0)),
            pl.BlockSpec((8, ROWS, HD), lambda g: (0, g, 0)),
            pl.BlockSpec((1, TOTAL, HD), lambda g: (g, 0, 0)),
            pl.BlockSpec((1, TOTAL, 1), lambda g: (g, 0, 0)),
        ],
        out_specs=pl.BlockSpec((8, 1, ROWS, 3 * HD), lambda g: (0, g, 0, 0)),
        scratch_shapes=[pltpu.VMEM((TOTAL, HD), F32)] * 3,
        compiler_params=pltpu.CompilerParams(vmem_limit_bytes=40 * 2**20),
        cost_estimate=pl.CostEstimate(flops=2_300_000_000, bytes_accessed=8_000_000, transcendentals=1_500_000),
        name="attend_back",
    )(bounds, qkv, grad, exact, total)


def dot(a, b):
    return jnp.dot(a, b, preferred_element_type=F32)


def dot_nt(a, b):
    return lax.dot_general(a, b, **NT)


def dot_tn(a, b):
    return lax.dot_general(a, b, **TN)


def normalize_back(field, inverse, gain, grad):
    weighted = grad * gain
    return inverse * weighted - field * inverse**3 * jnp.mean(weighted * field, axis=-1, keepdims=True)


def choose_adapters(slots, down_in, down_ff, up_model, up_hidden):
    def body(slots, down_in, down_ff, up_model, up_hidden, qkv_down, gu_down, out_down, ff_down, qkv_up, out_up, ff_up, gu_up):
        core = slots[2]
        qkv_down[...] = down_in[0, :3].reshape(3 * RANK, D)
        gu_down[...] = down_in[0, 4:].reshape(2 * RANK, D)
        out_up[...] = up_model[0, 3]
        ff_up[...] = up_model[0, 4]
        qkv_up[...] = jnp.zeros_like(qkv_up)
        gu_up[...] = jnp.zeros_like(gu_up)
        for h in range(8):
            head = pl.ds(pl.multiple_of((2 * h + core) * HD, HD), HD)
            out_down[:, HD * h : HD * (h + 1)] = down_in[0, 3, :, head]
            for n in range(3):
                here = slice(n * HALF + HD * h, n * HALF + HD * (h + 1))
                qkv_up[n * RANK : (n + 1) * RANK, here] = up_model[0, n, :, head]
        for m in range(FF // 128):
            start = (2 * (m // 4) + core) * 512 + (m % 4) * 128
            units = pl.ds(pl.multiple_of(start, 128), 128)
            ff_down[:, 128 * m : 128 * (m + 1)] = down_ff[0, :, units]
            for n in range(2):
                here = slice(256 * m + 128 * n, 256 * m + 128 * (n + 1))
                gu_up[n * RANK : (n + 1) * RANK, here] = up_hidden[0, n, :, units]

    def chosen(shape):
        return pl.BlockSpec((1,) + shape[1:], lambda g, slots: (slots[g],) + (0,) * (len(shape) - 1))

    shapes = [(48, D), (32, D), (16, HALF), (16, FF), (48, 3 * HALF), (16, D), (16, D), (32, 2 * FF)]
    maps = [down_in, down_ff, up_model, up_hidden]
    return pl.pallas_call(
        body,
        out_shape=[bf(2 * r, c) for r, c in shapes],
        grid_spec=pltpu.PrefetchScalarGridSpec(
            num_scalar_prefetch=1,
            grid=(2,),
            in_specs=[chosen(m.shape) for m in maps],
            out_specs=[pl.BlockSpec(shape, lambda g, slots: (g, 0)) for shape in shapes],
        ),
        cost_estimate=pl.CostEstimate(flops=0, bytes_accessed=7_000_000, transcendentals=0),
        name="choose_adapters",
    )(slots, *maps)


def rank_gradients(lows, acts, core, name, plan, width):
    count = len(lows)

    def body(core, *refs):
        lows, acts, out = refs[:count], refs[count:-1], refs[-1]
        at = 0
        for low, act, columns, factor, starts in plan:
            picked = [lows[low][:, c : c + RANK] for c in columns]
            picked = jnp.concatenate(picked, axis=1)
            if columns[0] == columns[1]:
                picked = jnp.where(_in_group(2 * ROWS, 2 * RANK, RANK), picked, jnp.zeros_like(picked))
            if factor != 1:
                picked = picked * factor
            for start in starts(core[0]):
                right = acts[act][:, start if isinstance(start, slice) else pl.ds(pl.multiple_of(start, 128), 128)]
                n = right.shape[1]
                grad = lax.dot_general(picked, right, **TN).astype(BF)
                for b in range(n // 128):
                    block, slot = divmod(at, width // 128)
                    out[block, :, 128 * slot : 128 * (slot + 1)] = grad[:, 128 * b : 128 * (b + 1)]
                    at += 1

    return _plain(body, name, [bf(8, 2 * RANK, width)], list(lows) + list(acts), [core])[0]


def adapter_outputs(core, halves, others, shapes, name, write, done=()):
    count = len(halves)

    def body(core, *refs):
        own, other = refs[:count], refs[count : 2 * count]
        ready, outs = refs[2 * count : 2 * count + len(done)], refs[2 * count + len(done) :]

        def place(start):
            return pl.ds(pl.multiple_of(start, 128), 128)

        for side, group in ((core[0], own), (1 - core[0], other)):

            def block(n, b, t):
                return group[n][b, 0, :, 128 * t : 128 * (t + 1)].astype(F32)

            write(side, block, place, outs, *ready)

    arrays = halves + others
    size = sum(v.size * 2 for v in arrays)
    return pl.pallas_call(
        body,
        grid=(8,),
        out_shape=[jax.ShapeDtypeStruct(s, F32) for s in shapes],
        in_specs=[_smem()] + [pl.BlockSpec((8, 1) + v.shape[2:], lambda i: (0, i, 0, 0)) for v in arrays]
        + [pl.BlockSpec((1,) + v.shape[1:], lambda i: (i, 0, 0, 0)) for v in done],
        out_specs=[pl.BlockSpec((1,) + s[1:], lambda i, n=len(s): (i,) + (0,) * (n - 1)) for s in shapes],
        compiler_params=pltpu.CompilerParams(vmem_limit_bytes=40 * 2**20),
        cost_estimate=pl.CostEstimate(flops=0, bytes_accessed=size, transcendentals=0),
        name=name,
    )(core, *arrays, *done)


def write_early(side, block, place, outs):
    up_hidden, down_ff, middle = outs
    slots = EARLY // 128
    for m in range(FF // 128):
        units = place((2 * (m // 4) + side) * 512 + (m % 4) * 128)
        up_hidden[0, 0, :, units] = block(0, *divmod(m, slots))
        up_hidden[0, 1, :, units] = block(0, *divmod(32 + m, slots))
        down_ff[0, :, units] = block(0, *divmod(64 + m, slots))
    for m in range(8):
        whole, head = place(side * HALF + 128 * m), place((2 * m + side) * HD)
        for n in range(2):
            middle[0, n, :, whole] = block(0, m, slots + n)
        middle[0, 2, :, head] = block(0, m, slots + 2)
        middle[0, 3, :, whole] = block(0, m, slots + 3)
        middle[0, 4, :, whole] = block(0, *divmod(96 + m, slots))


def write_late(side, block, place, outs, middle):
    down_in, up_model = outs
    for n, m in ((4, 0), (5, 1), (3, 2)):
        down_in[0, n] = middle[0, m]
    for n in (3, 4):
        up_model[0, n] = middle[0, n]
    slots = LATE // 128
    for m in range(8):
        whole, head = place(side * HALF + 128 * m), place((2 * m + side) * HD)
        for n in range(3):
            down_in[0, n, :, whole] = block(0, *divmod(8 * n + m, slots))
            up_model[0, n, :, head] = block(0, *divmod(24 + 8 * n + m, slots))


def on_device(
    tokens,
    cotangent,
    query_matrix,
    key_matrix,
    value_matrix,
    output_matrix,
    gate_matrix,
    upward_matrix,
    down_matrix,
    gains,
    adapter_down_inputs,
    adapter_down_feedforward,
    adapter_up_model_maps,
    adapter_up_hidden_maps,
    group_adapter_index,
    continuation_lengths,
):
    core = lax.axis_index("c")
    first = core == 0
    ctx = lax.axis_index("yl") * 4 + lax.axis_index("x")
    tokens, cotangent = tokens[0], cotangent[0]

    def both(own, other):
        return jnp.where(first, jnp.stack([own, other]), jnp.stack([other, own]))

    def rows_of_both(own):
        return both(own, swap(own)).reshape(2 * own.shape[0], own.shape[1])

    plan = Gather()
    me, places = plan.me, plan.places
    keep_a, give_a = split_a(me, query_matrix, key_matrix, value_matrix)
    keep_g, give_g = split_g(me, gate_matrix, upward_matrix)
    got_a, got_g = swap(give_a), swap(give_g)
    xs_a, ys_a = parts_a(me, keep_a, got_a, output_matrix)
    xs_m, ys_g = parts_m(me, keep_g, got_g, down_matrix)
    crossed = plan.across(xs_a)
    small_a = plan.small(ys_a)
    small_g = plan.small(ys_g)
    xs_a = plan.over_xz(xs_a, crossed, small_a[1])
    crossed = plan.across(after(xs_m, small_a[2]))
    y_a = spread(me, small_a, [(0, HALF, 1)], "spread_a")
    rings_a = [[v] for v in y_a]
    for _ in range(3):
        plan.round(rings_a)
    xs_m = plan.over_xz(xs_m, crossed, rings_a[0][1], rings_a[1][1])
    w_qkv, w_out = assemble(Chunks(256, CUT_A, 4 * HALF, places, xs_a, 0, rings_a))
    small_g[3] = after(small_g[3], w_qkv)
    rings_g = [[v] for v in spread(me, small_g, [(0, FF - CUT_G // 2, 1)], "spread_g")]
    plan.round(rings_g)

    facts = jnp.concatenate([group_adapter_index[0], continuation_lengths[0]]).astype(F32)
    facts = jnp.broadcast_to(jnp.pad(facts, (0, 125))[None], (8, 128))
    pair_facts = both(facts, swap(facts))[:, 0, :2].astype(jnp.int32)
    slots = pair_facts[:, 0]
    bounds = PROMPT + pair_facts[:, 1]
    (qkv_down, gu_down, out_down, ff_down, qkv_up, out_up2, ff_up2, gu_up) = choose_adapters(
        jnp.concatenate([slots, me[:1]]),
        adapter_down_inputs,
        adapter_down_feedforward,
        adapter_up_model_maps,
        adapter_up_hidden_maps,
    )

    group_row = lax.broadcasted_iota(jnp.int32, (2 * ROWS, 1), 0) // ROWS

    def own_columns(low, count):
        group_column = lax.broadcasted_iota(jnp.int32, (1, 2 * count), 1) // count
        return jnp.where(group_row == group_column, low, jnp.zeros_like(low))

    shard = ("z", "yh")

    def spread_over(value, axes):
        return lax.all_to_all(jnp.broadcast_to(value[None], (8,) + value.shape), axes, 0, 0, tiled=True)

    place = ctx * ROWS + lax.broadcasted_iota(jnp.int32, (2, ROWS), 1)
    position = jnp.where(place >= bounds[:, None], PROMPT + place - bounds[:, None], place)
    freq = BASE ** (-(jnp.arange(HD // 2, dtype=F32) * 2.0 / HD))
    angle = position.reshape(2 * ROWS, 1).astype(F32) * freq[None]
    cosine = jnp.concatenate([jnp.cos(angle)] * 2, axis=1)
    sine = jnp.concatenate([-jnp.sin(angle), jnp.sin(angle)], axis=1)

    def whole(n):
        return lambda core: [slice(0, n)]

    def half(core):
        return [core * HALF + 128 * m for m in range(8)]

    def turns(n):
        return lambda core: [slice(256 * m + 128 * n, 256 * m + 128 * (n + 1)) for m in range(FF // 128)]

    def third(n):
        return lambda core: [slice(n * HALF, (n + 1) * HALF)]

    x2 = rows_of_both(tokens)
    qkv_low = own_columns((2.0 * dot_nt(x2, qkv_down).astype(BF)).astype(BF), 3 * RANK)
    qkv, squares = project_qkv(x2, w_qkv, qkv_low, qkv_up)
    squares = (squares, swap(squares))
    packed = pack_heads(me, qkv, *squares, gains, cosine, sine)
    heads = lax.all_to_all(packed, CTX, 0, 0, tiled=True).reshape(8, 2, ROWS, 3 * HD)
    heads = after(heads, rings_g[0][-1], rings_g[1][-1])
    plan.round(rings_g, heads)
    out_heads, exact, log_total = attend(bounds, heads)
    attended = lax.all_to_all(out_heads, CTX, 0, 0, tiled=True).reshape(8, 2 * ROWS, HD)
    keep, give, attended = project_out(me, attended, w_out, out_down)
    attn_pre, hidden, sent = combine_attention(me, keep, swap(give), tokens, gains, out_up2)

    sent = after(sent, rings_g[0][-1], rings_g[1][-1])
    plan.round(rings_g, attended)
    wg = Chunks(256, CUT_G, 2 * FF, places, xs_m, 0, rings_g)
    gu, mixed, h2, gu_low, keep, give = feed_forward(wg, sent, swap(sent), gu_down, gu_up, ff_down)
    output, sent = combine_output(me, keep, swap(give), hidden, cotangent, gains, ff_up2)

    d_gu, d_mlp, ff_grad_low, keep, give = feed_forward_back(wg, sent, swap(sent), ff_up2, ff_down, gu, gu_up)
    early = rank_gradients(
        [gu_low, ff_grad_low, d_mlp],
        [d_gu, mixed, d_mlp],
        me,
        "early_gradients",
        [
            (0, 0, (0, 2 * RANK), 1, turns(0)),
            (0, 0, (RANK, 3 * RANK), 1, turns(1)),
            (1, 1, (0, RANK), 1, whole(FF)),
            (2, 2, (D, D), 2, half),
        ],
        EARLY,
    )
    d_hidden, sent = combine_hidden(me, keep, swap(give), cotangent, attn_pre, gains, gu_down)
    sent, early = lax.optimization_barrier((sent, early))
    early = lax.all_to_all(early, CTX, 0, 0, tiled=True)

    d_out_heads, _ = project_out_back(me, sent, swap(sent), w_out, out_up2, out_down, h2, attended)
    d_out_heads = lax.all_to_all(d_out_heads, CTX, 0, 0, tiled=True)
    own = jnp.sum(early.astype(F32), axis=0).astype(BF)
    middle = jnp.sum(d_out_heads[:, 2 * ROWS :].astype(F32), axis=0).astype(BF).reshape(4, 2 * RANK, HD)
    own = jnp.concatenate([own, *middle], axis=1)
    own_slot = jnp.repeat(slots, RANK)[:, None] == lax.broadcasted_iota(jnp.int32, (1, 128), 1)
    own = jnp.concatenate([own, own_slot.astype(BF)], axis=1)
    d_out_heads, own = lax.optimization_barrier((d_out_heads, own))
    groups = spread_over(own, shard).reshape(16, RANK, EARLY + MIDDLE + 128)
    d_heads = attend_back(bounds, heads, d_out_heads, exact, log_total)
    d_heads = lax.all_to_all(d_heads, CTX, 0, 0, tiled=True).reshape(8, 2 * ROWS, 3 * HD)

    def by_slot(groups):
        flat = groups.reshape(16, -1)
        return lax.dot_general(picker, flat, **TN).astype(BF).reshape(8 * RANK, -1)

    picker = groups[:, 0, EARLY + MIDDLE : EARLY + MIDDLE + 8]
    early, d_heads = lax.optimization_barrier((by_slot(groups[:, :, : EARLY + MIDDLE]), d_heads))
    early = lax.all_gather(early, CTX)
    w_q, w_k, d_v, sums = unpack_heads(me, d_heads, qkv, gains, cosine, sine)
    d_qkv, keep, give = project_qkv_back(me, (w_q, w_k), d_v, qkv, squares, (sums, swap(sums)), w_qkv, qkv_up)
    grad_tokens, low = combine_tokens(me, keep, swap(give), d_hidden, qkv_down)
    low = both(low, swap(low)).reshape(2 * ROWS, 128)

    late = rank_gradients(
        [low, qkv_low],
        [x2, d_qkv],
        me,
        "late_gradients",
        [(0, 0, (n * RANK, n * RANK), 1, half) for n in range(3)]
        + [(1, 1, (n * RANK, (3 + n) * RANK), 1, third(n)) for n in range(3)],
        LATE,
    )
    late = lax.all_to_all(late, CTX, 0, 0, tiled=True)
    late = jnp.sum(late.astype(F32), axis=0).astype(BF)
    late = spread_over(late, shard)
    early, late = lax.optimization_barrier((early, late))
    late = spread_over(by_slot(late.reshape(16, RANK, LATE)), CTX)
    shape = (8, 8, RANK, -1)
    early = early.reshape(shape)
    early_other = swap(early)
    grad_up_hidden, grad_down_ff, middle = adapter_outputs(
        me,
        [early],
        [early_other],
        [(8, 2, RANK, 2 * FF), (8, RANK, 2 * FF), (8, 5, RANK, D)],
        "early_outputs",
        write_early,
    )
    late, middle = lax.optimization_barrier((late, middle))
    late_other = swap(late)
    late, late_other = late.reshape(shape), late_other.reshape(shape)
    shapes = [(8, 6, RANK, D), (8, 5, RANK, D)]
    grad_down_in, grad_up_model = adapter_outputs(
        me, [late], [late_other], shapes, "late_outputs", write_late, [middle]
    )
    return (output[None], grad_tokens[None], grad_down_in, grad_down_ff, grad_up_model, grad_up_hidden)


def solution(mesh):
    fine = Mesh(mesh.devices.reshape(2, 4, 4, 2, 2), ALL)
    shard = ("z", "yh", "c")
    rows = P(shard, None)
    per_token = P(shard, CTX, None)
    return jax.shard_map(
        on_device,
        mesh=fine,
        in_specs=(per_token, per_token) + (rows,) * 7 + (P(),) * 5 + (rows, rows),
        out_specs=(per_token, per_token, P(), P(), P(), P()),
        check_vma=False,
    )
```

```python
import jax
import jax.numpy as jnp
from jax import lax
from jax.experimental import pallas as pl
from jax.experimental.pallas import tpu as pltpu
from jax.sharding import Mesh, PartitionSpec as P

HD = 128
PROMPT = 1024
ROWS = 144
TOTAL = 1152
D = 2048
HALF = 1024
FF = 4096
RANK = 16
SCALE = HD**-0.5
EPS = 1e-06
BASE = 500000.0
ALL = ("yl", "x", "z", "yh", "c")
CTX = ("yl", "x")
BF = jnp.bfloat16
F32 = jnp.float32
CUT_A, CUT_G = 2048, 4096
EARLY, MIDDLE, LATE = 1664, 512, 768


NT = dict(dimension_numbers=(((1,), (1,)), ((), ())), preferred_element_type=F32)
TN = dict(dimension_numbers=(((0,), (0,)), ((), ())), preferred_element_type=F32)


CORE, X, YL, YH, Z0 = 0, 1, 2, 3, 4


def _place(yl, x, z, yh, c):
    return (((yl * 4 + x) * 4 + z) * 2 + yh) * 2 + c


def _permutation(move):
    pairs = []
    for yl in range(2):
        for x in range(4):
            for z in range(4):
                for yh in range(2):
                    for c in range(2):
                        nx, ny, nz, nc = move(x, 2 * yh + yl, z, c)
                        pairs.append(
                            (_place(yl, x, z, yh, c), _place(ny % 2, nx % 4, nz % 4, (ny % 4) // 2, nc))
                        )
    return pairs


STEPS = {
    "y": _permutation(lambda x, y, z, c: (x, (y + 1 - 2 * c) % 4, z, c)),
    "z": _permutation(lambda x, y, z, c: (x, y, z + 1 - 2 * c, c)),
    "cross": _permutation(lambda x, y, z, c: (x, 3 - y, z, c)),
    "core": _permutation(lambda x, y, z, c: (x, y, z, 1 - c)),
}


def swap(value):
    return lax.ppermute(value, ALL, STEPS["core"])


class Lane:
    def __init__(self):
        self.last = None

    def send(self, value, how):
        if self.last is not None:
            value, _ = lax.optimization_barrier((value, self.last))
        self.last = lax.ppermute(value, ALL, STEPS[how])
        return self.last


def after(value, *others):
    return lax.optimization_barrier((value, *others))[0]


def _smem():
    return pl.BlockSpec(memory_space=pltpu.SMEM)


def _vmem():
    return pl.BlockSpec(memory_space=pltpu.VMEM)


def _plain(body, name, outs, ins, scalars, scratch=(), limit=48):
    size = sum(v.size * v.dtype.itemsize for v in list(ins) + list(outs))
    return pl.pallas_call(
        body,
        out_shape=outs,
        in_specs=[_smem()] * len(scalars) + [_vmem()] * len(ins),
        out_specs=[_vmem()] * len(outs),
        scratch_shapes=list(scratch),
        compiler_params=pltpu.CompilerParams(vmem_limit_bytes=limit * 2**20),
        cost_estimate=pl.CostEstimate(flops=0, bytes_accessed=size, transcendentals=0),
        name=name,
    )(*scalars, *ins)


def bf(*shape):
    return jax.ShapeDtypeStruct(shape, BF)


def split_a(core, q, k, v):
    def body(core, q, k, v, keep, give):
        for n, w in enumerate((q, k, v)):
            for h in range(8):
                here = slice(n * HALF + HD * h, n * HALF + HD * (h + 1))
                keep[:, here] = w[:, pl.ds(pl.multiple_of((2 * h + core[0]) * HD, HD), HD)]
                give[:, here] = w[:, pl.ds(pl.multiple_of((2 * h + 1 - core[0]) * HD, HD), HD)]

    return _plain(body, "split_a", [bf(HD, 3 * HALF)] * 2, [q, k, v], [core])


def split_g(core, gate, upward):
    def body(core, gate, upward, keep, give):
        for m in range(FF // 128):
            for n, w in enumerate((gate, upward)):
                here = slice(256 * m + 128 * n, 256 * m + 128 * (n + 1))
                for side, out in ((core[0], keep), (1 - core[0], give)):
                    start = (2 * (m // 4) + side) * 512 + (m % 4) * 128
                    out[:, here] = w[:, pl.ds(pl.multiple_of(start, 128), 128)]

    return _plain(body, "split_g", [bf(HD, 2 * FF)] * 2, [gate, upward], [core])


def parts_a(me, keep, got, out):
    quarter = CUT_A // 4

    def body(me, keep, got, out, xs, ys):
        for side, w in ((me[CORE], keep), (1 - me[CORE], got)):
            rows = pl.ds(pl.multiple_of(side * HD, HD), HD)
            xs[rows, :] = w[:, pl.ds(pl.multiple_of(me[X] * quarter, 128), quarter)]

            @pl.when(me[YL] == 0)
            def _():
                ys[rows, :] = w[:, 2 * HALF :]

        @pl.when(me[YL] == 1)
        def _():
            ys[:HD, :] = out[:, :HALF]
            ys[HD:, :] = out[:, HALF:]

    return _plain(body, "parts_a", [bf(256, quarter), bf(256, HALF)], [keep, got, out], [me])


def parts_m(me, keep, got, down):
    gx, dx, gy = CUT_G // 4, D // 4, FF - CUT_G // 2

    def body(me, keep, got, down, xs, ys):
        for side, w in ((me[CORE], keep), (1 - me[CORE], got)):
            rows = pl.ds(pl.multiple_of(side * HD, HD), HD)
            xs[rows, :gx] = w[:, pl.ds(pl.multiple_of(me[X] * gx, 128), gx)]
            ys[rows, :] = w[:, pl.ds(pl.multiple_of(CUT_G + me[YL] * gy, 128), gy)]
        for n in range(2):
            rows = slice(256 * n, 256 * (n + 1))
            xs[:, gx + n * dx : gx + (n + 1) * dx] = down[rows, pl.ds(pl.multiple_of(me[X] * dx, 128), dx)]

    return _plain(body, "parts_m", [bf(256, gx + 2 * dx), bf(256, gy)], [keep, got, down], [me])


def spread(me, got, pieces, name):
    def body(me, *refs):
        chunks, outs = refs[:4], refs[4:]
        for k in range(4):
            z = me[Z0 + k]
            for p, (column, width, folds) in enumerate(pieces):
                for half in range(2):

                    @pl.when(z // 2 == half)
                    def _():
                        for n in range(folds):
                            at = pl.multiple_of(((z - 2 * half) * folds + n) * 256, 256)
                            start = column + n * width
                            outs[2 * p + half][pl.ds(at, 256), :] = chunks[k][:, start : start + width]

    outs = [bf(2 * folds * 256, width) for _, width, folds in pieces for _ in range(2)]
    return _plain(body, name, outs, list(got), [me])


class Chunks:
    def __init__(self, rows, cut, width, places, xs, column, y):
        self.rows, self.cx, self.cy = rows, cut, width - cut
        self.depth = 8 * rows
        self.places = places
        self.column = column
        self.arrays = [xs] + (y[0] + y[1] if y else [])


def _y_rows(places, rows, half, j, k):
    return pl.multiple_of((2 * half + j) * 2 * rows + places[0, k] * rows, rows)


def _panel_copies(rows, width, column, xs, whole, panels):
    copies = []
    for at, k in enumerate(panels):
        for z in range(4):
            for yh in range(2):
                for n in range(rows // 256):
                    target = whole.at[pl.ds((2 * z + yh) * rows + 256 * n, 256), pl.ds(at * width, width)]
                    copies.append((xs.at[k, z, yh, :, pl.ds(column + n * width, width)], target))
    return copies


def _y_copies(places, y, whole, k, column, width):
    copies = []
    for half in range(2):
        for j in range(2):
            row = _y_rows(places, 256, half, j, k)
            copies.append((y[4 * half + k].at[pl.ds(j * 256, 256)], whole.at[pl.ds(row, 256), pl.ds(column, width)]))
    return copies


def assemble(w):
    anywhere = pl.BlockSpec(memory_space=pl.ANY)

    def body(places, *refs):
        out, out_matrix, sems = refs[9], refs[10], refs[11]
        panels = _panel_copies(256, w.cx // 4, 0, refs[0], out, range(4))
        plain = [pltpu.make_async_copy(a, b, sems.at[n]) for n, (a, b) in enumerate(panels)]
        for copy in plain:
            copy.start()

        def move(started):
            at = len(plain)
            for k in range(4):
                for half in range(2):
                    for j in range(2):
                        source = refs[1 + 4 * half + k].at[pl.ds(j * 256, 256)]
                        block = 2 * (2 * half + j) + places[0, k]

                        @pl.when(places[1, k] == 0)
                        def _():
                            row = pl.multiple_of(block * 256, 256)
                            target = out.at[pl.ds(row, 256), pl.ds(2 * HALF, HALF)]
                            copy = pltpu.make_async_copy(source, target, sems.at[at])
                            copy.wait() if started else copy.start()

                        @pl.when(places[1, k] == 1)
                        def _():
                            for n in range(2):
                                row = pl.multiple_of(block * HD, HD)
                                target = out_matrix.at[pl.ds(row, HD), pl.ds(n * HALF, HALF)]
                                copy = pltpu.make_async_copy(source.at[pl.ds(n * HD, HD)], target, sems.at[at + n])
                                copy.wait() if started else copy.start()

                        at += 2

        move(False)
        for copy in plain:
            copy.wait()
        move(True)

    return pl.pallas_call(
        body,
        out_shape=[bf(D, 3 * HALF), bf(HALF, D)],
        in_specs=[_smem()] + [anywhere] * 9,
        out_specs=[_vmem()] * 2,
        scratch_shapes=[pltpu.SemaphoreType.DMA((64,))],
        compiler_params=pltpu.CompilerParams(vmem_limit_bytes=48 * 2**20),
        cost_estimate=pl.CostEstimate(flops=0, bytes_accessed=64 * 2**20, transcendentals=0),
        name="assemble",
    )(w.places, *w.arrays)


WIDE = D + 128


def _f32(*shape):
    return jax.ShapeDtypeStruct(shape, F32)


def _pair_up(core, own, other, pair):
    pair[pl.ds(pl.multiple_of(core * ROWS, ROWS), ROWS), :] = own[...]
    pair[pl.ds(pl.multiple_of((1 - core) * ROWS, ROWS), ROWS), :] = other[...]


def _split(core, sums, keep, give):
    keep[...] = sums[pl.ds(pl.multiple_of(core * ROWS, ROWS), ROWS), :]
    give[...] = sums[pl.ds(pl.multiple_of((1 - core) * ROWS, ROWS), ROWS), :].astype(BF)


def _in_group(rows, columns, count):
    row = lax.broadcasted_iota(jnp.int32, (rows, columns), 0) >= ROWS
    column = lax.broadcasted_iota(jnp.int32, (rows, columns), 1) >= count
    return row == column


def _own_group(low, count):
    row = lax.broadcasted_iota(jnp.int32, (low.shape[0], count), 0)
    return jnp.where(row >= ROWS, low[:, count:], low[:, :count])


def _put_low(sums, low):
    count = low.shape[1]
    sums[:, D:] = jnp.zeros((sums.shape[0], WIDE - D), F32)
    sums[:, D : D + count] = low


SLOT = D
SLOTS = 4


class Stream:
    def __init__(self, w):
        self.w = w

    def gate_up(self, places, refs, n):
        xs, y, quarter = refs[0], refs[1:9], CUT_G // 4
        if n < 2:
            return n * SLOT, lambda slot: _panel_copies(256, quarter, 0, xs, slot, range(2 * n, 2 * n + 2))
        column = pl.multiple_of(CUT_G + places[1, n - 2] * SLOT, SLOT)
        return column, lambda slot: [
            copy for k in (n - 2, n) for copy in _y_copies(places, y, slot, k, 0, SLOT)
        ]

    def down(self, refs, n):
        xs, quarter = refs[0], D // 4

        def copies(slot):
            made = []
            for k in range(4):
                for block in range(4 * n, 4 * n + 4):
                    for m in range(2):
                        source = xs.at[k, block // 2, block % 2, :, pl.ds(CUT_G // 4 + m * quarter, quarter)]
                        row = (block - 4 * n) * 512 + 256 * m
                        made.append((source, slot.at[pl.ds(row, 256), pl.ds(k * quarter, quarter)]))
            return made

        return n * SLOT, copies

    def run(self, pieces, slots, sems, first, use):
        copies = []
        for n, (_, made) in enumerate(pieces):
            slot = n % SLOTS
            pairs = made(slots.at[slot])
            copies.append([pltpu.make_async_copy(a, b, sems.at[slot, m]) for m, (a, b) in enumerate(pairs)])

        def begin(n):
            if n < len(copies):
                for copy in copies[n]:
                    copy.start()

        for n in range(SLOTS - 1):
            begin(n)
        first()
        for n, (at, _) in enumerate(pieces):
            for copy in copies[n]:
                copy.wait()
            use(n, at, slots.at[n % SLOTS])
            begin(n + SLOTS - 1)

    def call(self, body, name, ins, outs, scratch=()):
        w = self.w
        anywhere = pl.BlockSpec(memory_space=pl.ANY)
        size = 6 * D * FF + sum(v.size * v.dtype.itemsize for v in ins)
        return pl.pallas_call(
            body,
            out_shape=outs,
            in_specs=[_smem()] + [anywhere] * 9 + [_vmem()] * len(ins),
            out_specs=[_vmem()] * len(outs),
            scratch_shapes=[pltpu.VMEM((SLOTS, SLOT, SLOT), BF), pltpu.SemaphoreType.DMA((SLOTS, 32)), *scratch],
            compiler_params=pltpu.CompilerParams(vmem_limit_bytes=60 * 2**20),
            cost_estimate=pl.CostEstimate(flops=4 * ROWS * D * 3 * FF, bytes_accessed=size, transcendentals=0),
            name=name,
        )(w.places, *w.arrays, *ins)


def feed_forward(w, own, other, maps_down, maps_up, ff_down):
    rows = 2 * ROWS
    stream = Stream(w)

    def body(places, *refs):
        weights, (own_ref, other_ref, down_ref, up_ref, ff_ref) = refs[:9], refs[9:14]
        gu, mixed, pair, low_ref, keep, give, slots, sems, sums = refs[14:]

        def first():
            _pair_up(places[2, 0], own_ref, other_ref, pair)
            low = 2.0 * lax.dot_general(pair[:, :D], down_ref[...], **NT).astype(BF).astype(F32)
            low_ref[...] = jnp.where(_in_group(rows, 4 * RANK, 2 * RANK), low, 0.0).astype(BF)

        def use(n, at, slot):
            tile = SLOT // 2
            if n < 4:
                for t in range(2):
                    column = at + t * tile
                    unit = column // 2
                    if not isinstance(at, int):
                        column, unit = pl.multiple_of(column, tile), pl.multiple_of(unit, tile // 2)
                    total = jnp.dot(pair[:, :D], slot[:, t * tile : (t + 1) * tile], preferred_element_type=F32)
                    total = total + jnp.dot(low_ref[...], up_ref[:, pl.ds(column, tile)], preferred_element_type=F32)
                    gu[:, pl.ds(column, tile)] = total.astype(BF)
                    for m in range(tile // 256):
                        g, u = total[:, 256 * m : 256 * m + 128], total[:, 256 * m + 128 : 256 * m + 256]
                        mixed[:, pl.ds(unit + 128 * m, 128)] = (g * jax.nn.sigmoid(g) * u).astype(BF)
                return
            left = mixed[:, at : at + SLOT]
            for t in range(2):
                here = slice(t * tile, (t + 1) * tile)
                part = jnp.dot(left, slot[:, here], preferred_element_type=F32)
                if n == 4:
                    sums[:, here] = part
                else:
                    sums[:, here] += part

        pieces = [stream.gate_up(places, weights, n) for n in range(4)] + [stream.down(weights, n) for n in range(2)]
        stream.run(pieces, slots, sems, first, use)
        _put_low(sums, _own_group(lax.dot_general(mixed[...], ff_ref[...], **NT), RANK))
        _split(places[2, 0], sums, keep, give)

    outs = [bf(rows, 2 * FF), bf(rows, FF), bf(rows, WIDE), bf(rows, 4 * RANK), _f32(ROWS, WIDE), bf(ROWS, WIDE)]
    ins = [own, other, maps_down, maps_up, ff_down]
    return stream.call(body, "feed_forward", ins, outs, [pltpu.VMEM((rows, WIDE), F32)])


def feed_forward_back(w, own, other, ff_up, ff_down, gu, maps_up):
    rows = 2 * ROWS
    stream = Stream(w)

    def body(places, *refs):
        weights, (own_ref, other_ref, ff_up_ref, ff_down_ref, gu_ref, up_ref) = refs[:9], refs[9:15]
        out, pair, low_ref, keep, give, slots, sems, sums, lows = refs[15:]

        def first():
            _pair_up(places[2, 0], own_ref, other_ref, pair)
            low = 2.0 * lax.dot_general(pair[:, :D], ff_up_ref[...], **NT)
            low_ref[...] = jnp.where(_in_group(rows, 2 * RANK, RANK), low, 0.0).astype(BF)

        def use(n, at, slot):
            tile = SLOT // 2
            if n < 2:
                for t in range(2):
                    units = slice(at + t * tile, at + (t + 1) * tile)
                    d_mixed = lax.dot_general(pair[:, :D], slot[t * tile : (t + 1) * tile, :], **NT)
                    d_mixed = d_mixed + jnp.dot(low_ref[...], ff_down_ref[:, units], preferred_element_type=F32)
                    for m in range(tile // 128):
                        column = 2 * (at + t * tile) + 256 * m
                        g = gu_ref[:, column : column + 128].astype(F32)
                        u = gu_ref[:, column + 128 : column + 256].astype(F32)
                        d = d_mixed[:, 128 * m : 128 * (m + 1)]
                        s = jax.nn.sigmoid(g)
                        out[:, column : column + 128] = (d * u * s * (1.0 + g * (1.0 - s))).astype(BF)
                        out[:, column + 128 : column + 256] = (d * g * s).astype(BF)
                return
            left = out[:, pl.ds(at, SLOT)]
            low = lax.dot_general(left, up_ref[:, pl.ds(at, SLOT)], **NT)
            for t in range(2):
                here = slice(t * tile, (t + 1) * tile)
                part = lax.dot_general(left, slot[here, :], **NT)
                if n == 2:
                    sums[:, here] = part
                else:
                    sums[:, here] += part
            if n == 2:
                lows[...] = low
            else:
                lows[...] += low

        pieces = [stream.down(weights, n) for n in range(2)] + [stream.gate_up(places, weights, n) for n in range(4)]
        stream.run(pieces, slots, sems, first, use)
        _put_low(sums, _own_group(lows[...], 2 * RANK))
        _split(places[2, 0], sums, keep, give)

    outs = [bf(rows, 2 * FF), bf(rows, WIDE), bf(rows, 2 * RANK), _f32(ROWS, WIDE), bf(ROWS, WIDE)]
    ins = [own, other, ff_up, ff_down, gu, maps_up]
    scratch = [pltpu.VMEM((rows, WIDE), F32), pltpu.VMEM((rows, 4 * RANK), F32)]
    return stream.call(body, "feed_forward_back", ins, outs, scratch)


def project_qkv(x, w, low, maps_up):
    rows, tile = x.shape[0], 512

    def body(x, w, low, up, out, squares):
        i = pl.program_id(0)

        @pl.when(i == 0)
        def _():
            squares[...] = jnp.zeros_like(squares)

        total = jnp.dot(x[...], w[...], preferred_element_type=F32)
        total = total + jnp.dot(low[...], up[...], preferred_element_type=F32)
        out[...] = total
        here = lax.broadcasted_iota(jnp.int32, squares.shape, 1) == i // 2
        squares[...] += jnp.where(here, jnp.sum(total * total, axis=1, keepdims=True), 0.0)

    whole = lambda v: pl.BlockSpec(v.shape, lambda i: (0, 0))
    column = lambda n: pl.BlockSpec((n, tile), lambda i: (0, i))
    return pl.pallas_call(
        body,
        grid=(3 * HALF // tile,),
        out_shape=[_f32(rows, 3 * HALF), _f32(rows, 128)],
        in_specs=[whole(x), column(D), whole(low), column(maps_up.shape[0])],
        out_specs=[column(rows), pl.BlockSpec((rows, 128), lambda i: (0, 0))],
        compiler_params=pltpu.CompilerParams(vmem_limit_bytes=60 * 2**20),
        cost_estimate=pl.CostEstimate(flops=2 * rows * D * 3 * HALF, bytes_accessed=18_000_000, transcendentals=0),
        name="project_qkv",
    )(x, w, low, maps_up)


def project_out(me, heads, w, maps_down):
    rows = 2 * ROWS

    def body(me, heads, w, down, keep, give, flat, sums):
        flat[...] = jnp.concatenate([heads[h] for h in range(8)], axis=1)
        for n in range(0, D, 512):
            sums[:, n : n + 512] = jnp.dot(flat[...], w[:, n : n + 512], preferred_element_type=F32)
        _put_low(sums, _own_group(lax.dot_general(flat[...], down[...], **NT), RANK))
        _split(me[CORE], sums, keep, give)

    outs = [_f32(ROWS, WIDE), bf(ROWS, WIDE), bf(rows, HALF)]
    return _plain(body, "project_out", outs, [heads, w, maps_down], [me], [pltpu.VMEM((rows, WIDE), F32)])


def _low_and_sum(me, keep, got, maps, count, factor):
    total = keep[...] + got[...].astype(F32)
    low = (factor * total[:, D : D + count]).astype(BF)
    start = pl.multiple_of(me[CORE] * count, count)
    return total[:, :D], low, jnp.dot(low, maps[pl.ds(start, count), :], preferred_element_type=F32)


def _send(out, value, low):
    out[:, :D] = value.astype(BF)
    out[:, D:] = jnp.zeros((ROWS, WIDE - D), BF)
    out[:, D : D + low.shape[1]] = low


def _inverse(field):
    return lax.rsqrt(jnp.mean(field * field, axis=1, keepdims=True) + EPS)


def combine_attention(me, keep, got, tokens, gains, maps_up):
    def body(me, keep, got, tokens, gains, up, pre, hidden, out):
        total, low, raised = _low_and_sum(me, keep, got, up, RANK, 1.0)
        field = total + 2.0 * raised
        pre[...] = field
        value = tokens[...].astype(F32) + field * _inverse(field) * gains[2:3]
        hidden[...] = value
        _send(out, value, low)

    outs = [_f32(ROWS, D), _f32(ROWS, D), bf(ROWS, WIDE)]
    return _plain(body, "combine_attention", outs, [keep, got, tokens, gains, maps_up], [me])


def combine_output(me, keep, got, hidden, cotangent, gains, maps_up):
    def body(me, keep, got, hidden, cotangent, gains, up, output, out):
        total, low, raised = _low_and_sum(me, keep, got, up, RANK, 1.0)
        field = total + 2.0 * raised
        inverse = _inverse(field)
        output[...] = (hidden[...] + field * inverse * gains[3:4]).astype(BF)
        _send(out, normalize_back(field, inverse, gains[3:4], cotangent[...].astype(F32)), low)

    outs = [bf(ROWS, D), bf(ROWS, WIDE)]
    return _plain(body, "combine_output", outs, [keep, got, hidden, cotangent, gains, maps_up], [me])


def combine_hidden(me, keep, got, cotangent, pre, gains, maps_down):
    def body(me, keep, got, cotangent, pre, gains, down, hidden, out):
        total, low, lowered = _low_and_sum(me, keep, got, down, 2 * RANK, 2.0)
        value = cotangent[...].astype(F32) + total + lowered
        hidden[...] = value
        field = pre[...]
        _send(out, normalize_back(field, _inverse(field), gains[2:3], value), low)

    outs = [_f32(ROWS, D), bf(ROWS, WIDE)]
    return _plain(body, "combine_hidden", outs, [keep, got, cotangent, pre, gains, maps_down], [me])


def combine_tokens(me, keep, got, hidden, maps_down):
    def body(me, keep, got, hidden, down, out, low_out):
        total, low, lowered = _low_and_sum(me, keep, got, down, 3 * RANK, 2.0)
        out[...] = (hidden[...] + total + lowered).astype(BF)
        low_out[...] = jnp.zeros_like(low_out)
        low_out[:, : 3 * RANK] = low

    outs = [bf(ROWS, D), bf(ROWS, 128)]
    return _plain(body, "combine_tokens", outs, [keep, got, hidden, maps_down], [me])


def project_out_back(me, own, other, w, maps_up, maps_down, h2, attended):
    rows = 2 * ROWS

    def body(me, own, other, w, up, down, h2, attended, out, low_ref, pair):
        _pair_up(me[CORE], own, other, pair)
        low = 2.0 * lax.dot_general(pair[:, :D], up[...], **NT)
        low_ref[...] = jnp.where(_in_group(rows, 2 * RANK, RANK), low, 0.0).astype(BF)
        for n in range(0, HALF, 512):
            total = lax.dot_general(pair[:, :D], w[n : n + 512, :], **NT)
            total = total + jnp.dot(low_ref[...], down[:, n : n + 512], preferred_element_type=F32)
            for h in range(4):
                out[n // HD + h, :rows] = total[:, h * HD : (h + 1) * HD].astype(BF)

        def shared(columns, start):
            picked = jnp.concatenate([columns[:, start : start + RANK]] * 2, axis=1)
            return jnp.where(_in_group(rows, 2 * RANK, RANK), picked, jnp.zeros_like(picked))

        here = pl.ds(pl.multiple_of(me[CORE] * HALF, HALF), HALF)
        pieces = [
            (shared(pair, D), h2[:, here]),
            (shared(pair, D + RANK), h2[:, here]),
            (low_ref[...], attended[...]),
            (2 * shared(h2, D), pair[:, here]),
        ]
        for p, (picked, act) in enumerate(pieces):
            grad = lax.dot_general(picked, act, **TN).astype(BF)
            at = slice(rows + 2 * RANK * p, rows + 2 * RANK * (p + 1))
            for b in range(8):
                out[b, at] = grad[:, HD * b : HD * (b + 1)]

    outs = [bf(8, rows + 8 * RANK, HD), bf(rows, 2 * RANK)]
    ins = [own, other, w, maps_up, maps_down, h2, attended]
    return _plain(body, "project_out_back", outs, ins, [me], [pltpu.VMEM((rows, WIDE), BF)])


def project_qkv_back(me, weighted, value_grad, qkv, squares, sums, w, maps_up):
    rows, tile = 2 * ROWS, 512

    def body(me, wq, wk, dv, q, k, sq, sq_other, su, su_other, w, up, d_qkv, keep, give, acc):
        i = pl.program_id(0)

        @pl.when(i == 0)
        def _():
            inverse = lax.rsqrt((sq[...] + sq_other[...]) / D + EPS)
            mean = (su[...] + su_other[...]) / D
            for n, (weight, field) in enumerate(((wq, q), (wk, k))):
                r, m = inverse[:, n : n + 1], mean[:, n : n + 1]
                d_qkv[:, n * HALF : (n + 1) * HALF] = (r * weight[...] - field[...] * (r * r * r * m)).astype(BF)
            d_qkv[:, 2 * HALF :] = dv[...]
            _put_low(acc, _own_group(lax.dot_general(d_qkv[...], up[...], **NT), 3 * RANK))

        acc[:, pl.ds(pl.multiple_of(i * tile, tile), tile)] = lax.dot_general(d_qkv[...], w[...], **NT)

        @pl.when(i == D // tile - 1)
        def _():
            _split(me[CORE], acc, keep, give)

    once = lambda v: pl.BlockSpec(v.shape, lambda i: (0, 0), pipeline_mode=pl.Buffered(1))
    third = lambda n: pl.BlockSpec((rows, HALF), lambda i: (0, n), pipeline_mode=pl.Buffered(1))
    ins = [*weighted, value_grad]
    return pl.pallas_call(
        body,
        grid=(D // tile,),
        out_shape=[bf(rows, 3 * HALF), _f32(ROWS, WIDE), bf(ROWS, WIDE)],
        in_specs=[_smem()]
        + [once(v) for v in ins]
        + [third(0), third(1)]
        + [once(v) for v in (*squares, *sums)]
        + [pl.BlockSpec((tile, 3 * HALF), lambda i: (i, 0)), once(maps_up)],
        out_specs=[once(jax.ShapeDtypeStruct((rows, 3 * HALF), BF))] + [once(_f32(ROWS, WIDE))] * 2,
        scratch_shapes=[pltpu.VMEM((rows, WIDE), F32)],
        compiler_params=pltpu.CompilerParams(vmem_limit_bytes=48 * 2**20),
        cost_estimate=pl.CostEstimate(flops=2 * rows * D * 3 * HALF, bytes_accessed=22_000_000, transcendentals=0),
        name="project_qkv_back",
    )(me, *ins, qkv, qkv, *squares, *sums, w, maps_up)


class Gather:
    def __init__(self):
        core = lax.axis_index("c")
        x, z = lax.axis_index("x"), lax.axis_index("z")
        yl, yh = lax.axis_index("yl"), lax.axis_index("yh")
        y = 2 * yh + yl
        sign = 1 - 2 * core
        ys = [lax.rem(y - sign * k + 8, 4) for k in range(4)]
        zs = [lax.rem(z - sign * k + 8, 4) for k in range(4)]
        self.yh = yh
        self.me = jnp.stack([core, x, yl, yh] + zs).astype(jnp.int32)
        self.places = jnp.stack([jnp.stack([v // 2 for v in ys]), jnp.stack([v % 2 for v in ys]), self.me[:4]]).astype(jnp.int32)
        self.lanes = {"y0": Lane(), "y1": Lane(), "z": Lane(), "cross": Lane()}

    def across(self, own):
        return self.lanes["cross"].send(own, "cross")

    def over_xz(self, own, other, *before):
        other = after(other, *before)
        both = jnp.where(self.yh == 0, jnp.stack([own, other]), jnp.stack([other, own]))
        return lax.all_gather(both, ("x", "z")).reshape(4, 4, 2, *own.shape)

    def small(self, own):
        got = [own]
        for _ in range(3):
            got.append(self.lanes["z"].send(got[-1], "z"))
        return got

    def round(self, rings, *before):
        for n in range(2):
            value = after(rings[n][-1], *before) if before else rings[n][-1]
            rings[n].append(self.lanes["y%d" % n].send(value, "y"))


def turn(value, cosine, sine):
    return value * cosine + pltpu.roll(value, 64, 1) * sine


def _gain(gains, n, h, core):
    return gains[n : n + 1, pl.ds(pl.multiple_of((2 * h + core) * HD, HD), HD)]


def _pack_body(me, q, k, v, squares, other, gains, cosine, sine, out):
    scales = lax.rsqrt((squares[...] + other[...]) / D + EPS)
    c, s = cosine[...], sine[...]
    for h in range(4):
        here = slice(h * HD, (h + 1) * HD)
        out[h, :, 0:HD] = turn(q[:, here] * scales[:, 0:1] * _gain(gains, 0, h, me[CORE]), c, s).astype(BF)
        out[h, :, HD : 2 * HD] = turn(k[:, here] * scales[:, 1:2] * _gain(gains, 1, h, me[CORE]), c, s).astype(BF)
        out[h, :, 2 * HD :] = v[:, here].astype(BF)


def _head_specs(rows):
    whole = pl.BlockSpec((rows, HD), lambda i: (0, 0))
    columns = [pl.BlockSpec((rows, 4 * HD), lambda i, n=n: (0, 2 * n + i)) for n in range(3)]
    heads = pl.BlockSpec((4, rows, 3 * HD), lambda i: (i, 0, 0))
    gains = pl.BlockSpec((4, 8 * HD), lambda i: (0, i))
    return whole, columns, heads, gains


def pack_heads(me, qkv, squares, other, gains, cosine, sine):
    rows = qkv.shape[0]
    whole, columns, heads, gain = _head_specs(rows)
    return pl.pallas_call(
        _pack_body,
        grid=(2,),
        out_shape=bf(8, rows, 3 * HD),
        in_specs=[_smem(), *columns, whole, whole, gain, whole, whole],
        out_specs=heads,
        name="pack_heads",
    )(me, qkv, qkv, qkv, squares, other, gains, cosine, sine)


def _unpack_body(me, d, q, k, gains, cosine, sine, wq, wk, dv, sums):
    c, s = cosine[...], -sine[...]

    @pl.when(pl.program_id(0) == 0)
    def _():
        sums[...] = jnp.zeros_like(sums)

    lane = lax.broadcasted_iota(jnp.int32, sums.shape, 1)
    of_q, of_k = 0.0, 0.0
    for h in range(4):
        here = slice(h * HD, (h + 1) * HD)
        gq = turn(d[h, :, 0:HD].astype(F32), c, s) * _gain(gains, 0, h, me[CORE])
        gk = turn(d[h, :, HD : 2 * HD].astype(F32), c, s) * _gain(gains, 1, h, me[CORE])
        wq[:, here] = gq
        wk[:, here] = gk
        dv[:, here] = d[h, :, 2 * HD :]
        of_q += gq * q[:, here]
        of_k += gk * k[:, here]
    of_q, of_k = jnp.sum(of_q, axis=1, keepdims=True), jnp.sum(of_k, axis=1, keepdims=True)
    sums[...] += jnp.where(lane == 0, of_q, jnp.where(lane == 1, of_k, 0.0))


def unpack_heads(me, d, qkv, gains, cosine, sine):
    rows = qkv.shape[0]
    whole, columns, heads, gain = _head_specs(rows)
    return pl.pallas_call(
        _unpack_body,
        grid=(2,),
        out_shape=[_f32(rows, HALF), _f32(rows, HALF), bf(rows, HALF), _f32(rows, HD)],
        in_specs=[_smem(), heads, *columns[:2], gain, whole, whole],
        out_specs=[columns[0], columns[0], columns[0], whole],
        name="unpack_heads",
    )(me, d, qkv, qkv, gains, cosine, sine)


TILE = 128
def hidden_pairs(t, bound):
    query = t * TILE + lax.broadcasted_iota(jnp.int32, (TILE, TILE), 0)
    key = t * TILE + lax.broadcasted_iota(jnp.int32, (TILE, TILE), 1)
    hidden = key > query
    if t * TILE >= PROMPT:
        hidden = hidden | ((query >= bound) & (key < bound))
    return hidden


def tile_scores(q, k, t, bound):
    n = (t + 1) * TILE
    s = lax.dot_general(q[t * TILE : n], k[:n], **NT) * SCALE
    last = jnp.where(hidden_pairs(t, bound), -1e30, s[:, n - TILE :])
    return last if t == 0 else jnp.concatenate([s[:, : n - TILE], last], axis=1)


def _attend_body(bounds, qkv, out, exact, total):
    bound = bounds[pl.program_id(0)]
    q = qkv[:, 0, :, 0:HD].reshape(TOTAL, HD)
    k = qkv[:, 0, :, HD : 2 * HD].reshape(TOTAL, HD)
    v = qkv[:, 0, :, 2 * HD :].reshape(TOTAL, HD)
    for t in range(TOTAL // TILE):
        n = (t + 1) * TILE
        s = tile_scores(q, k, t, bound)
        top = jnp.max(s, axis=1, keepdims=True)
        p = jnp.exp(s - top)
        denom = jnp.sum(p, axis=1, keepdims=True)
        o = jnp.dot(p.astype(BF), v[:n], preferred_element_type=F32) / denom
        exact[0, t * TILE : n] = o
        total[0, t * TILE : n] = top + jnp.log(denom)
    out[:, 0] = exact[0].reshape(8, ROWS, HD).astype(BF)


def attend(bounds, qkv):
    return pl.pallas_call(
        _attend_body,
        grid=(2,),
        out_shape=[
            jax.ShapeDtypeStruct((8, 2, ROWS, HD), BF),
            jax.ShapeDtypeStruct((2, TOTAL, HD), F32),
            jax.ShapeDtypeStruct((2, TOTAL, 1), F32),
        ],
        in_specs=[
            pl.BlockSpec(memory_space=pltpu.SMEM),
            pl.BlockSpec((8, 1, ROWS, 3 * HD), lambda g: (0, g, 0, 0)),
        ],
        out_specs=[
            pl.BlockSpec((8, 1, ROWS, HD), lambda g: (0, g, 0, 0)),
            pl.BlockSpec((1, TOTAL, HD), lambda g: (g, 0, 0)),
            pl.BlockSpec((1, TOTAL, 1), lambda g: (g, 0, 0)),
        ],
        compiler_params=pltpu.CompilerParams(vmem_limit_bytes=40 * 2**20),
        cost_estimate=pl.CostEstimate(flops=900_000_000, bytes_accessed=5_000_000, transcendentals=1_500_000),
        name="attend",
    )(bounds, qkv)


def _attend_back_body(bounds, qkv, grad, exact, total, out, dk, dv, dq):
    bound = bounds[pl.program_id(0)]
    q = qkv[:, 0, :, 0:HD].reshape(TOTAL, HD)
    k = qkv[:, 0, :, HD : 2 * HD].reshape(TOTAL, HD)
    v = qkv[:, 0, :, 2 * HD :].reshape(TOTAL, HD)
    g = grad[...].reshape(TOTAL, HD)
    dk[...] = jnp.zeros_like(dk)
    dv[...] = jnp.zeros_like(dv)
    for t in range(TOTAL // TILE):
        n = (t + 1) * TILE
        here = slice(t * TILE, n)
        s = tile_scores(q, k, t, bound)
        p = jnp.exp(s - total[0, here])
        delta = jnp.sum(g[here].astype(F32) * exact[0, here], axis=1, keepdims=True)
        dp = lax.dot_general(g[here], v[:n], **NT)
        ds = (p * (dp - delta)).astype(BF)
        dq[here] = jnp.dot(ds, k[:n], preferred_element_type=F32) * SCALE
        dk[:n] += lax.dot_general(ds, q[here], **TN) * SCALE
        dv[:n] += lax.dot_general(p.astype(BF), g[here], **TN)
    out[:, 0, :, 0:HD] = dq[...].reshape(8, ROWS, HD).astype(BF)
    out[:, 0, :, HD : 2 * HD] = dk[...].reshape(8, ROWS, HD).astype(BF)
    out[:, 0, :, 2 * HD :] = dv[...].reshape(8, ROWS, HD).astype(BF)


def attend_back(bounds, qkv, grad, exact, total):
    return pl.pallas_call(
        _attend_back_body,
        grid=(2,),
        out_shape=jax.ShapeDtypeStruct((8, 2, ROWS, 3 * HD), BF),
        in_specs=[
            pl.BlockSpec(memory_space=pltpu.SMEM),
            pl.BlockSpec((8, 1, ROWS, 3 * HD), lambda g: (0, g, 0, 0)),
            pl.BlockSpec((8, ROWS, HD), lambda g: (0, g, 0)),
            pl.BlockSpec((1, TOTAL, HD), lambda g: (g, 0, 0)),
            pl.BlockSpec((1, TOTAL, 1), lambda g: (g, 0, 0)),
        ],
        out_specs=pl.BlockSpec((8, 1, ROWS, 3 * HD), lambda g: (0, g, 0, 0)),
        scratch_shapes=[pltpu.VMEM((TOTAL, HD), F32)] * 3,
        compiler_params=pltpu.CompilerParams(vmem_limit_bytes=40 * 2**20),
        cost_estimate=pl.CostEstimate(flops=2_300_000_000, bytes_accessed=8_000_000, transcendentals=1_500_000),
        name="attend_back",
    )(bounds, qkv, grad, exact, total)


def dot(a, b):
    return jnp.dot(a, b, preferred_element_type=F32)


def dot_nt(a, b):
    return lax.dot_general(a, b, **NT)


def dot_tn(a, b):
    return lax.dot_general(a, b, **TN)


def normalize_back(field, inverse, gain, grad):
    weighted = grad * gain
    return inverse * weighted - field * inverse**3 * jnp.mean(weighted * field, axis=-1, keepdims=True)


def choose_adapters(slots, down_in, down_ff, up_model, up_hidden):
    def body(slots, down_in, down_ff, up_model, up_hidden, qkv_down, gu_down, out_down, ff_down, qkv_up, out_up, ff_up, gu_up):
        core = slots[2]
        qkv_down[...] = down_in[0, :3].reshape(3 * RANK, D)
        gu_down[...] = down_in[0, 4:].reshape(2 * RANK, D)
        out_up[...] = up_model[0, 3]
        ff_up[...] = up_model[0, 4]
        qkv_up[...] = jnp.zeros_like(qkv_up)
        gu_up[...] = jnp.zeros_like(gu_up)
        for h in range(8):
            head = pl.ds(pl.multiple_of((2 * h + core) * HD, HD), HD)
            out_down[:, HD * h : HD * (h + 1)] = down_in[0, 3, :, head]
            for n in range(3):
                here = slice(n * HALF + HD * h, n * HALF + HD * (h + 1))
                qkv_up[n * RANK : (n + 1) * RANK, here] = up_model[0, n, :, head]
        for m in range(FF // 128):
            start = (2 * (m // 4) + core) * 512 + (m % 4) * 128
            units = pl.ds(pl.multiple_of(start, 128), 128)
            ff_down[:, 128 * m : 128 * (m + 1)] = down_ff[0, :, units]
            for n in range(2):
                here = slice(256 * m + 128 * n, 256 * m + 128 * (n + 1))
                gu_up[n * RANK : (n + 1) * RANK, here] = up_hidden[0, n, :, units]

    def chosen(shape):
        return pl.BlockSpec((1,) + shape[1:], lambda g, slots: (slots[g],) + (0,) * (len(shape) - 1))

    shapes = [(48, D), (32, D), (16, HALF), (16, FF), (48, 3 * HALF), (16, D), (16, D), (32, 2 * FF)]
    maps = [down_in, down_ff, up_model, up_hidden]
    return pl.pallas_call(
        body,
        out_shape=[bf(2 * r, c) for r, c in shapes],
        grid_spec=pltpu.PrefetchScalarGridSpec(
            num_scalar_prefetch=1,
            grid=(2,),
            in_specs=[chosen(m.shape) for m in maps],
            out_specs=[pl.BlockSpec(shape, lambda g, slots: (g, 0)) for shape in shapes],
        ),
        cost_estimate=pl.CostEstimate(flops=0, bytes_accessed=7_000_000, transcendentals=0),
        name="choose_adapters",
    )(slots, *maps)


def rank_gradients(lows, acts, core, name, plan, width):
    count = len(lows)

    def body(core, *refs):
        lows, acts, out = refs[:count], refs[count:-1], refs[-1]
        at = 0
        for low, act, columns, factor, starts in plan:
            picked = [lows[low][:, c : c + RANK] for c in columns]
            picked = jnp.concatenate(picked, axis=1)
            if columns[0] == columns[1]:
                picked = jnp.where(_in_group(2 * ROWS, 2 * RANK, RANK), picked, jnp.zeros_like(picked))
            if factor != 1:
                picked = picked * factor
            for start in starts(core[0]):
                right = acts[act][:, start if isinstance(start, slice) else pl.ds(pl.multiple_of(start, 128), 128)]
                n = right.shape[1]
                grad = lax.dot_general(picked, right, **TN).astype(BF)
                for b in range(n // 128):
                    block, slot = divmod(at, width // 128)
                    out[block, :, 128 * slot : 128 * (slot + 1)] = grad[:, 128 * b : 128 * (b + 1)]
                    at += 1

    return _plain(body, name, [bf(8, 2 * RANK, width)], list(lows) + list(acts), [core])[0]


def adapter_outputs(core, halves, others, shapes, name, write, done=()):
    count = len(halves)

    def body(core, *refs):
        own, other = refs[:count], refs[count : 2 * count]
        ready, outs = refs[2 * count : 2 * count + len(done)], refs[2 * count + len(done) :]

        def place(start):
            return pl.ds(pl.multiple_of(start, 128), 128)

        for side, group in ((core[0], own), (1 - core[0], other)):

            def block(n, b, t):
                return group[n][b, 0, :, 128 * t : 128 * (t + 1)].astype(F32)

            write(side, block, place, outs, *ready)

    arrays = halves + others
    size = sum(v.size * 2 for v in arrays)
    return pl.pallas_call(
        body,
        grid=(8,),
        out_shape=[jax.ShapeDtypeStruct(s, F32) for s in shapes],
        in_specs=[_smem()] + [pl.BlockSpec((8, 1) + v.shape[2:], lambda i: (0, i, 0, 0)) for v in arrays]
        + [pl.BlockSpec((1,) + v.shape[1:], lambda i: (i, 0, 0, 0)) for v in done],
        out_specs=[pl.BlockSpec((1,) + s[1:], lambda i, n=len(s): (i,) + (0,) * (n - 1)) for s in shapes],
        compiler_params=pltpu.CompilerParams(vmem_limit_bytes=60 * 2**20),
        cost_estimate=pl.CostEstimate(flops=0, bytes_accessed=size, transcendentals=0),
        name=name,
    )(core, *arrays, *done)


def write_early(side, block, place, outs):
    up_hidden, down_ff, middle = outs
    slots = EARLY // 128
    for m in range(FF // 128):
        units = place((2 * (m // 4) + side) * 512 + (m % 4) * 128)
        up_hidden[0, 0, :, units] = block(0, *divmod(m, slots))
        up_hidden[0, 1, :, units] = block(0, *divmod(32 + m, slots))
        down_ff[0, :, units] = block(0, *divmod(64 + m, slots))
    for m in range(8):
        whole, head = place(side * HALF + 128 * m), place((2 * m + side) * HD)
        for n in range(2):
            middle[0, n, :, whole] = block(0, m, slots + n)
        middle[0, 2, :, head] = block(0, m, slots + 2)
        middle[0, 3, :, whole] = block(0, m, slots + 3)
        middle[0, 4, :, whole] = block(0, *divmod(96 + m, slots))


def write_late(side, block, place, outs, middle):
    down_in, up_model = outs
    for n, m in ((4, 0), (5, 1), (3, 2)):
        down_in[0, n] = middle[0, m]
    for n in (3, 4):
        up_model[0, n] = middle[0, n]
    slots = LATE // 128
    for m in range(8):
        whole, head = place(side * HALF + 128 * m), place((2 * m + side) * HD)
        for n in range(3):
            down_in[0, n, :, whole] = block(0, *divmod(8 * n + m, slots))
            up_model[0, n, :, head] = block(0, *divmod(24 + 8 * n + m, slots))


def on_device(
    tokens,
    cotangent,
    query_matrix,
    key_matrix,
    value_matrix,
    output_matrix,
    gate_matrix,
    upward_matrix,
    down_matrix,
    gains,
    adapter_down_inputs,
    adapter_down_feedforward,
    adapter_up_model_maps,
    adapter_up_hidden_maps,
    group_adapter_index,
    continuation_lengths,
):
    core = lax.axis_index("c")
    first = core == 0
    ctx = lax.axis_index("yl") * 4 + lax.axis_index("x")
    tokens, cotangent = tokens[0], cotangent[0]

    def both(own, other):
        return jnp.where(first, jnp.stack([own, other]), jnp.stack([other, own]))

    def rows_of_both(own):
        return both(own, swap(own)).reshape(2 * own.shape[0], own.shape[1])

    plan = Gather()
    me, places = plan.me, plan.places
    keep_a, give_a = split_a(me, query_matrix, key_matrix, value_matrix)
    keep_g, give_g = split_g(me, gate_matrix, upward_matrix)
    got_a, got_g = swap(give_a), swap(give_g)
    xs_a, ys_a = parts_a(me, keep_a, got_a, output_matrix)
    xs_m, ys_g = parts_m(me, keep_g, got_g, down_matrix)
    crossed = plan.across(xs_a)
    small_a = plan.small(ys_a)
    small_g = plan.small(ys_g)
    xs_a = plan.over_xz(xs_a, crossed, small_a[1])
    crossed = plan.across(after(xs_m, small_a[2]))
    y_a = spread(me, small_a, [(0, HALF, 1)], "spread_a")
    rings_a = [[v] for v in y_a]
    for _ in range(3):
        plan.round(rings_a)
    xs_m = plan.over_xz(xs_m, crossed, rings_a[0][1], rings_a[1][1])
    w_qkv, w_out = assemble(Chunks(256, CUT_A, 4 * HALF, places, xs_a, 0, rings_a))
    small_g[3] = after(small_g[3], w_qkv)
    rings_g = [[v] for v in spread(me, small_g, [(0, FF - CUT_G // 2, 1)], "spread_g")]
    plan.round(rings_g)

    facts = jnp.concatenate([group_adapter_index[0], continuation_lengths[0]]).astype(F32)
    facts = jnp.broadcast_to(jnp.pad(facts, (0, 125))[None], (8, 128))
    pair_facts = both(facts, swap(facts))[:, 0, :2].astype(jnp.int32)
    slots = pair_facts[:, 0]
    bounds = PROMPT + pair_facts[:, 1]
    (qkv_down, gu_down, out_down, ff_down, qkv_up, out_up2, ff_up2, gu_up) = choose_adapters(
        jnp.concatenate([slots, me[:1]]),
        adapter_down_inputs,
        adapter_down_feedforward,
        adapter_up_model_maps,
        adapter_up_hidden_maps,
    )

    group_row = lax.broadcasted_iota(jnp.int32, (2 * ROWS, 1), 0) // ROWS

    def own_columns(low, count):
        group_column = lax.broadcasted_iota(jnp.int32, (1, 2 * count), 1) // count
        return jnp.where(group_row == group_column, low, jnp.zeros_like(low))

    shard = ("z", "yh")

    def spread_over(value, axes):
        return lax.all_to_all(jnp.broadcast_to(value[None], (8,) + value.shape), axes, 0, 0, tiled=True)

    place = ctx * ROWS + lax.broadcasted_iota(jnp.int32, (2, ROWS), 1)
    position = jnp.where(place >= bounds[:, None], PROMPT + place - bounds[:, None], place)
    freq = BASE ** (-(jnp.arange(HD // 2, dtype=F32) * 2.0 / HD))
    angle = position.reshape(2 * ROWS, 1).astype(F32) * freq[None]
    cosine = jnp.concatenate([jnp.cos(angle)] * 2, axis=1)
    sine = jnp.concatenate([-jnp.sin(angle), jnp.sin(angle)], axis=1)

    def whole(n):
        return lambda core: [slice(0, n)]

    def half(core):
        return [core * HALF + 128 * m for m in range(8)]

    def turns(n):
        return lambda core: [slice(256 * m + 128 * n, 256 * m + 128 * (n + 1)) for m in range(FF // 128)]

    def third(n):
        return lambda core: [slice(n * HALF, (n + 1) * HALF)]

    x2 = rows_of_both(tokens)
    qkv_low = own_columns((2.0 * dot_nt(x2, qkv_down).astype(BF)).astype(BF), 3 * RANK)
    qkv, squares = project_qkv(x2, w_qkv, qkv_low, qkv_up)
    squares = (squares, swap(squares))
    packed = pack_heads(me, qkv, *squares, gains, cosine, sine)
    heads = lax.all_to_all(packed, CTX, 0, 0, tiled=True).reshape(8, 2, ROWS, 3 * HD)
    heads = after(heads, rings_g[0][-1], rings_g[1][-1])
    plan.round(rings_g, heads)
    out_heads, exact, log_total = attend(bounds, heads)
    attended = lax.all_to_all(out_heads, CTX, 0, 0, tiled=True).reshape(8, 2 * ROWS, HD)
    keep, give, attended = project_out(me, attended, w_out, out_down)
    attn_pre, hidden, sent = combine_attention(me, keep, swap(give), tokens, gains, out_up2)

    sent = after(sent, rings_g[0][-1], rings_g[1][-1])
    plan.round(rings_g, attended)
    wg = Chunks(256, CUT_G, 2 * FF, places, xs_m, 0, rings_g)
    gu, mixed, h2, gu_low, keep, give = feed_forward(wg, sent, swap(sent), gu_down, gu_up, ff_down)
    output, sent = combine_output(me, keep, swap(give), hidden, cotangent, gains, ff_up2)

    d_gu, d_mlp, ff_grad_low, keep, give = feed_forward_back(wg, sent, swap(sent), ff_up2, ff_down, gu, gu_up)
    early = rank_gradients(
        [gu_low, ff_grad_low, d_mlp],
        [d_gu, mixed, d_mlp],
        me,
        "early_gradients",
        [
            (0, 0, (0, 2 * RANK), 1, turns(0)),
            (0, 0, (RANK, 3 * RANK), 1, turns(1)),
            (1, 1, (0, RANK), 1, whole(FF)),
            (2, 2, (D, D), 2, half),
        ],
        EARLY,
    )
    d_hidden, sent = combine_hidden(me, keep, swap(give), cotangent, attn_pre, gains, gu_down)
    sent, early = lax.optimization_barrier((sent, early))
    early = lax.all_to_all(early, CTX, 0, 0, tiled=True)

    d_out_heads, _ = project_out_back(me, sent, swap(sent), w_out, out_up2, out_down, h2, attended)
    d_out_heads = lax.all_to_all(d_out_heads, CTX, 0, 0, tiled=True)
    own = jnp.sum(early.astype(F32), axis=0).astype(BF)
    middle = jnp.sum(d_out_heads[:, 2 * ROWS :].astype(F32), axis=0).astype(BF).reshape(4, 2 * RANK, HD)
    own = jnp.concatenate([own, *middle], axis=1)
    own_slot = jnp.repeat(slots, RANK)[:, None] == lax.broadcasted_iota(jnp.int32, (1, 128), 1)
    own = jnp.concatenate([own, own_slot.astype(BF)], axis=1)
    d_out_heads, own = lax.optimization_barrier((d_out_heads, own))
    groups = spread_over(own, shard).reshape(16, RANK, EARLY + MIDDLE + 128)
    d_heads = attend_back(bounds, heads, d_out_heads, exact, log_total)
    d_heads = lax.all_to_all(d_heads, CTX, 0, 0, tiled=True).reshape(8, 2 * ROWS, 3 * HD)

    def by_slot(groups):
        flat = groups.reshape(16, -1)
        return lax.dot_general(picker, flat, **TN).astype(BF).reshape(8 * RANK, -1)

    picker = groups[:, 0, EARLY + MIDDLE : EARLY + MIDDLE + 8]
    early, d_heads = lax.optimization_barrier((by_slot(groups[:, :, : EARLY + MIDDLE]), d_heads))
    early = lax.all_gather(early, CTX)
    w_q, w_k, d_v, sums = unpack_heads(me, d_heads, qkv, gains, cosine, sine)
    d_qkv, keep, give = project_qkv_back(me, (w_q, w_k), d_v, qkv, squares, (sums, swap(sums)), w_qkv, qkv_up)
    grad_tokens, low = combine_tokens(me, keep, swap(give), d_hidden, qkv_down)
    low = both(low, swap(low)).reshape(2 * ROWS, 128)

    late = rank_gradients(
        [low, qkv_low],
        [x2, d_qkv],
        me,
        "late_gradients",
        [(0, 0, (n * RANK, n * RANK), 1, half) for n in range(3)]
        + [(1, 1, (n * RANK, (3 + n) * RANK), 1, third(n)) for n in range(3)],
        LATE,
    )
    late = lax.all_to_all(late, CTX, 0, 0, tiled=True)
    late = jnp.sum(late.astype(F32), axis=0).astype(BF)
    late = spread_over(late, shard)
    early, late = lax.optimization_barrier((early, late))
    late = spread_over(by_slot(late.reshape(16, RANK, LATE)), CTX)
    shape = (8, 8, RANK, -1)
    early = early.reshape(shape)
    early_other = swap(early)
    grad_up_hidden, grad_down_ff, middle = adapter_outputs(
        me,
        [early],
        [early_other],
        [(8, 2, RANK, 2 * FF), (8, RANK, 2 * FF), (8, 5, RANK, D)],
        "early_outputs",
        write_early,
    )
    late, middle = lax.optimization_barrier((late, middle))
    late_other = swap(late)
    late, late_other = late.reshape(shape), late_other.reshape(shape)
    shapes = [(8, 6, RANK, D), (8, 5, RANK, D)]
    grad_down_in, grad_up_model = adapter_outputs(
        me, [late], [late_other], shapes, "late_outputs", write_late, [middle]
    )
    return (output[None], grad_tokens[None], grad_down_in, grad_down_ff, grad_up_model, grad_up_hidden)


def solution(mesh):
    fine = Mesh(mesh.devices.reshape(2, 4, 4, 2, 2), ALL)
    shard = ("z", "yh", "c")
    rows = P(shard, None)
    per_token = P(shard, CTX, None)
    return jax.shard_map(
        on_device,
        mesh=fine,
        in_specs=(per_token, per_token) + (rows,) * 7 + (P(),) * 5 + (rows, rows),
        out_specs=(per_token, per_token, P(), P(), P(), P()),
        check_vma=False,
    )
```
